32 devices in a mesh: dp: 8 (over z, x), mp: 4 (over y, core).
Axes of the slice: x: 2, y: 2, z: 4, core: 2. Of those that a mesh axis runs over, the one named last changes fastest.
Arguments:
- tokens: bfloat16 [8192, 2048], P(('dp', 'mp')), may hold values from -6 to 6
- cotangent: bfloat16 [8192, 2048], P(('dp', 'mp'))
- group_ids: int32 [8], P('dp'), may hold values from 0 to 5
- group_scales: float32 [6], replicated, may hold values from 0.5 to 2
- gains: float32 [2, 2048], replicated
- gains_first: float32 [2, 2048], replicated, may hold values from -0.00024414062 to 0.00024414062
- gains_second: float32 [2, 2048], replicated, may hold values from 1.0219479e-09 to 4.08002e-09
- taps: float32 [3, 3, 2048], replicated, may hold values from -1 to 1
- taps_first: float32 [3, 3, 2048], replicated, may hold values from -0.00024414062 to 0.00024414062
- taps_second: float32 [3, 3, 2048], replicated, may hold values from 1.0219479e-09 to 4.08002e-09
- residues: float32 [16, 2048], replicated
- residues_first: float32 [16, 2048], replicated, may hold values from -0.00024414062 to 0.00024414062
- residues_second: float32 [16, 2048], replicated, may hold values from 1.0219479e-09 to 4.08002e-09
- log_rates: float32 [16, 2048], replicated
- log_rates_first: float32 [16, 2048], replicated, may hold values from -0.00024414062 to 0.00024414062
- log_rates_second: float32 [16, 2048], replicated, may hold values from 1.0219479e-09 to 4.08002e-09
- skip: float32 [2048], replicated, may hold values from 0.5 to 1.5
- skip_first: float32 [2048], replicated, may hold values from -0.00024414062 to 0.00024414062
- skip_second: float32 [2048], replicated, may hold values from 1.0219479e-09 to 4.08002e-09
- in_weight: float32 [2048, 3, 2048], P('dp', None, 'mp'), may hold values from -0.125 to 0.125
- in_weight_first: float32 [2048, 3, 2048], P('dp', None, 'mp'), may hold values from -0.00024414062 to 0.00024414062
- in_weight_second: float32 [2048, 3, 2048], P('dp', None, 'mp'), may hold values from 1.0219479e-09 to 4.08002e-09
- out_weight: float32 [2048, 2048], P('mp', 'dp'), may hold values from -0.125 to 0.125
- out_weight_first: float32 [2048, 2048], P('mp', 'dp'), may hold values from -0.00024414062 to 0.00024414062
- out_weight_second: float32 [2048, 2048], P('mp', 'dp'), may hold values from 1.0219479e-09 to 4.08002e-09
- gate_weight: float32 [2048, 5632], P('dp', 'mp'), may hold values from -0.125 to 0.125
- gate_weight_first: float32 [2048, 5632], P('dp', 'mp'), may hold values from -0.00024414062 to 0.00024414062
- gate_weight_second: float32 [2048, 5632], P('dp', 'mp'), may hold values from 2.564584e-10 to 1.0219479e-09
- up_weight: float32 [2048, 5632], P('dp', 'mp'), may hold values from -0.125 to 0.125
- up_weight_first: float32 [2048, 5632], P('dp', 'mp'), may hold values from -0.00024414062 to 0.00024414062
- up_weight_second: float32 [2048, 5632], P('dp', 'mp'), may hold values from 2.564584e-10 to 1.0219479e-09
- down_weight: float32 [5632, 2048], P('mp', 'dp'), may hold values from -0.078125 to 0.078125
- down_weight_first: float32 [5632, 2048], P('mp', 'dp'), may hold values from -0.00024414062 to 0.00024414062
- down_weight_second: float32 [5632, 2048], P('mp', 'dp'), may hold values from 1.0219479e-09 to 4.08002e-09
Outputs:
- output: bfloat16 [8192, 2048], P(('dp', 'mp'))
- input_grad: bfloat16 [8192, 2048], P(('dp', 'mp'))
- radial_grad: float32 [8192], P(('dp', 'mp'))
- gains_new: float32 [2, 2048], replicated
- gains_first_new: float32 [2, 2048], replicated
- gains_second_new: float32 [2, 2048], replicated
- taps_new: float32 [3, 3, 2048], replicated
- taps_first_new: float32 [3, 3, 2048], replicated
- taps_second_new: float32 [3, 3, 2048], replicated
- residues_new: float32 [16, 2048], replicated
- residues_first_new: float32 [16, 2048], replicated
- residues_second_new: float32 [16, 2048], replicated
- log_rates_new: float32 [16, 2048], replicated
- log_rates_first_new: float32 [16, 2048], replicated
- log_rates_second_new: float32 [16, 2048], replicated
- skip_new: float32 [2048], replicated
- skip_first_new: float32 [2048], replicated
- skip_second_new: float32 [2048], replicated
- in_weight_new: float32 [2048, 3, 2048], P('dp', None, 'mp')
- in_weight_first_new: float32 [2048, 3, 2048], P('dp', None, 'mp')
- in_weight_second_new: float32 [2048, 3, 2048], P('dp', None, 'mp')
- out_weight_new: float32 [2048, 2048], P('mp', 'dp')
- out_weight_first_new: float32 [2048, 2048], P('mp', 'dp')
- out_weight_second_new: float32 [2048, 2048], P('mp', 'dp')
- gate_weight_new: float32 [2048, 5632], P('dp', 'mp')
- gate_weight_first_new: float32 [2048, 5632], P('dp', 'mp')
- gate_weight_second_new: float32 [2048, 5632], P('dp', 'mp')
- up_weight_new: float32 [2048, 5632], P('dp', 'mp')
- up_weight_first_new: float32 [2048, 5632], P('dp', 'mp')
- up_weight_second_new: float32 [2048, 5632], P('dp', 'mp')
- down_weight_new: float32 [5632, 2048], P('mp', 'dp')
- down_weight_first_new: float32 [5632, 2048], P('mp', 'dp')
- down_weight_second_new: float32 [5632, 2048], P('mp', 'dp')
- grad_norm: float32 [], replicated
The draws below stay inside these ranges and needn't reach their ends.
All inputs are finite; a program needn't handle non-finite values.
Results may differ from the reference program's by a relative error of at most 0.024.
Values may be sent and summed in bfloat16 or wider, within the bound.
No kernel may reach another device: no remote copies, remote signals or barrier semaphores. Data moves between devices by JAX's collectives and lax.ppermute only.
A program may use at most 320 MiB of HBM per device.

```python
import math
import jax
import jax.numpy as jnp
import numpy as np
from jax import lax

D = 2048
FF = 5632
POLES = 16
KS = 3
LEN = 1024
GROUPS = 6
STEP = 10
SEQS = 8
TOKENS = 8192
NPARAM = 51470336


def ramp(count, top):
    return top ** (jnp.arange(count, dtype=jnp.float32) / (count - 1)) / jnp.sqrt(top)


def draw_cotangent(key, part):
    key = jax.random.fold_in(key, 11)
    values = jax.random.normal(key, (TOKENS, D), jnp.float32) * ramp(D, 3.0)[None, :]
    return jnp.clip(values, -3.0, 3.0).astype(jnp.bfloat16)


def draw_gains(key, part):
    key = jax.random.fold_in(key, 12)
    rough = (1.0 + 0.1 * jnp.clip(jax.random.normal(key, (2, D), jnp.float32), -2.0, 2.0)) * ramp(D, 3.0)[None, :]
    return rough


def draw_residues(key, part):
    key = jax.random.fold_in(key, 13)
    base = 2.0 / jnp.sqrt(jnp.float32(POLES * LEN))
    values = jnp.clip(jax.random.normal(key, (POLES, D), jnp.float32), -3.0, 3.0) * ramp(D, 3.0)[None, :]
    return values * base


def draw_log_rates(key, part):
    key = jax.random.fold_in(key, 14)
    pick_key, slow_key, fast_key = jax.random.split(key, 3)
    slow = jnp.log(jax.random.uniform(slow_key, (POLES, D), jnp.float32, 0.2, 2.0) / LEN)
    fast = jnp.log(jax.random.uniform(fast_key, (POLES, D), jnp.float32, 1.0 / 50.0, 1.0 / 30.0))
    chosen = jax.random.uniform(pick_key, (POLES, D), jnp.float32) < 0.5
    return jnp.where(chosen, slow, fast)


def set_ends(values, own_key, least, largest):
    extent = values.shape
    place = [jax.random.randint(jax.random.fold_in(own_key, axis), (), 0, extent[axis]) for axis in range(len(extent))]
    values = values.at[tuple(place)].set(least)
    longest = extent.index(max(extent))
    place[longest] = (place[longest] + 1) % extent[longest]
    return values.at[tuple(place)].set(largest)


def block_scale(own_key, dims, shards, least, top_value):
    loudness, own = 1.0, jax.random.fold_in(own_key, 6)
    for position, shards_of in shards:
        heights = jnp.exp(jax.random.uniform(jax.random.fold_in(own, position), (shards_of,), jnp.float32, least / len(shards), top_value / len(shards)))
        loudness = loudness * jnp.repeat(heights, dims[position] // shards_of).reshape([-1 if axis == position else 1 for axis in range(len(dims))])
    return loudness


def rank_table(number_of, lean):
    weights = [(1 << 20) // math.isqrt(standing ** lean) + 1 for standing in range(1, number_of + 1)]
    width = 1 + sum(weights) // (1 << 30)
    return np.cumsum(np.array([max(1, weight // width) for weight in weights]))


def ranked_ids(rng, dims, count, slope):
    grid = rank_table(count, slope)
    pick = jax.random.randint(jax.random.fold_in(rng, 1), dims, 0, int(grid[count - 1]))
    grade = jnp.searchsorted(jnp.asarray(grid, jnp.int32), pick, side="right")
    return jax.random.permutation(jax.random.fold_in(rng, 2), count)[grade].astype(jnp.int32)


def bell_draw(rng, extent, deviation, reach, shards=(), kind=jnp.bfloat16):
    values = deviation * jax.random.normal(rng, extent, jnp.float32)
    if shards:
        values = values * block_scale(rng, extent, shards, -0.22, 0.18)
    return jnp.clip(values, -reach, reach).astype(kind)


def setup_inputs(seed: int = 0) -> dict:
    keys = jax.random.split(jax.random.key(seed), 35)
    return {
        "tokens": bell_draw(keys[0], (TOKENS, D), 1.0, 6.0, ((0, 32),)),
        "cotangent": draw_cotangent(jax.random.fold_in(keys[34], 71), 0),
        "group_ids": set_ends(ranked_ids(keys[2], (SEQS,), GROUPS, 2), jax.random.fold_in(keys[2], 3), 0, GROUPS - 1).astype(jnp.int32),
        "group_scales": jnp.clip(jnp.exp(jax.random.uniform(keys[3], (GROUPS,), jnp.float32, math.log(0.5), math.log(2.0))), 0.5, 2.0),
        "gains": draw_gains(jax.random.fold_in(keys[34], 71), 0),
        "gains_first": bell_draw(keys[5], (2, D), (0.111 / NPARAM ** 0.5), 0.00024414062, (), jnp.float32),
        "gains_second": jnp.clip(jnp.exp(jax.random.uniform(keys[6], (2, D), jnp.float32, math.log(1.0219478596695808e-09), math.log(4.080019877505947e-09))), 1.0219478596695808e-09, 4.080019877505947e-09),
        "taps": jnp.clip(jax.random.uniform(keys[7], (KS, 3, D), jnp.float32, -1.0, 1.0), -1.0, 1.0),
        "taps_first": bell_draw(keys[8], (KS, 3, D), (0.111 / NPARAM ** 0.5), 0.00024414062, (), jnp.float32),
        "taps_second": jnp.clip(jnp.exp(jax.random.uniform(keys[9], (KS, 3, D), jnp.float32, math.log(1.0219478596695808e-09), math.log(4.080019877505947e-09))), 1.0219478596695808e-09, 4.080019877505947e-09),
        "residues": draw_residues(jax.random.fold_in(keys[34], 71), 0),
        "residues_first": bell_draw(keys[11], (POLES, D), (0.111 / NPARAM ** 0.5), 0.00024414062, (), jnp.float32),
        "residues_second": jnp.clip(jnp.exp(jax.random.uniform(keys[12], (POLES, D), jnp.float32, math.log(1.0219478596695808e-09), math.log(4.080019877505947e-09))), 1.0219478596695808e-09, 4.080019877505947e-09),
        "log_rates": draw_log_rates(jax.random.fold_in(keys[34], 71), 0),
        "log_rates_first": bell_draw(keys[14], (POLES, D), (0.111 / NPARAM ** 0.5), 0.00024414062, (), jnp.float32),
        "log_rates_second": jnp.clip(jnp.exp(jax.random.uniform(keys[15], (POLES, D), jnp.float32, math.log(1.0219478596695808e-09), math.log(4.080019877505947e-09))), 1.0219478596695808e-09, 4.080019877505947e-09),
        "skip": jnp.clip(jax.random.uniform(keys[16], (D,), jnp.float32, 0.5, 1.5), 0.5, 1.5),
        "skip_first": bell_draw(keys[17], (D,), (0.111 / NPARAM ** 0.5), 0.00024414062, (), jnp.float32),
        "skip_second": jnp.clip(jnp.exp(jax.random.uniform(keys[18], (D,), jnp.float32, math.log(1.0219478596695808e-09), math.log(4.080019877505947e-09))), 1.0219478596695808e-09, 4.080019877505947e-09),
        "in_weight": bell_draw(keys[19], (D, 3, D), D ** -0.5, 0.125, ((0, 8), (2, 4)), jnp.float32),
        "in_weight_first": bell_draw(keys[20], (D, 3, D), (0.111 / NPARAM ** 0.5), 0.00024414062, ((0, 8), (2, 4)), jnp.float32),
        "in_weight_second": jnp.clip(jnp.exp(math.log(4.080019877505947e-09) - 1.3843914 * jax.random.uniform(keys[21], (D, 3, D), jnp.float32) ** block_scale(keys[21], (D, 3, D), ((0, 8), (2, 4)), -0.2, 0.2)), 1.0219478596695808e-09, 4.080019877505947e-09),
        "out_weight": bell_draw(keys[22], (D, D), D ** -0.5, 0.125, ((0, 4), (1, 8)), jnp.float32),
        "out_weight_first": bell_draw(keys[23], (D, D), (0.111 / NPARAM ** 0.5), 0.00024414062, ((0, 4), (1, 8)), jnp.float32),
        "out_weight_second": jnp.clip(jnp.exp(math.log(4.080019877505947e-09) - 1.3843914 * jax.random.uniform(keys[24], (D, D), jnp.float32) ** block_scale(keys[24], (D, D), ((0, 4), (1, 8)), -0.2, 0.2)), 1.0219478596695808e-09, 4.080019877505947e-09),
        "gate_weight": bell_draw(keys[25], (D, FF), D ** -0.5, 0.125, ((0, 8), (1, 4)), jnp.float32),
        "gate_weight_first": bell_draw(keys[26], (D, FF), (0.111 / NPARAM ** 0.5), 0.00024414062, ((0, 8), (1, 4)), jnp.float32),
        "gate_weight_second": jnp.clip(jnp.exp(math.log(1.0219478596695808e-09) - 1.3824992 * jax.random.uniform(keys[27], (D, FF), jnp.float32) ** block_scale(keys[27], (D, FF), ((0, 8), (1, 4)), -0.2, 0.2)), 2.564584100639422e-10, 1.0219478596695808e-09),
        "up_weight": bell_draw(keys[28], (D, FF), D ** -0.5, 0.125, ((0, 8), (1, 4)), jnp.float32),
        "up_weight_first": bell_draw(keys[29], (D, FF), (0.111 / NPARAM ** 0.5), 0.00024414062, ((0, 8), (1, 4)), jnp.float32),
        "up_weight_second": jnp.clip(jnp.exp(math.log(1.0219478596695808e-09) - 1.3824992 * jax.random.uniform(keys[30], (D, FF), jnp.float32) ** block_scale(keys[30], (D, FF), ((0, 8), (1, 4)), -0.2, 0.2)), 2.564584100639422e-10, 1.0219478596695808e-09),
        "down_weight": bell_draw(keys[31], (FF, D), FF ** -0.5, 0.078125, ((0, 4), (1, 8)), jnp.float32),
        "down_weight_first": bell_draw(keys[32], (FF, D), (0.111 / NPARAM ** 0.5), 0.00024414062, ((0, 4), (1, 8)), jnp.float32),
        "down_weight_second": jnp.clip(jnp.exp(math.log(4.080019877505947e-09) - 1.3843914 * jax.random.uniform(keys[33], (FF, D), jnp.float32) ** block_scale(keys[33], (FF, D), ((0, 4), (1, 8)), -0.2, 0.2)), 1.0219478596695808e-09, 4.080019877505947e-09),
    }


EPSILON = 1e-05
CLIP = 1.0
BETA_ONE = 0.9
BETA_TWO = 0.95
ADAM_EPSILON = 1e-08
DECAY = 0.1
RATE_MATRIX = 0.05
RATE_SMALL = 0.5
RATE_RATES = 4.0
HIGHEST = lax.Precision.HIGHEST

@jax.custom_vjp
def low(v):
    return lax.optimization_barrier(v.astype(jnp.bfloat16)).astype(jnp.float32)

@jax.custom_vjp
def low_back(v):
    return v

def low_keep(v):
    return (low(v), None)

def low_pass(kept, grad):
    return (grad,)

def back_keep(v):
    return (v, None)

def back_low(kept, grad):
    return (low(grad),)
low.defvjp(low_keep, low_pass)
low_back.defvjp(back_keep, back_low)

def matmul(left, right):
    return jnp.dot(left, right, precision=HIGHEST, preferred_element_type=jnp.float32)

def rms_norm(values, gain):
    scale = lax.rsqrt(lax.optimization_barrier(jnp.mean(values * values, axis=-1, keepdims=True)) + EPSILON)
    return values * scale * gain

def short_conv(values, kernel):
    length = values.shape[0]
    result = kernel[0] * values
    for offset in range(1, kernel.shape[0]):
        shifted = jnp.pad(values, ((offset, 0), (0, 0), (0, 0)))[:length]
        result = result + kernel[offset] * shifted
    return result

def long_filter(residues, log_rates):
    positions = jnp.arange(LEN, dtype=jnp.float32)
    decays = jnp.exp(-positions[:, None, None] * jnp.exp(log_rates)[None])
    return lax.optimization_barrier(jnp.sum(decays * residues[None], axis=1))

def causal_conv(signal, filt):
    size = 2 * LEN
    product = jnp.fft.rfft(signal, n=size, axis=0) * jnp.fft.rfft(filt, n=size, axis=0)
    return jnp.fft.irfft(product, n=size, axis=0)[:LEN]

def block(sequence, gains, taps, residues, log_rates, skip, in_weight, out_weight, gate_weight, up_weight, down_weight):
    normed = low(rms_norm(sequence, gains[0]))
    proj = low_back(matmul(normed, low(in_weight).reshape(D, 3 * D))).reshape(LEN, 3, D)
    mixed = short_conv(proj, taps)
    query, key, value = (mixed[:, 0], mixed[:, 1], mixed[:, 2])
    gated = key * value
    conv = causal_conv(gated, long_filter(residues, log_rates)) + skip * gated
    branch = low(query * conv)
    middle = sequence + low_back(matmul(branch, low(out_weight)))
    normed_two = low(rms_norm(middle, gains[1]))
    gate = low_back(matmul(normed_two, low(gate_weight)))
    up = low_back(matmul(normed_two, low(up_weight)))
    inner = low(jax.nn.silu(gate) * up)
    return middle + matmul(inner, low(down_weight))

def adam(weight, first, second, grad, rate, decay):
    first_new = BETA_ONE * first + (1.0 - BETA_ONE) * grad
    second_new = BETA_TWO * second + (1.0 - BETA_TWO) * grad * grad
    stride = first_new / (1.0 - BETA_ONE ** STEP) / (jnp.sqrt(second_new / (1.0 - BETA_TWO ** STEP)) + ADAM_EPSILON)
    return (weight - rate * (stride + decay * weight), first_new, second_new)

def reference(tokens, cotangent, group_ids, group_scales, gains, gains_first, gains_second, taps, taps_first, taps_second, residues, residues_first, residues_second, log_rates, log_rates_first, log_rates_second, skip, skip_first, skip_second, in_weight, in_weight_first, in_weight_second, out_weight, out_weight_first, out_weight_second, gate_weight, gate_weight_first, gate_weight_second, up_weight, up_weight_first, up_weight_second, down_weight, down_weight_first, down_weight_second):
    params = (gains, taps, residues, log_rates, skip, in_weight, out_weight, gate_weight, up_weight, down_weight)
    count = tokens.shape[0] // LEN
    rows = tokens.astype(jnp.float32).reshape(count, LEN, D)
    backs = cotangent.astype(jnp.float32).reshape(count, LEN, D)
    picked = lax.optimization_barrier(jnp.sum(jnp.where(group_ids[:, None] == jnp.arange(GROUPS, dtype=jnp.int32)[None, :], group_scales[None, :], 0.0), axis=1))

    def one(carry, item):
        sequence, back, weight = item
        result, pull = jax.vjp(block, sequence, *params)
        grads = pull(back * weight)
        summed = tuple((held + fresh for held, fresh in zip(carry, grads[1:])))
        row_scale = lax.rsqrt(lax.optimization_barrier(jnp.mean(sequence * sequence, axis=-1)) + EPSILON)
        radial = row_scale * lax.optimization_barrier(jnp.sum(sequence * grads[0], axis=-1)) / D ** 0.5
        return (summed, (result, grads[0], radial))
    start = tuple((jnp.zeros_like(param) for param in params))
    sums, (results, input_grads, radials) = lax.scan(one, start, (rows, backs, picked))
    grad_norm = jnp.sqrt(sum((jnp.sum(grad * grad) for grad in sums)))
    factor = jnp.minimum(1.0, CLIP / (grad_norm + 1e-06))
    gains_new, gains_first_new, gains_second_new = adam(gains, gains_first, gains_second, sums[0] * factor, RATE_SMALL, 0.0)
    taps_new, taps_first_new, taps_second_new = adam(taps, taps_first, taps_second, sums[1] * factor, RATE_SMALL, 0.0)
    residues_new, residues_first_new, residues_second_new = adam(residues, residues_first, residues_second, sums[2] * factor, RATE_SMALL, 0.0)
    log_rates_new, log_rates_first_new, log_rates_second_new = adam(log_rates, log_rates_first, log_rates_second, sums[3] * factor, RATE_RATES, 0.0)
    skip_new, skip_first_new, skip_second_new = adam(skip, skip_first, skip_second, sums[4] * factor, RATE_SMALL, 0.0)
    in_weight_new, in_weight_first_new, in_weight_second_new = adam(in_weight, in_weight_first, in_weight_second, sums[5] * factor, RATE_MATRIX, DECAY)
    out_weight_new, out_weight_first_new, out_weight_second_new = adam(out_weight, out_weight_first, out_weight_second, sums[6] * factor, RATE_MATRIX, DECAY)
    gate_weight_new, gate_weight_first_new, gate_weight_second_new = adam(gate_weight, gate_weight_first, gate_weight_second, sums[7] * factor, RATE_MATRIX, DECAY)
    up_weight_new, up_weight_first_new, up_weight_second_new = adam(up_weight, up_weight_first, up_weight_second, sums[8] * factor, RATE_MATRIX, DECAY)
    down_weight_new, down_weight_first_new, down_weight_second_new = adam(down_weight, down_weight_first, down_weight_second, sums[9] * factor, RATE_MATRIX, DECAY)
    output = results.reshape(count * LEN, D).astype(jnp.bfloat16)
    input_grad = input_grads.reshape(count * LEN, D).astype(jnp.bfloat16)
    radial_grad = radials.reshape(count * LEN)
    return (output, input_grad, radial_grad, gains_new, gains_first_new, gains_second_new, taps_new, taps_first_new, taps_second_new, residues_new, residues_first_new, residues_second_new, log_rates_new, log_rates_first_new, log_rates_second_new, skip_new, skip_first_new, skip_second_new, in_weight_new, in_weight_first_new, in_weight_second_new, out_weight_new, out_weight_first_new, out_weight_second_new, gate_weight_new, gate_weight_first_new, gate_weight_second_new, up_weight_new, up_weight_first_new, up_weight_second_new, down_weight_new, down_weight_first_new, down_weight_second_new, grad_norm)
```

```python
import functools

import jax
import jax.numpy as jnp
from jax import lax
from jax.experimental import pallas as pl
from jax.experimental.pallas import tpu as pltpu
from jax.sharding import PartitionSpec as P

STEP = 10


EPSILON = 1e-05
CLIP = 1.0
BETA_ONE = 0.9
BETA_TWO = 0.95
ADAM_EPSILON = 1e-08
DECAY = 0.1
RATE_MATRIX = 0.05
RATE_SMALL = 0.5
RATE_RATES = 4.0

LANES = 128
CHUNK = 128
CHUNKS = 8
LENGTH = CHUNK * CHUNKS
PAD = 8
TAPS = 3
POLES = 16
SKIP_ROW = TAPS * 3
RES_ROW = 16
RATE_ROW = RES_ROW + POLES
COEF_ROWS = RATE_ROW + POLES
MODE_GROUP = 8

f32 = jnp.float32
bf16 = jnp.bfloat16


def chunk_row(pos_ref, seq, n):
    block, half = n // 2, n % 2
    y, c = pos_ref[0], pos_ref[1]
    dy = y if block // 2 == 0 else 1 - y
    dc = c if block % 2 == 0 else 1 - c
    if half == 0:
        row = dc * LENGTH + seq * (2 * CHUNK) + dy * CHUNK
    else:
        row = dc * LENGTH + LENGTH // 2 + dy * (2 * CHUNK) + seq * CHUNK
    return pl.multiple_of(row, CHUNK)


def mix_chunk(pad_ref, coef, which, n):
    base = PAD + n * CHUNK
    total = coef[which : which + 1, :] * pad_ref[pl.ds(base, CHUNK), :]
    for i in range(1, TAPS):
        row = 3 * i + which
        total = total + coef[row : row + 1, :] * pad_ref[pl.ds(base - i, CHUNK), :]
    return total


def spread(row):
    return jnp.broadcast_to(row, (CHUNKS, LANES))


def power_of_two(value, doublings):
    for _ in range(doublings):
        value = value * value
    return value


def shift_down(value, count):
    rolled = pltpu.roll(value, count, 0)
    place = lax.broadcasted_iota(jnp.int32, (CHUNKS, LANES), 0)
    return jnp.where(place >= count, rolled, 0.0)


def shift_up(value, count):
    rolled = pltpu.roll(value, CHUNKS - count, 0)
    place = lax.broadcasted_iota(jnp.int32, (CHUNKS, LANES), 0)
    return jnp.where(place < CHUNKS - count, rolled, 0.0)


def tile_rows(t):
    return pl.ds(pl.multiple_of(t * CHUNKS, CHUNKS), CHUNKS)


def forward_kernel(pos_ref, proj_ref, coef_ref, branch_ref, conv_ref, pads, u_ref, y_ref):
    coef = coef_ref[...]
    decay = [spread(coef[RATE_ROW + p : RATE_ROW + p + 1, :]) for p in range(POLES)]
    weight = [spread(coef[RES_ROW + p : RES_ROW + p + 1, :]) for p in range(POLES)]
    skip = coef[SKIP_ROW : SKIP_ROW + 1, :]
    y_ref[pl.ds(0, CHUNKS), :] = jnp.zeros((CHUNKS, LANES), f32)
    zero = y_ref[pl.ds(0, CHUNKS), :]
    for seq in range(2):
        for j in range(3):
            pads[j, pl.ds(0, PAD), :] = jnp.zeros((PAD, LANES), f32)
        for n in range(CHUNKS):
            rows = pl.ds(chunk_row(pos_ref, seq, n), CHUNK)
            for j in range(3):
                pads[j, pl.ds(PAD + n * CHUNK, CHUNK), :] = proj_ref[
                    rows, j * LANES : (j + 1) * LANES
                ]
        for n in range(CHUNKS):
            gated = mix_chunk(pads.at[1], coef, 1, n) * mix_chunk(pads.at[2], coef, 2, n)
            u_ref[pl.ds(n, CHUNK, stride=CHUNKS), :] = gated

        def ends(t, state):
            u = u_ref[tile_rows(t), :]
            return [a * h + u for a, h in zip(decay, state)]

        state = lax.fori_loop(0, CHUNK, ends, [zero] * POLES, unroll=2)
        start = []
        for a, h in zip(decay, state):
            jump = power_of_two(a, 7)
            for count in (1, 2, 4):
                h = h + jump * shift_down(h, count)
                jump = jump * jump
            start.append(shift_down(h, 1))

        def outputs(t, state):
            u = u_ref[tile_rows(t), :]
            state = [a * h + u for a, h in zip(decay, state)]
            terms = [w * h for w, h in zip(weight, state)]
            while len(terms) > 1:
                terms = [l + r for l, r in zip(terms[0::2], terms[1::2])]
            y_ref[tile_rows(t), :] = terms[0]
            return state

        lax.fori_loop(0, CHUNK, outputs, start, unroll=2)
        for n in range(CHUNKS):
            rows = pl.ds(chunk_row(pos_ref, seq, n), CHUNK)
            strided = pl.ds(n, CHUNK, stride=CHUNKS)
            conv = y_ref[strided, :] + skip * u_ref[strided, :]
            conv_ref[rows, :] = conv
            branch_ref[rows, :] = (mix_chunk(pads.at[0], coef, 0, n) * conv).astype(bf16)


def backward_kernel(
    pos_ref,
    proj_ref,
    conv_ref,
    grad_ref,
    coef_ref,
    out_ref,
    sums_ref,
    pads,
    mixed,
    grads,
    u_ref,
    g_ref,
    y_ref,
):
    coef = coef_ref[...]
    decay = [spread(coef[RATE_ROW + p : RATE_ROW + p + 1, :]) for p in range(POLES)]
    weight = [spread(coef[RES_ROW + p : RES_ROW + p + 1, :]) for p in range(POLES)]
    skip = coef[SKIP_ROW : SKIP_ROW + 1, :]
    y_ref[pl.ds(0, CHUNKS), :] = jnp.zeros((CHUNKS, LANES), f32)
    zero = y_ref[pl.ds(0, CHUNKS), :]
    row_zero = jnp.zeros((1, LANES), f32)
    tap_sums = [row_zero] * (3 * TAPS)
    skip_sum = row_zero
    res_sums = [zero] * POLES
    rate_sums = [zero] * POLES
    for seq in range(2):
        for j in range(3):
            pads[j, pl.ds(0, PAD), :] = jnp.zeros((PAD, LANES), f32)
            grads[j, pl.ds(LENGTH, PAD), :] = jnp.zeros((PAD, LANES), f32)
        for n in range(CHUNKS):
            rows = pl.ds(chunk_row(pos_ref, seq, n), CHUNK)
            for j in range(3):
                pads[j, pl.ds(PAD + n * CHUNK, CHUNK), :] = proj_ref[
                    rows, j * LANES : (j + 1) * LANES
                ]
        for n in range(CHUNKS):
            rows = pl.ds(chunk_row(pos_ref, seq, n), CHUNK)
            strided = pl.ds(n, CHUNK, stride=CHUNKS)
            plain = pl.ds(n * CHUNK, CHUNK)
            query = mix_chunk(pads.at[0], coef, 0, n)
            key = mix_chunk(pads.at[1], coef, 1, n)
            value = mix_chunk(pads.at[2], coef, 2, n)
            mixed[0, plain, :] = key
            mixed[1, plain, :] = value
            branch_grad = grad_ref[rows, :]
            grads[0, plain, :] = branch_grad * conv_ref[rows, :]
            u_ref[strided, :] = key * value
            g_ref[strided, :] = branch_grad * query

        def ends(step, state):
            g = g_ref[tile_rows(CHUNK - 1 - step), :]
            after = []
            for a, (b, e) in zip(decay, state):
                ab = a * b
                after.append((ab + g, a * e + ab))
            return after

        state = lax.fori_loop(0, CHUNK, ends, [(zero, zero)] * POLES, unroll=2)
        start = []
        for a, (b, e) in zip(decay, state):
            jump = power_of_two(a, 7)
            span = float(CHUNK)
            for count in (1, 2, 4):
                b_next, e_next = shift_up(b, count), shift_up(e, count)
                e = e + jump * (e_next + span * b_next)
                b = b + jump * b_next
                jump = jump * jump
                span = 2.0 * span
            start.append((shift_up(b, 1), shift_up(e, 1)))

        for first in range(0, POLES, MODE_GROUP):
            modes = range(first, first + MODE_GROUP)

            def outputs(step, state, modes=modes, first=first):
                t = CHUNK - 1 - step
                g = g_ref[tile_rows(t), :]
                u = u_ref[tile_rows(t), :]
                after, terms = [], []
                for p, (b, e, res, rate) in zip(modes, state):
                    ab = decay[p] * b
                    e = decay[p] * e + ab
                    b = ab + g
                    terms.append(weight[p] * b)
                    after.append((b, e, res + u * b, rate + u * e))
                while len(terms) > 1:
                    terms = [l + r for l, r in zip(terms[0::2], terms[1::2])]
                total = terms[0]
                if first > 0:
                    total = total + y_ref[tile_rows(t), :]
                y_ref[tile_rows(t), :] = total
                return after

            begin = [(*start[p], res_sums[p], rate_sums[p]) for p in modes]
            after = lax.fori_loop(0, CHUNK, outputs, begin, unroll=2)
            for p, (_, _, res, rate) in zip(modes, after):
                res_sums[p], rate_sums[p] = res, rate

        for n in range(CHUNKS):
            strided = pl.ds(n, CHUNK, stride=CHUNKS)
            plain = pl.ds(n * CHUNK, CHUNK)
            conv_grad = g_ref[strided, :]
            gated_grad = y_ref[strided, :] + skip * conv_grad
            skip_sum = skip_sum + jnp.sum(conv_grad * u_ref[strided, :], axis=0, keepdims=True)
            grads[1, plain, :] = gated_grad * mixed[1, plain, :]
            grads[2, plain, :] = gated_grad * mixed[0, plain, :]
        for n in range(CHUNKS):
            rows = pl.ds(chunk_row(pos_ref, seq, n), CHUNK)
            for j in range(3):
                here = grads[j, pl.ds(n * CHUNK, CHUNK), :]
                total = coef[j : j + 1, :] * here
                for i in range(TAPS):
                    behind = pads[j, pl.ds(PAD + n * CHUNK - i, CHUNK), :]
                    row = 3 * i + j
                    tap_sums[row] = tap_sums[row] + jnp.sum(here * behind, axis=0, keepdims=True)
                    if i > 0:
                        ahead = grads[j, pl.ds(n * CHUNK + i, CHUNK), :]
                        total = total + coef[row : row + 1, :] * ahead
                out_ref[rows, j * LANES : (j + 1) * LANES] = total.astype(bf16)
    for row in range(3 * TAPS):
        sums_ref[row : row + 1, :] = tap_sums[row]
    sums_ref[SKIP_ROW : SKIP_ROW + 1, :] = skip_sum
    for row in range(SKIP_ROW + 1, RES_ROW):
        sums_ref[row : row + 1, :] = row_zero
    for p in range(POLES):
        sums_ref[RES_ROW + p : RES_ROW + p + 1, :] = jnp.sum(res_sums[p], axis=0, keepdims=True)
        sums_ref[RATE_ROW + p : RATE_ROW + p + 1, :] = jnp.sum(
            rate_sums[p], axis=0, keepdims=True
        )


def mixer_forward(position, proj, coef):
    rows, channels = proj.shape[0], coef.shape[1]
    return pl.pallas_call(
        forward_kernel,
        grid=(channels // LANES,),
        in_specs=[
            pl.BlockSpec(memory_space=pltpu.SMEM),
            pl.BlockSpec((rows, 3 * LANES), lambda i: (0, i)),
            pl.BlockSpec((COEF_ROWS, LANES), lambda i: (0, i)),
        ],
        out_specs=[
            pl.BlockSpec((rows, LANES), lambda i: (0, i)),
            pl.BlockSpec((rows, LANES), lambda i: (0, i)),
        ],
        out_shape=[
            jax.ShapeDtypeStruct((rows, channels), bf16),
            jax.ShapeDtypeStruct((rows, channels), f32),
        ],
        scratch_shapes=[
            pltpu.VMEM((3, PAD + LENGTH, LANES), f32),
            pltpu.VMEM((LENGTH, LANES), f32),
            pltpu.VMEM((LENGTH, LANES), f32),
        ],
        compiler_params=pltpu.CompilerParams(vmem_limit_bytes=28 << 20),
        cost_estimate=pl.CostEstimate(
            flops=20_000_000, bytes_accessed=12 << 20, transcendentals=0
        ),
        name="mixer_forward",
    )(position, proj, coef)


def mixer_backward(position, proj, conv, grad, coef):
    rows, channels = proj.shape[0], coef.shape[1]
    return pl.pallas_call(
        backward_kernel,
        grid=(channels // LANES,),
        in_specs=[
            pl.BlockSpec(memory_space=pltpu.SMEM),
            pl.BlockSpec((rows, 3 * LANES), lambda i: (0, i)),
            pl.BlockSpec((rows, LANES), lambda i: (0, i)),
            pl.BlockSpec((rows, LANES), lambda i: (0, i)),
            pl.BlockSpec((COEF_ROWS, LANES), lambda i: (0, i)),
        ],
        out_specs=[
            pl.BlockSpec((rows, 3 * LANES), lambda i: (0, i)),
            pl.BlockSpec((COEF_ROWS, LANES), lambda i: (0, i)),
        ],
        out_shape=[
            jax.ShapeDtypeStruct((rows, 3 * channels), bf16),
            jax.ShapeDtypeStruct((COEF_ROWS, channels), f32),
        ],
        scratch_shapes=[
            pltpu.VMEM((3, PAD + LENGTH, LANES), f32),
            pltpu.VMEM((2, LENGTH, LANES), f32),
            pltpu.VMEM((3, LENGTH + PAD, LANES), f32),
            pltpu.VMEM((LENGTH, LANES), f32),
            pltpu.VMEM((LENGTH, LANES), f32),
            pltpu.VMEM((LENGTH, LANES), f32),
        ],
        compiler_params=pltpu.CompilerParams(vmem_limit_bytes=36 << 20),
        cost_estimate=pl.CostEstimate(
            flops=60_000_000, bytes_accessed=16 << 20, transcendentals=0
        ),
        name="mixer_backward",
    )(position, proj, conv, grad, coef)


def rows_by_rows(left, right):
    return lax.dot_general(left, right, (((1,), (1,)), ((), ())), preferred_element_type=f32)


def columns_by_columns(left, right):
    return lax.dot_general(left, right, (((0,), (0,)), ((), ())), preferred_element_type=f32)


def plain_dot(left, right):
    return jnp.dot(left, right, preferred_element_type=f32)


def low(values):
    return values.astype(bf16)


def add_low(left, right):
    return (left.astype(f32) + right.astype(f32)).astype(bf16)


def norm_back(values, scale, gain, grad):
    weighted = grad * gain
    inner_mean = jnp.mean(values * weighted, axis=1, keepdims=True)
    return (
        scale * weighted - values * (scale * scale * scale) * inner_mean,
        jnp.sum(grad * values * scale, axis=0),
    )


def adam(weight, first, second, grad, rate, decay):
    first_new = BETA_ONE * first + (1.0 - BETA_ONE) * grad
    second_new = BETA_TWO * second + (1.0 - BETA_TWO) * grad * grad
    stride = (
        first_new
        / (1.0 - BETA_ONE**STEP)
        / (jnp.sqrt(second_new / (1.0 - BETA_TWO**STEP)) + ADAM_EPSILON)
    )
    return (weight - rate * (stride + decay * weight), first_new, second_new)


class Links:
    def __init__(self, groups, holders):
        self.groups = groups
        self.ring = [(2 * z + x, 2 * ((z + 1) % groups) + x) for z in range(groups) for x in (0, 1)]
        self.over_x = [(2 * z + x, 2 * z + 1 - x) for z in range(groups) for x in (0, 1)]
        self.over_y = [(2 * y + c, 2 * (1 - y) + c) for y in (0, 1) for c in (0, 1)]
        self.over_c = [(2 * y + c, 2 * y + 1 - c) for y in (0, 1) for c in (0, 1)]
        self.turns = [
            [(2 * z + x, 2 * ((z + s) % groups) + x) for z in range(groups) for x in (0, 1)]
            for s in range(groups)
        ]

    def z(self, v):
        return lax.ppermute(v, "dp", self.ring)

    def turn(self, v, s):
        return lax.ppermute(v, "dp", self.turns[s])

    def x(self, v):
        return lax.ppermute(v, "dp", self.over_x)

    def y(self, v):
        return lax.ppermute(v, "mp", self.over_y)

    def c(self, v):
        return lax.ppermute(v, "mp", self.over_c)


def gather_rows(net, block):
    half = block.shape[0] // 2
    a, b = block[:half], block[half:]
    a_x, b_y = net.x(a), net.y(b)
    a_y, b_x = net.y(a), net.x(b)
    a_xy, b_yx = net.y(a_x), net.x(b_y)
    mine = [a, a_y, a_x, a_xy, b, b_x, b_y, b_yx]
    return jnp.concatenate(mine + [net.c(piece) for piece in mine], axis=0)


def scatter_rows(net, partial):
    rows = partial.shape[0]
    near = add_low(partial[: rows // 2], net.c(partial[rows // 2 :]))
    piece = rows // 16
    a, b = near[: 4 * piece], near[4 * piece :]
    a = add_low(a[: 2 * piece], net.x(a[2 * piece :]))
    b = add_low(b[: 2 * piece], net.y(b[2 * piece :]))
    a = a[:piece].astype(f32) + net.y(a[piece:]).astype(f32)
    b = b[:piece].astype(f32) + net.x(b[piece:]).astype(f32)
    return jnp.concatenate([a, b], axis=0)


def pick(pair, index):
    return lax.dynamic_index_in_dim(pair, index, 0, keepdims=False)


def in_order(mine, other, x, axis):
    return jnp.where(
        x == 0,
        jnp.concatenate([mine, other], axis=axis),
        jnp.concatenate([other, mine], axis=axis),
    )


def gather_units(net, halves, x, z):
    piece = in_order(pick(halves, x), net.x(pick(halves, 1 - x)), x, 1)
    units, width = piece.shape
    whole = jnp.zeros((units, width * net.groups), bf16)
    for step in range(net.groups):
        place = lax.rem(z + net.groups - step, net.groups) * width
        whole = lax.dynamic_update_slice(whole, piece, (0, place))
        if step < net.groups - 1:
            piece = net.z(piece)
    return whole


def scatter_units(net, grad, z):
    width = grad.shape[1] // net.groups

    def part(step):
        place = lax.rem(z + 2 * net.groups - 1 - step, net.groups) * width
        return lax.dynamic_slice_in_dim(grad, place, width, 1)

    total = part(0)
    for step in range(1, net.groups):
        total = net.z(total).astype(f32) + part(step).astype(f32)
        if step < net.groups - 1:
            total = total.astype(bf16)
    return total


def trade_units(net, total, x):
    width = total.shape[1] // 2
    mine = lax.dynamic_slice_in_dim(total, x * width, width, 1)
    other = lax.dynamic_slice_in_dim(total, (1 - x) * width, width, 1)
    got = net.x(other.astype(bf16)).astype(f32)
    return jnp.where(x == 0, jnp.stack([mine, got]), jnp.stack([got, mine]))


def on_device(
    net,
    tokens,
    cotangent,
    group_ids,
    group_scales,
    gains,
    gains_first,
    gains_second,
    taps,
    taps_first,
    taps_second,
    residues,
    residues_first,
    residues_second,
    log_rates,
    log_rates_first,
    log_rates_second,
    skip,
    skip_first,
    skip_second,
    in_weight,
    in_weight_first,
    in_weight_second,
    out_weight,
    out_weight_first,
    out_weight_second,
    gate_weight,
    gate_weight_first,
    gate_weight_second,
    up_weight,
    up_weight_first,
    up_weight_second,
    down_weight,
    down_weight_first,
    down_weight_second,
):
    model = tokens.shape[1]
    depth = in_weight.shape[0]
    channels = in_weight.shape[2] // 2
    hidden = gate_weight.shape[1] // 2
    tiles = channels // LANES
    dp, mp = lax.axis_index("dp"), lax.axis_index("mp")
    z, x, y, c = dp // 2, dp % 2, mp // 2, mp % 2
    begin = (mp * 2 + x) * channels
    position = jnp.stack([y, c]).astype(jnp.int32)

    in_halves = (
        low(in_weight).reshape(depth, 3, 2, tiles, LANES).transpose(2, 3, 1, 4, 0)
    ).reshape(2, 3 * channels, depth)
    w_in = gather_units(net, in_halves, x, z)
    w_out = gather_units(net, low(out_weight).reshape(2, channels, depth), x, z)
    w_gate = gather_units(net, low(gate_weight).T.reshape(2, hidden, depth), x, z)
    w_up = gather_units(net, low(up_weight).T.reshape(2, hidden, depth), x, z)
    w_down = gather_units(net, low(down_weight).reshape(2, hidden, depth), x, z)

    def own(array):
        return lax.dynamic_slice_in_dim(array, begin, channels, array.ndim - 1)

    residues_own = own(residues)
    rates_own = jnp.exp(own(log_rates))
    coef = jnp.concatenate(
        [
            own(taps).reshape(3 * TAPS, channels),
            own(skip)[None],
            jnp.zeros((RES_ROW - SKIP_ROW - 1, channels), f32),
            residues_own,
            jnp.exp(-rates_own),
        ],
        axis=0,
    )

    sequence_scale = jnp.sum(
        jnp.where(
            group_ids[:, None] == jnp.arange(group_scales.shape[0], dtype=jnp.int32)[None, :],
            group_scales[None, :],
            0.0,
        )
    )
    other_scale = net.x(sequence_scale.reshape(1, 1))

    resid = tokens.astype(f32)
    scale_one = lax.rsqrt(jnp.mean(resid * resid, axis=1, keepdims=True) + EPSILON)
    normed = low(resid * scale_one * gains[0])
    normed_all = gather_rows(net, normed)
    back_all = gather_rows(net, cotangent)
    proj = rows_by_rows(normed_all, w_in)
    branch, conv = mixer_forward(position, proj, coef)
    middle = resid + scatter_rows(net, low(plain_dot(branch, w_out)))
    scale_two = lax.rsqrt(jnp.mean(middle * middle, axis=1, keepdims=True) + EPSILON)
    normed_two = low(middle * scale_two * gains[1])
    normed_two_all = gather_rows(net, normed_two)
    gate = rows_by_rows(normed_two_all, w_gate)
    up = rows_by_rows(normed_two_all, w_up)
    sigma = jax.nn.sigmoid(gate)
    silu = gate * sigma
    inner = silu * up
    rows = normed_two_all.shape[0]
    index = lax.broadcasted_iota(jnp.int32, (rows, 1), 0)
    half, within = (index // (rows // 4)) % 2, (index // (rows // 16)) % 4
    other_row = jnp.where(half == 0, within // 2, within % 2) == 1
    row_scale = jnp.where(other_row, other_scale, sequence_scale.reshape(1, 1))

    grad_down = low(columns_by_columns(low(inner * row_scale), back_all))
    total_down = scatter_units(net, grad_down, z)
    grad_inner = rows_by_rows(back_all, w_down) * row_scale
    grad_gate = low(grad_inner * up * sigma * (1.0 + gate * (1.0 - sigma)))
    grad_up = low(grad_inner * silu)
    total_gate = scatter_units(net, low(columns_by_columns(grad_gate, normed_two_all)), z)
    total_up = scatter_units(net, low(columns_by_columns(grad_up, normed_two_all)), z)
    output = low(middle + scatter_rows(net, low(plain_dot(low(inner), w_down))))
    grad_normed_two = scatter_rows(
        net, low(plain_dot(grad_gate, w_gate) + plain_dot(grad_up, w_up))
    )
    grad_from_norm, gain_two = norm_back(middle, scale_two, gains[1], grad_normed_two)
    grad_middle = cotangent.astype(f32) * sequence_scale + grad_from_norm
    grad_middle_all = gather_rows(net, low(grad_middle))
    total_out = scatter_units(net, low(columns_by_columns(branch, grad_middle_all)), z)
    grad_branch = rows_by_rows(grad_middle_all, w_out)
    grad_proj, sums = mixer_backward(position, proj, conv, grad_branch, coef)
    total_in = scatter_units(net, low(columns_by_columns(grad_proj, normed_all)), z)
    grad_normed = scatter_rows(net, low(plain_dot(grad_proj, w_in)))
    grad_from_first, gain_one = norm_back(resid, scale_one, gains[0], grad_normed)
    grad_input = grad_middle + grad_from_first
    input_grad = low(grad_input)
    radial_grad = scale_one[:, 0] * jnp.sum(resid * grad_input, axis=1) / model**0.5

    sums = jnp.concatenate(
        [sums[:RATE_ROW], -rates_own * residues_own * sums[RATE_ROW:]], axis=0
    )
    sums = sum((net.turn(sums, s) for s in range(1, net.groups)), sums)
    sums = in_order(sums[None], net.x(sums)[None], x, 0)[None]
    sums = in_order(sums, net.c(sums), c, 0)[None]
    sums = in_order(sums, net.y(sums), y, 0)
    sums = sums.reshape(8, COEF_ROWS, channels).transpose(1, 0, 2).reshape(COEF_ROWS, model)
    grad_taps = sums[: 3 * TAPS].reshape(taps.shape)
    grad_skip = sums[SKIP_ROW]
    grad_residues = sums[RES_ROW:RATE_ROW]
    grad_log_rates = sums[RATE_ROW:]

    totals = (total_in, total_out, total_gate, total_up, total_down)
    square_big = sum((jnp.sum(grad * grad) for grad in totals))
    last = jnp.concatenate(
        [gain_one.reshape(-1, LANES), gain_two.reshape(-1, LANES), jnp.full((8, LANES), square_big)]
    )
    last = last + net.x(last)
    last = last + net.y(last)
    last = last + net.c(last)
    last = sum((net.turn(last, s) for s in range(1, net.groups)), last)
    span = model // LANES
    grad_gains = last[: 2 * span].reshape(2, model)
    small = (grad_gains, grad_taps, grad_residues, grad_log_rates, grad_skip)
    square_total = last[2 * span, 0] + sum((jnp.sum(grad * grad) for grad in small))
    grad_norm = jnp.sqrt(square_total)
    factor = jnp.minimum(1.0, CLIP / (grad_norm + 1e-06))

    pair_in, pair_out, pair_gate, pair_up, pair_down = (
        trade_units(net, total, x) for total in totals
    )
    shard_in = (
        pair_in.reshape(2, tiles, 3, LANES, depth)
        .transpose(4, 2, 0, 1, 3)
        .reshape(depth, 3, 2 * channels)
    )
    shard_out = pair_out.reshape(2 * channels, depth)
    shard_gate = pair_gate.reshape(2 * hidden, depth).T
    shard_up = pair_up.reshape(2 * hidden, depth).T
    shard_down = pair_down.reshape(2 * hidden, depth)

    return (
        output,
        input_grad,
        radial_grad,
        *adam(gains, gains_first, gains_second, grad_gains * factor, RATE_SMALL, 0.0),
        *adam(taps, taps_first, taps_second, grad_taps * factor, RATE_SMALL, 0.0),
        *adam(
            residues, residues_first, residues_second, grad_residues * factor, RATE_SMALL, 0.0
        ),
        *adam(
            log_rates,
            log_rates_first,
            log_rates_second,
            grad_log_rates * factor,
            RATE_RATES,
            0.0,
        ),
        *adam(skip, skip_first, skip_second, grad_skip * factor, RATE_SMALL, 0.0),
        *adam(
            in_weight, in_weight_first, in_weight_second, shard_in * factor, RATE_MATRIX, DECAY
        ),
        *adam(
            out_weight, out_weight_first, out_weight_second, shard_out * factor, RATE_MATRIX, DECAY
        ),
        *adam(
            gate_weight,
            gate_weight_first,
            gate_weight_second,
            shard_gate * factor,
            RATE_MATRIX,
            DECAY,
        ),
        *adam(up_weight, up_weight_first, up_weight_second, shard_up * factor, RATE_MATRIX, DECAY),
        *adam(
            down_weight,
            down_weight_first,
            down_weight_second,
            shard_down * factor,
            RATE_MATRIX,
            DECAY,
        ),
        grad_norm,
    )


def solution(mesh):
    net = Links(mesh.shape["dp"] // 2, mesh.shape["mp"])
    rows = P(("dp", "mp"), None)
    split_in = P("dp", None, "mp")
    split_out = P("mp", "dp")
    split_up = P("dp", "mp")
    matrices = (split_in,) * 3 + (split_out,) * 3 + (split_up,) * 6 + (split_out,) * 3
    return jax.shard_map(
        functools.partial(on_device, net),
        mesh=mesh,
        in_specs=(rows, rows, P("dp"), P()) + (P(),) * 15 + matrices,
        out_specs=(rows, rows, P(("dp", "mp"))) + (P(),) * 15 + matrices + (P(),),
        check_vma=False,
    )
```

```python
import functools

import jax
import jax.numpy as jnp
from jax import lax
from jax.experimental import pallas as pl
from jax.experimental.pallas import tpu as pltpu
from jax.sharding import PartitionSpec as P

STEP = 10


EPSILON = 1e-05
CLIP = 1.0
BETA_ONE = 0.9
BETA_TWO = 0.95
ADAM_EPSILON = 1e-08
DECAY = 0.1
RATE_MATRIX = 0.05
RATE_SMALL = 0.5
RATE_RATES = 4.0

LANES = 128
CHUNK = 128
CHUNKS = 8
LENGTH = CHUNK * CHUNKS
PAD = 8
TAPS = 3
POLES = 16
SKIP_ROW = TAPS * 3
RES_ROW = 16
RATE_ROW = RES_ROW + POLES
COEF_ROWS = RATE_ROW + POLES
MODE_GROUP = 8

f32 = jnp.float32
bf16 = jnp.bfloat16


def chunk_row(pos_ref, seq, n):
    block, half = n // 2, n % 2
    y, c = pos_ref[0], pos_ref[1]
    dy = y if block // 2 == 0 else 1 - y
    dc = c if block % 2 == 0 else 1 - c
    if half == 0:
        row = dc * LENGTH + seq * (4 * CHUNK) + dy * CHUNK
    else:
        row = dc * LENGTH + dy * (4 * CHUNK) + 2 * CHUNK + seq * CHUNK
    return pl.multiple_of(row, CHUNK)


def mix_chunk(pad_ref, coef, which, n):
    base = PAD + n * CHUNK
    total = coef[which : which + 1, :] * pad_ref[pl.ds(base, CHUNK), :]
    for i in range(1, TAPS):
        row = 3 * i + which
        total = total + coef[row : row + 1, :] * pad_ref[pl.ds(base - i, CHUNK), :]
    return total


def spread(row):
    return jnp.broadcast_to(row, (CHUNKS, LANES))


def power_of_two(value, doublings):
    for _ in range(doublings):
        value = value * value
    return value


def shift_down(value, count):
    rolled = pltpu.roll(value, count, 0)
    place = lax.broadcasted_iota(jnp.int32, (CHUNKS, LANES), 0)
    return jnp.where(place >= count, rolled, 0.0)


def shift_up(value, count):
    rolled = pltpu.roll(value, CHUNKS - count, 0)
    place = lax.broadcasted_iota(jnp.int32, (CHUNKS, LANES), 0)
    return jnp.where(place < CHUNKS - count, rolled, 0.0)


def tile_rows(t):
    return pl.ds(pl.multiple_of(t * CHUNKS, CHUNKS), CHUNKS)


def forward_kernel(pos_ref, proj_ref, coef_ref, branch_ref, conv_ref, pads, u_ref, y_ref):
    coef = coef_ref[...]
    decay = [spread(coef[RATE_ROW + p : RATE_ROW + p + 1, :]) for p in range(POLES)]
    weight = [spread(coef[RES_ROW + p : RES_ROW + p + 1, :]) for p in range(POLES)]
    skip = coef[SKIP_ROW : SKIP_ROW + 1, :]
    y_ref[pl.ds(0, CHUNKS), :] = jnp.zeros((CHUNKS, LANES), f32)
    zero = y_ref[pl.ds(0, CHUNKS), :]
    for seq in range(2):
        for j in range(3):
            pads[j, pl.ds(0, PAD), :] = jnp.zeros((PAD, LANES), f32)
        for n in range(CHUNKS):
            rows = pl.ds(chunk_row(pos_ref, seq, n), CHUNK)
            for j in range(3):
                pads[j, pl.ds(PAD + n * CHUNK, CHUNK), :] = proj_ref[
                    rows, j * LANES : (j + 1) * LANES
                ]
        for n in range(CHUNKS):
            gated = mix_chunk(pads.at[1], coef, 1, n) * mix_chunk(pads.at[2], coef, 2, n)
            u_ref[pl.ds(n, CHUNK, stride=CHUNKS), :] = gated

        def ends(t, state):
            u = u_ref[tile_rows(t), :]
            return [a * h + u for a, h in zip(decay, state)]

        state = lax.fori_loop(0, CHUNK, ends, [zero] * POLES, unroll=2)
        start = []
        for a, h in zip(decay, state):
            jump = power_of_two(a, 7)
            for count in (1, 2, 4):
                h = h + jump * shift_down(h, count)
                jump = jump * jump
            start.append(shift_down(h, 1))

        def outputs(t, state):
            u = u_ref[tile_rows(t), :]
            state = [a * h + u for a, h in zip(decay, state)]
            terms = [w * h for w, h in zip(weight, state)]
            while len(terms) > 1:
                terms = [l + r for l, r in zip(terms[0::2], terms[1::2])]
            y_ref[tile_rows(t), :] = terms[0]
            return state

        lax.fori_loop(0, CHUNK, outputs, start, unroll=2)
        for n in range(CHUNKS):
            rows = pl.ds(chunk_row(pos_ref, seq, n), CHUNK)
            strided = pl.ds(n, CHUNK, stride=CHUNKS)
            conv = y_ref[strided, :] + skip * u_ref[strided, :]
            conv_ref[rows, :] = conv
            branch_ref[rows, :] = (mix_chunk(pads.at[0], coef, 0, n) * conv).astype(bf16)


def backward_kernel(
    pos_ref,
    proj_ref,
    conv_ref,
    grad_ref,
    coef_ref,
    out_ref,
    sums_ref,
    pads,
    mixed,
    grads,
    u_ref,
    g_ref,
    y_ref,
):
    coef = coef_ref[...]
    decay = [spread(coef[RATE_ROW + p : RATE_ROW + p + 1, :]) for p in range(POLES)]
    weight = [spread(coef[RES_ROW + p : RES_ROW + p + 1, :]) for p in range(POLES)]
    skip = coef[SKIP_ROW : SKIP_ROW + 1, :]
    y_ref[pl.ds(0, CHUNKS), :] = jnp.zeros((CHUNKS, LANES), f32)
    zero = y_ref[pl.ds(0, CHUNKS), :]
    row_zero = jnp.zeros((1, LANES), f32)
    tap_sums = [row_zero] * (3 * TAPS)
    skip_sum = row_zero
    res_sums = [zero] * POLES
    rate_sums = [zero] * POLES
    for seq in range(2):
        for j in range(3):
            pads[j, pl.ds(0, PAD), :] = jnp.zeros((PAD, LANES), f32)
            grads[j, pl.ds(LENGTH, PAD), :] = jnp.zeros((PAD, LANES), f32)
        for n in range(CHUNKS):
            rows = pl.ds(chunk_row(pos_ref, seq, n), CHUNK)
            for j in range(3):
                pads[j, pl.ds(PAD + n * CHUNK, CHUNK), :] = proj_ref[
                    rows, j * LANES : (j + 1) * LANES
                ]
        for n in range(CHUNKS):
            rows = pl.ds(chunk_row(pos_ref, seq, n), CHUNK)
            strided = pl.ds(n, CHUNK, stride=CHUNKS)
            plain = pl.ds(n * CHUNK, CHUNK)
            query = mix_chunk(pads.at[0], coef, 0, n)
            key = mix_chunk(pads.at[1], coef, 1, n)
            value = mix_chunk(pads.at[2], coef, 2, n)
            mixed[0, plain, :] = key
            mixed[1, plain, :] = value
            branch_grad = grad_ref[rows, :]
            grads[0, plain, :] = branch_grad * conv_ref[rows, :]
            u_ref[strided, :] = key * value
            g_ref[strided, :] = branch_grad * query

        def ends(step, state):
            g = g_ref[tile_rows(CHUNK - 1 - step), :]
            after = []
            for a, (b, e) in zip(decay, state):
                ab = a * b
                after.append((ab + g, a * e + ab))
            return after

        state = lax.fori_loop(0, CHUNK, ends, [(zero, zero)] * POLES, unroll=2)
        start = []
        for a, (b, e) in zip(decay, state):
            jump = power_of_two(a, 7)
            span = float(CHUNK)
            for count in (1, 2, 4):
                b_next, e_next = shift_up(b, count), shift_up(e, count)
                e = e + jump * (e_next + span * b_next)
                b = b + jump * b_next
                jump = jump * jump
                span = 2.0 * span
            start.append((shift_up(b, 1), shift_up(e, 1)))

        for first in range(0, POLES, MODE_GROUP):
            modes = range(first, first + MODE_GROUP)

            def outputs(step, state, modes=modes, first=first):
                t = CHUNK - 1 - step
                g = g_ref[tile_rows(t), :]
                u = u_ref[tile_rows(t), :]
                after, terms = [], []
                for p, (b, e, res, rate) in zip(modes, state):
                    ab = decay[p] * b
                    e = decay[p] * e + ab
                    b = ab + g
                    terms.append(weight[p] * b)
                    after.append((b, e, res + u * b, rate + u * e))
                while len(terms) > 1:
                    terms = [l + r for l, r in zip(terms[0::2], terms[1::2])]
                total = terms[0]
                if first > 0:
                    total = total + y_ref[tile_rows(t), :]
                y_ref[tile_rows(t), :] = total
                return after

            begin = [(*start[p], res_sums[p], rate_sums[p]) for p in modes]
            after = lax.fori_loop(0, CHUNK, outputs, begin, unroll=2)
            for p, (_, _, res, rate) in zip(modes, after):
                res_sums[p], rate_sums[p] = res, rate

        for n in range(CHUNKS):
            strided = pl.ds(n, CHUNK, stride=CHUNKS)
            plain = pl.ds(n * CHUNK, CHUNK)
            conv_grad = g_ref[strided, :]
            gated_grad = y_ref[strided, :] + skip * conv_grad
            skip_sum = skip_sum + jnp.sum(conv_grad * u_ref[strided, :], axis=0, keepdims=True)
            grads[1, plain, :] = gated_grad * mixed[1, plain, :]
            grads[2, plain, :] = gated_grad * mixed[0, plain, :]
        for n in range(CHUNKS):
            rows = pl.ds(chunk_row(pos_ref, seq, n), CHUNK)
            for j in range(3):
                here = grads[j, pl.ds(n * CHUNK, CHUNK), :]
                total = coef[j : j + 1, :] * here
                for i in range(TAPS):
                    behind = pads[j, pl.ds(PAD + n * CHUNK - i, CHUNK), :]
                    row = 3 * i + j
                    tap_sums[row] = tap_sums[row] + jnp.sum(here * behind, axis=0, keepdims=True)
                    if i > 0:
                        ahead = grads[j, pl.ds(n * CHUNK + i, CHUNK), :]
                        total = total + coef[row : row + 1, :] * ahead
                out_ref[rows, j * LANES : (j + 1) * LANES] = total.astype(bf16)
    for row in range(3 * TAPS):
        sums_ref[row : row + 1, :] = tap_sums[row]
    sums_ref[SKIP_ROW : SKIP_ROW + 1, :] = skip_sum
    for row in range(SKIP_ROW + 1, RES_ROW):
        sums_ref[row : row + 1, :] = row_zero
    for p in range(POLES):
        sums_ref[RES_ROW + p : RES_ROW + p + 1, :] = jnp.sum(res_sums[p], axis=0, keepdims=True)
        sums_ref[RATE_ROW + p : RATE_ROW + p + 1, :] = jnp.sum(
            rate_sums[p], axis=0, keepdims=True
        )


def mixer_forward(position, proj, coef):
    rows, channels = proj.shape[0], coef.shape[1]
    return pl.pallas_call(
        forward_kernel,
        grid=(channels // LANES,),
        in_specs=[
            pl.BlockSpec(memory_space=pltpu.SMEM),
            pl.BlockSpec((rows, 3 * LANES), lambda i: (0, i)),
            pl.BlockSpec((COEF_ROWS, LANES), lambda i: (0, i)),
        ],
        out_specs=[
            pl.BlockSpec((rows, LANES), lambda i: (0, i)),
            pl.BlockSpec((rows, LANES), lambda i: (0, i)),
        ],
        out_shape=[
            jax.ShapeDtypeStruct((rows, channels), bf16),
            jax.ShapeDtypeStruct((rows, channels), f32),
        ],
        scratch_shapes=[
            pltpu.VMEM((3, PAD + LENGTH, LANES), f32),
            pltpu.VMEM((LENGTH, LANES), f32),
            pltpu.VMEM((LENGTH, LANES), f32),
        ],
        compiler_params=pltpu.CompilerParams(vmem_limit_bytes=28 << 20),
        cost_estimate=pl.CostEstimate(
            flops=1 << 20, bytes_accessed=1 << 10, transcendentals=0
        ),
        name="mixer_forward",
    )(position, proj, coef)


def mixer_backward(position, proj, conv, grad, coef, tile):
    rows = proj.shape[0]
    return pl.pallas_call(
        backward_kernel,
        grid=(1,),
        in_specs=[
            pl.BlockSpec(memory_space=pltpu.SMEM),
            pl.BlockSpec((rows, 3 * LANES), lambda i: (0, tile)),
            pl.BlockSpec((rows, LANES), lambda i: (0, tile)),
            pl.BlockSpec((rows, LANES), lambda i: (0, tile)),
            pl.BlockSpec((COEF_ROWS, LANES), lambda i: (0, tile)),
        ],
        out_specs=[
            pl.BlockSpec((rows, 3 * LANES), lambda i: (0, 0)),
            pl.BlockSpec((COEF_ROWS, LANES), lambda i: (0, 0)),
        ],
        out_shape=[
            jax.ShapeDtypeStruct((rows, 3 * LANES), bf16),
            jax.ShapeDtypeStruct((COEF_ROWS, LANES), f32),
        ],
        scratch_shapes=[
            pltpu.VMEM((3, PAD + LENGTH, LANES), f32),
            pltpu.VMEM((2, LENGTH, LANES), f32),
            pltpu.VMEM((3, LENGTH + PAD, LANES), f32),
            pltpu.VMEM((LENGTH, LANES), f32),
            pltpu.VMEM((LENGTH, LANES), f32),
            pltpu.VMEM((LENGTH, LANES), f32),
        ],
        compiler_params=pltpu.CompilerParams(vmem_limit_bytes=32 << 20),
        cost_estimate=pl.CostEstimate(
            flops=1 << 20, bytes_accessed=1 << 10, transcendentals=0
        ),
        name="mixer_backward",
    )(position, proj, conv, grad, coef)


TILE = 256
NO_COST = pl.CostEstimate(flops=1 << 10, bytes_accessed=1 << 10, transcendentals=0)
NT = (((1,), (1,)), ((), ()))
NN = (((1,), (0,)), ((), ()))


def whole_spec(array):
    return pl.BlockSpec(array.shape, lambda i: (0,) * array.ndim, pipeline_mode=pl.Buffered(1))


def up_kernel(scales, rows_ref, gate_w, up_w, inner_ref, scaled_ref, by_gate_ref, by_up_ref):
    piece = TILE // 2
    gate_all = lax.dot_general(rows_ref[...], gate_w[...], NT, preferred_element_type=f32)
    up_all = lax.dot_general(rows_ref[...], up_w[...], NT, preferred_element_type=f32)
    for part in range(2):
        at = slice(part * piece, (part + 1) * piece)
        index = lax.rem(2 * pl.program_id(0) + part, 8)
        other = jnp.where(lax.rem(index, 4) < 2, index // 4, lax.rem(index, 2))
        scale = jnp.where(other == 1, scales[1], scales[0])
        gate, up = gate_all[at], up_all[at]
        sigma = jax.nn.sigmoid(gate)
        silu = gate * sigma
        inner = silu * up
        inner_ref[at, :] = inner.astype(bf16)
        scaled_ref[at, :] = (inner * scale).astype(bf16)
        by_gate_ref[at, :] = (scale * up * sigma * (1.0 + gate * (1.0 - sigma))).astype(bf16)
        by_up_ref[at, :] = (scale * silu).astype(bf16)


def ffn_up(scales, rows, gate_w, up_w):
    count, hidden = rows.shape[0], gate_w.shape[0]
    tile = pl.BlockSpec((TILE, hidden), lambda i: (i, 0))
    return pl.pallas_call(
        up_kernel,
        grid=(count // TILE,),
        in_specs=[
            pl.BlockSpec(memory_space=pltpu.SMEM),
            pl.BlockSpec((TILE, rows.shape[1]), lambda i: (i, 0)),
            whole_spec(gate_w),
            whole_spec(up_w),
        ],
        out_specs=[tile] * 4,
        out_shape=[jax.ShapeDtypeStruct((count, hidden), bf16)] * 4,
        compiler_params=pltpu.CompilerParams(vmem_limit_bytes=24 << 20),
        cost_estimate=NO_COST,
        name="ffn_up",
    )(scales, rows, gate_w, up_w)


def rows_kernel(left, right, out):
    out[...] = lax.dot_general(left[...], right[...], NT, preferred_element_type=f32)


def rows_product(left, right):
    count, width = left.shape
    return pl.pallas_call(
        rows_kernel,
        grid=(count // TILE,),
        in_specs=[pl.BlockSpec((TILE, width), lambda i: (i, 0)), whole_spec(right)],
        out_specs=pl.BlockSpec((TILE, right.shape[0]), lambda i: (i, 0)),
        out_shape=jax.ShapeDtypeStruct((count, right.shape[0]), f32),
        compiler_params=pltpu.CompilerParams(vmem_limit_bytes=24 << 20),
        cost_estimate=NO_COST,
        name="rows_product",
    )(left, right)


def grad_kernel(rows_ref, down_w, by_gate_ref, by_up_ref, gate_ref, up_ref):
    grad = lax.dot_general(rows_ref[...], down_w[...], NT, preferred_element_type=f32)
    gate_ref[...] = (grad * by_gate_ref[...].astype(f32)).astype(bf16)
    up_ref[...] = (grad * by_up_ref[...].astype(f32)).astype(bf16)


def ffn_grad(rows, down_w, by_gate, by_up):
    count, hidden = rows.shape[0], down_w.shape[0]
    tile = pl.BlockSpec((TILE, hidden), lambda i: (i, 0))
    return pl.pallas_call(
        grad_kernel,
        grid=(count // TILE,),
        in_specs=[
            pl.BlockSpec((TILE, rows.shape[1]), lambda i: (i, 0)),
            whole_spec(down_w),
            tile,
            tile,
        ],
        out_specs=[tile] * 2,
        out_shape=[jax.ShapeDtypeStruct((count, hidden), bf16)] * 2,
        compiler_params=pltpu.CompilerParams(vmem_limit_bytes=24 << 20),
        cost_estimate=NO_COST,
        name="ffn_grad",
    )(rows, down_w, by_gate, by_up)


def product_kernel(count, adds, tiles, *refs):
    lefts, rights = refs[:count], refs[count : 2 * count]
    outs = refs[-tiles:]
    total = None
    for left, right in zip(lefts, rights):
        term = lax.dot_general(left[...], right[...], NN, preferred_element_type=f32)
        total = term if total is None else total + term
    for tile in range(tiles):

        @pl.when(pl.program_id(0) == tile)
        def _(tile=tile):
            if adds:
                outs[tile][...] = (total + refs[2 * count + tile][...].astype(f32)).astype(bf16)
            else:
                outs[tile][...] = total.astype(bf16)


def product_tiles(lefts, rights, first, tiles, adds=()):
    width = rights[0].shape[1]
    start = first // TILE
    tile_spec = pl.BlockSpec((TILE, width), lambda i: (0, 0))
    return pl.pallas_call(
        functools.partial(product_kernel, len(lefts), len(adds), tiles),
        grid=(tiles,),
        in_specs=[
            pl.BlockSpec((TILE, left.shape[1]), lambda i: (start + i, 0)) for left in lefts
        ]
        + [whole_spec(right) for right in rights]
        + [whole_spec(add) for add in adds],
        out_specs=[tile_spec] * tiles,
        out_shape=[jax.ShapeDtypeStruct((TILE, width), bf16)] * tiles,
        compiler_params=pltpu.CompilerParams(vmem_limit_bytes=28 << 20),
        cost_estimate=NO_COST,
        name="product",
    )(*lefts, *rights, *adds)


def halves_spec(rows, depth):
    return [jax.ShapeDtypeStruct((rows, depth), bf16)] * 2


def mixer_weights_kernel(where_ref, in_ref, out_ref, in_mine, in_other, out_mine, out_other):
    units = in_ref.shape[2] // 2
    tiles = units // LANES
    for side, target in ((where_ref[3], in_mine), (1 - where_ref[3], in_other)):
        for tile in range(tiles):
            start = pl.multiple_of(side * units + tile * LANES, LANES)
            for j in range(3):
                row = (tile * 3 + j) * LANES
                block = in_ref[j, :, pl.ds(start, LANES)]
                target[row : row + LANES, :] = block.T.astype(bf16)
    for side, target in ((where_ref[3], out_mine), (1 - where_ref[3], out_other)):
        rows = pl.ds(pl.multiple_of(side * units, units), units)
        target[...] = out_ref[rows, :].astype(bf16)


def mixer_weights(where, in_weight, out_weight):
    _, depth, channels = in_weight.shape
    units = channels // 2
    return pl.pallas_call(
        mixer_weights_kernel,
        in_specs=[pl.BlockSpec(memory_space=pltpu.SMEM)]
        + [pl.BlockSpec(memory_space=pltpu.VMEM)] * 2,
        out_specs=[pl.BlockSpec(memory_space=pltpu.VMEM)] * 4,
        out_shape=halves_spec(3 * units, depth) + halves_spec(units, depth),
        compiler_params=pltpu.CompilerParams(vmem_limit_bytes=12 << 20),
        cost_estimate=NO_COST,
        name="mixer_weights",
    )(where, in_weight, out_weight)


def ffn_weights_kernel(
    where_ref, gate_ref, up_ref, down_ref, mine, other, down_mine, down_other, turned
):
    units = down_ref.shape[0] // 2
    mine_rows = pl.ds(pl.multiple_of(where_ref[3] * units, units), units)
    other_rows = pl.ds(pl.multiple_of((1 - where_ref[3]) * units, units), units)
    for n, source in enumerate((gate_ref, up_ref)):
        turned[...] = source[...].T
        mine[n * units : (n + 1) * units, :] = turned[mine_rows, :].astype(bf16)
        other[n * units : (n + 1) * units, :] = turned[other_rows, :].astype(bf16)
    down_mine[...] = down_ref[mine_rows, :].astype(bf16)
    down_other[...] = down_ref[other_rows, :].astype(bf16)


def ffn_weights(where, gate_weight, up_weight, down_weight):
    units, depth = down_weight.shape
    return pl.pallas_call(
        ffn_weights_kernel,
        in_specs=[pl.BlockSpec(memory_space=pltpu.SMEM)]
        + [pl.BlockSpec(memory_space=pltpu.VMEM)] * 3,
        out_specs=[pl.BlockSpec(memory_space=pltpu.VMEM)] * 4,
        out_shape=halves_spec(units, depth) + halves_spec(units // 2, depth),
        scratch_shapes=[pltpu.VMEM((units, depth), f32)],
        compiler_params=pltpu.CompilerParams(vmem_limit_bytes=20 << 20),
        cost_estimate=NO_COST,
        name="ffn_weights",
    )(where, gate_weight, up_weight, down_weight)


def weight_grad_kernel(left, right, out):
    out[...] = lax.dot_general(
        left[...], right[...], (((0,), (0,)), ((), ())), preferred_element_type=f32
    ).astype(bf16)


def weight_product(left, right, blocks=0):
    depth, units = left.shape
    width = right.shape[1]
    if blocks:
        tile = width // blocks
        out_spec = pl.BlockSpec((None, units, tile), lambda i: (i, 0, 0))
        shape = (blocks, units, tile)
    else:
        tile = min(width, 512)
        out_spec = pl.BlockSpec((units, tile), lambda i: (0, i))
        shape = (units, width)
    return pl.pallas_call(
        weight_grad_kernel,
        grid=(width // tile,),
        in_specs=[whole_spec(left), pl.BlockSpec((depth, tile), lambda i: (0, i))],
        out_specs=out_spec,
        out_shape=jax.ShapeDtypeStruct(shape, bf16),
        compiler_params=pltpu.CompilerParams(vmem_limit_bytes=28 << 20),
        cost_estimate=NO_COST,
        name="weight_product",
    )(left, right)


def rows_by_rows(left, right):
    return lax.dot_general(left, right, (((1,), (1,)), ((), ())), preferred_element_type=f32)


def columns_by_columns(left, right):
    return lax.dot_general(left, right, (((0,), (0,)), ((), ())), preferred_element_type=f32)


def plain_dot(left, right):
    return jnp.dot(left, right, preferred_element_type=f32)


def low(values):
    return values.astype(bf16)


def add_low(left, right):
    return (left.astype(f32) + right.astype(f32)).astype(bf16)


def norm_back(values, scale, gain, grad):
    weighted = grad * gain
    inner_mean = jnp.mean(values * weighted, axis=1, keepdims=True)
    return (
        scale * weighted - values * (scale * scale * scale) * inner_mean,
        jnp.sum(grad * values * scale, axis=0),
    )


def adam(weight, first, second, grad, rate, decay):
    first_new = BETA_ONE * first + (1.0 - BETA_ONE) * grad
    second_new = BETA_TWO * second + (1.0 - BETA_TWO) * grad * grad
    stride = (
        first_new
        / (1.0 - BETA_ONE**STEP)
        / (jnp.sqrt(second_new / (1.0 - BETA_TWO**STEP)) + ADAM_EPSILON)
    )
    return (weight - rate * (stride + decay * weight), first_new, second_new)


class Links:
    def __init__(self, groups):
        self.groups = groups
        places = [(z, x) for z in range(groups) for x in (0, 1)]
        self.ring = [(2 * z + x, 2 * ((z + 1) % groups) + x) for z, x in places]
        self.lines = [[2 * z + x for z in range(groups)] for x in (0, 1)]
        self.over_x = [(2 * z + x, 2 * z + 1 - x) for z, x in places]
        self.over_y = [(2 * y + c, 2 * (1 - y) + c) for y in (0, 1) for c in (0, 1)]
        self.over_c = [(2 * y + c, 2 * y + 1 - c) for y in (0, 1) for c in (0, 1)]
        self.bits = [1 << n for n in range(groups.bit_length() - 1)]
        self.across = {
            bit: [(2 * z + x, 2 * (z ^ bit) + x) for z, x in places] for bit in self.bits
        }

    def z(self, v):
        return lax.ppermute(v, "dp", self.ring)

    def z_across(self, v, bit):
        return lax.ppermute(v, "dp", self.across[bit])

    def x(self, v):
        return lax.ppermute(v, "dp", self.over_x)

    def y(self, v):
        return lax.ppermute(v, "mp", self.over_y)

    def c(self, v):
        return lax.ppermute(v, "mp", self.over_c)


def tie(value, *before):
    return lax.optimization_barrier((value, *before))[0] if before else value


class Chain:
    def __init__(self):
        self.held = ()

    def __call__(self, value, *before):
        return tie(value, *self.held, *before)

    def mark(self, *done):
        self.held = done

    def wait(self, *arrived):
        together = lax.optimization_barrier((*arrived, *self.held))[: len(arrived)]
        self.held = together[:1]
        return together[0] if len(arrived) == 1 else together


def copy_kernel(count, place, *refs):
    where, pieces, whole, sems = refs[0], refs[1 : count + 1], refs[count + 1], refs[count + 2]
    copies = [
        pltpu.make_async_copy(piece, whole.at[place(where, i)], sems.at[i])
        for i, piece in enumerate(pieces)
    ]
    for copy in copies:
        copy.start()
    for copy in copies:
        copy.wait()


def assemble_columns(first, pieces, place, where, shape):
    arrays, offsets = [first], [pieces[0][1]]
    index = []
    for i, (array, offset) in enumerate(pieces):
        known = [n for n, other in enumerate(arrays) if other is array]
        if i == 0:
            index.append((0, offset))
        elif array is pieces[0][0]:
            index.append((0, offset))
        elif known:
            index.append((known[0], offset))
        else:
            arrays.append(array)
            index.append((len(arrays) - 1, offset))
    count = len(arrays)
    units = shape[0]

    def kernel(*refs):
        where_ref, sources, whole, sems = refs[0], refs[1 : count + 1], refs[count + 1], refs[-1]
        copies = [
            pltpu.make_async_copy(
                sources[n].at[pl.ds(offset, units), :],
                whole.at[place(where_ref, i)],
                sems.at[i],
            )
            for i, (n, offset) in enumerate(index)
        ]
        for copy in copies:
            copy.start()
        for copy in copies:
            copy.wait()

    return pl.pallas_call(
        kernel,
        in_specs=[pl.BlockSpec(memory_space=pltpu.SMEM)]
        + [pl.BlockSpec(memory_space=pl.ANY)] * count,
        out_specs=pl.BlockSpec(memory_space=pltpu.VMEM),
        out_shape=jax.ShapeDtypeStruct(shape, bf16),
        scratch_shapes=[pltpu.SemaphoreType.DMA((len(pieces),))],
        compiler_params=pltpu.CompilerParams(vmem_limit_bytes=8 << 20),
        cost_estimate=pl.CostEstimate(
            flops=0, bytes_accessed=4 * units * shape[1], transcendentals=0
        ),
        name="assemble_columns",
    )(where, *arrays)


def assemble_blocks(blocks, where):
    groups, rows, width = blocks.shape

    def kernel(where_ref, source, whole, sems):
        copies = [
            pltpu.make_async_copy(
                source.at[i], whole.at[:, pl.ds(i * width, width)], sems.at[i]
            )
            for i in range(groups)
        ]
        for copy in copies:
            copy.start()
        for copy in copies:
            copy.wait()

    return pl.pallas_call(
        kernel,
        in_specs=[pl.BlockSpec(memory_space=pltpu.SMEM), pl.BlockSpec(memory_space=pl.ANY)],
        out_specs=pl.BlockSpec(memory_space=pltpu.VMEM),
        out_shape=jax.ShapeDtypeStruct((rows, groups * width), bf16),
        scratch_shapes=[pltpu.SemaphoreType.DMA((groups,))],
        compiler_params=pltpu.CompilerParams(vmem_limit_bytes=10 << 20),
        cost_estimate=NO_COST,
        name="assemble_blocks",
    )(where, blocks)


def assemble_rows(pieces, where, shape):
    arrays = []
    for array, *_ in pieces:
        if not any(array is other for other in arrays):
            arrays.append(array)
    index = [next(n for n, other in enumerate(arrays) if other is p[0]) for p in pieces]
    count = len(arrays)

    def kernel(*refs):
        sources, whole, sems = refs[1 : count + 1], refs[-2], refs[-1]
        copies = []
        for i, (n, (_, start, rows, target)) in enumerate(zip(index, pieces)):
            source = sources[n].at[pl.ds(start, rows), :]
            copies.append(
                pltpu.make_async_copy(source, whole.at[pl.ds(target, rows), :], sems.at[i])
            )
        for copy in copies:
            copy.start()
        for copy in copies:
            copy.wait()

    return pl.pallas_call(
        kernel,
        in_specs=[pl.BlockSpec(memory_space=pltpu.SMEM)]
        + [pl.BlockSpec(memory_space=pl.ANY)] * count,
        out_specs=pl.BlockSpec(memory_space=pltpu.VMEM),
        out_shape=jax.ShapeDtypeStruct(shape, bf16),
        scratch_shapes=[pltpu.SemaphoreType.DMA((len(pieces),))],
        compiler_params=pltpu.CompilerParams(vmem_limit_bytes=10 << 20),
        cost_estimate=NO_COST,
        name="assemble_rows",
    )(where, *arrays)


class GatherRows:
    def __init__(self, net, chain, block):
        self.net, self.chain = net, chain
        half = block.shape[0] // 2
        self.a, self.b = block[:half], block[half:]
        self.a_x, self.b_y = net.x(self.a), net.y(self.b)

    def second(self, *more):
        net, chain = self.net, self.chain
        got = chain.wait(self.a_x, self.b_y, *more)
        a_x, b_y = got[:2]
        self.a = jnp.concatenate([self.a, a_x], axis=0)
        self.b = jnp.concatenate([self.b, b_y], axis=0)
        chain.mark(self.a, self.b)
        self.a_y, self.b_x = net.y(self.a), net.x(self.b)
        self.far_a, self.far_b = net.c(self.a), net.c(self.b)
        return got[2:]

    def third(self, *more):
        got = self.chain.wait(self.a_y, self.b_x, *more)
        self.a_y, self.b_x = got[:2]
        return got[2:]

    def trade(self):
        a_y, b_x = (tie(piece, *self.chain.held) for piece in (self.a_y, self.b_x))
        self.far_a_y, self.far_b_x = self.net.c(a_y), self.net.c(b_x)

    def whole(self, where):
        chain = self.chain
        far_a, far_b, far_a_y, far_b_x = chain.wait(
            self.far_a, self.far_b, self.far_a_y, self.far_b_x
        )
        rows = self.a.shape[0] // 2
        near = (self.a, self.a_y, self.b, self.b_x)
        far = (far_a, far_a_y, far_b, far_b_x)
        pieces = []
        for core, arrays in enumerate((near, far)):
            for place, array in enumerate(arrays):
                first = (8 * core + place) * rows
                pieces += [(array, 0, rows, first), (array, rows, rows, first + 4 * rows)]
        whole = assemble_rows(pieces, where, (16 * rows, self.a.shape[1]))
        chain.mark(whole)
        return whole


class ScatterProduct:
    def __init__(self, net, chain, lefts, rights):
        self.net, self.chain = net, chain
        self.lefts, self.rights = lefts, rights
        self.far = self.tiles(4, 4)

    def tiles(self, first, count, adds=()):
        lefts = [self.chain(self.lefts[0]), *self.lefts[1:]]
        tiles = product_tiles(lefts, self.rights, first * TILE, count, adds)
        self.chain.mark(tiles[0])
        return tiles

    def trade(self):
        held = [tie(tile, *self.chain.held) for tile in self.far]
        self.far = [self.net.c(tile) for tile in held]

    def near(self, *more):
        got = self.chain.wait(*self.far, *more)
        self.far = got[:4]
        self.for_x, self.for_y = self.tiles(2, 2, self.far[2:])
        return got[4:]

    def send(self):
        net = self.net
        for_x, for_y = (tie(tile, *self.chain.held) for tile in (self.for_x, self.for_y))
        self.from_x, self.from_y = net.x(for_x), net.y(for_y)

    def hold(self):
        self.a, self.b = self.tiles(0, 2, self.far[:2])

    def second(self, *more):
        net, chain, piece = self.net, self.chain, TILE // 2
        got = chain.wait(self.from_x, self.from_y, *more)
        self.from_x, self.from_y = got[:2]
        a_y = add_low(self.a[piece:], self.from_x[piece:])
        b_x = add_low(self.b[piece:], self.from_y[piece:])
        self.a_y, self.b_x = net.y(a_y), net.x(b_x)
        chain.mark(a_y, b_x)
        return got[2:]

    def last(self, *more):
        piece = TILE // 2
        got = self.chain.wait(self.a_y, self.b_x, *more)
        a_y, b_x = got[:2]
        a = self.a[:piece].astype(f32) + self.from_x[:piece].astype(f32) + a_y.astype(f32)
        b = self.b[:piece].astype(f32) + self.from_y[:piece].astype(f32) + b_x.astype(f32)
        return (jnp.concatenate([a, b], axis=0), *got[2:])


def pick(pair, index):
    return lax.dynamic_index_in_dim(pair, index, 0, keepdims=False)


def in_order(mine, other, x, axis):
    return jnp.where(
        x == 0,
        jnp.concatenate([mine, other], axis=axis),
        jnp.concatenate([other, mine], axis=axis),
    )


class GatherUnits:
    def __init__(self, net, chain, mine, other, x, z):
        self.net, self.chain, self.x, self.z = net, chain, x, z
        self.first, self.out = mine, other

    def trade(self, *after):
        self.got = self.net.x(tie(self.out, *after))

    def traded(self, merge, got=None):
        got = self.chain.wait(self.got) if got is None else got
        if merge:
            pair = self.chain(jnp.concatenate([self.first, got], axis=0))
            self.chain.mark(pair)
            self.rings = [[pair]]
        else:
            self.rings = [[self.first], [got]]

    def send(self, ring=0, *after):
        hops = self.rings[ring]
        hops.append(self.net.z(tie(hops[-1], *after)))

    def gather(self, first, last):
        pair = self.rings[0][0]
        units = pair.shape[0] // 2
        mine, other = pair[first:last], pair[units + first : units + last]
        piece = self.chain(in_order(mine, other, self.x, 1))
        self.chain.mark(piece)
        return lax.all_gather(piece, "dp", axis_index_groups=self.net.lines)

    def coming(self, ring=0):
        return self.rings[ring][-1]

    def came(self, piece, ring=0):
        self.rings[ring][-1] = piece

    def arrived(self, ring=0):
        self.came(self.chain.wait(self.coming(ring)), ring)

    def whole(self, where, ranges):
        groups, chain = self.net.groups, self.chain
        for ring in range(len(self.rings)):
            while len(self.rings[ring]) < groups:
                self.send(ring)
                self.arrived(ring)
        units, width = self.first.shape
        merged = len(self.rings) == 1
        wholes = []
        for first, last in ranges:
            pieces = []
            for step in range(groups):
                for side in range(2):
                    piece = self.rings[0 if merged else side][step]
                    offset = side * units if merged else 0
                    pieces.append((piece, offset + first))
            if width % LANES == 0:

                def place(where_ref, i):
                    block = lax.rem(where_ref[2] + (groups - i // 2), groups) * 2
                    side = where_ref[3] if i % 2 == 0 else 1 - where_ref[3]
                    start = pl.multiple_of((block + side) * width, LANES)
                    return (slice(None), pl.ds(start, width))

                shape = (last - first, 2 * width * groups)
                whole = assemble_columns(
                    chain(pieces[0][0]), pieces, place, where, shape
                )
            else:
                whole = jnp.zeros((last - first, 2 * width * groups), bf16)
                for i, (piece, offset) in enumerate(pieces):
                    block = 2 * lax.rem(self.z + groups - i // 2, groups)
                    side = self.x if i % 2 == 0 else 1 - self.x
                    part = piece[offset : offset + last - first]
                    whole = lax.dynamic_update_slice(whole, part, (0, (block + side) * width))
            chain.mark(whole)
            wholes.append(whole)
        return wholes


class ScatterUnits:
    def __init__(self, net, chain, grads, x, z, depth):
        self.net, self.chain, self.grads, self.x, self.z = net, chain, grads, x, z
        self.depth = depth
        self.step = 0
        self.total = self.part()
        chain.mark(self.total)
        self.hop()

    def part(self):
        groups = self.net.groups
        place = lax.rem(self.z + 2 * groups - 1 - self.step, groups)
        parts = [
            lax.dynamic_slice_in_dim(grad, place * 2 * self.depth, 2 * self.depth, 1)
            for grad in self.grads
        ]
        return parts[0] if len(parts) == 1 else jnp.concatenate(parts, axis=0)

    def hop(self):
        self.total = self.net.z(self.total)

    def got(self):
        self.came(self.chain.wait(self.total))

    def came(self, total):
        self.step += 1
        total = total.astype(f32) + self.part().astype(f32)
        self.total = low(total) if self.step < self.net.groups - 1 else total
        self.chain.mark(self.total)
        if self.step < self.net.groups - 1:
            self.hop()

    def finish(self):
        while self.step < self.net.groups - 1:
            self.got()
        self.square = jnp.sum(self.total * self.total)
        other = lax.dynamic_slice_in_dim(self.total, (1 - self.x) * self.depth, self.depth, 1)
        self.other = low(other)
        self.chain.mark(self.square, self.other)

    def trade(self):
        self.traded = self.net.x(tie(self.other, *self.chain.held))

    def pair(self):
        got, total = self.chain.wait(self.traded, self.total)
        mine = lax.dynamic_slice_in_dim(total, self.x * self.depth, self.depth, 1)
        got = got.astype(f32)
        return jnp.where(self.x == 0, jnp.stack([mine, got]), jnp.stack([got, mine]))


class ReducedUnits(ScatterUnits):
    def __init__(self, net, chain, blocks, x, z, depth):
        self.net, self.chain, self.x, self.z, self.depth = net, chain, x, z, depth
        self.step = net.groups - 1
        self.total = lax.psum_scatter(blocks, "dp", axis_index_groups=net.lines)

    def came(self, total):
        self.total = total.astype(f32)


def on_device(
    net,
    tokens,
    cotangent,
    group_ids,
    group_scales,
    gains,
    gains_first,
    gains_second,
    taps,
    taps_first,
    taps_second,
    residues,
    residues_first,
    residues_second,
    log_rates,
    log_rates_first,
    log_rates_second,
    skip,
    skip_first,
    skip_second,
    in_weight,
    in_weight_first,
    in_weight_second,
    out_weight,
    out_weight_first,
    out_weight_second,
    gate_weight,
    gate_weight_first,
    gate_weight_second,
    up_weight,
    up_weight_first,
    up_weight_second,
    down_weight,
    down_weight_first,
    down_weight_second,
):
    model = tokens.shape[1]
    depth = in_weight.shape[0]
    channels = in_weight.shape[2] // 2
    hidden = gate_weight.shape[1] // 2
    tiles = channels // LANES
    dp, mp = lax.axis_index("dp"), lax.axis_index("mp")
    z, x, y, c = dp // 2, dp % 2, mp // 2, mp % 2
    begin = (mp * 2 + x) * channels
    position = jnp.stack([y, c, z, x]).astype(jnp.int32)

    def own(array):
        return lax.dynamic_slice_in_dim(array, begin, channels, array.ndim - 1)

    chain = Chain()
    resid = tokens.astype(f32)
    scale_one = lax.rsqrt(jnp.mean(resid * resid, axis=1, keepdims=True) + EPSILON)
    normed = low(resid * scale_one * gains[0])
    chain.mark(normed)
    in_mine, in_other, out_mine, out_other = mixer_weights(
        position, chain(in_weight.transpose(1, 0, 2)), out_weight
    )
    chain.mark(in_mine)
    ring_in = GatherUnits(net, chain, in_mine, in_other, x, z)
    ring_in.trade()
    ring_in.rings = [[ring_in.first]]
    ring_in.send()
    ring_out = GatherUnits(net, chain, out_mine, out_other, x, z)
    sequence_scale = jnp.sum(
        jnp.where(
            group_ids[:, None] == jnp.arange(group_scales.shape[0], dtype=jnp.int32)[None, :],
            group_scales[None, :],
            0.0,
        )
    )

    first, got = chain.wait(ring_in.coming(0), ring_in.got)
    ring_in.came(first, 0)
    ring_in.rings.append([got])
    ring_in.send(0)
    ring_in.send(1)
    normed_rows = GatherRows(net, chain, chain(normed))
    gate_mine, gate_other, down_mine, down_other = ffn_weights(
        position, chain(gate_weight), up_weight, down_weight
    )
    chain.mark(gate_mine)
    ring_gu = GatherUnits(net, chain, gate_mine, gate_other, x, z)
    ring_down = GatherUnits(net, chain, down_mine, down_other, x, z)
    ring_out.trade()
    other_scale = net.x(chain(sequence_scale).reshape(1, 1))
    got, other_scale, first, second = normed_rows.second(
        ring_out.got, other_scale, ring_in.coming(0), ring_in.coming(1)
    )
    ring_in.came(first, 0)
    ring_in.came(second, 1)
    ring_in.send(0)
    ring_in.send(1)
    ring_out.traded(True, got)
    ring_out.send()
    residues_own = own(residues)
    rates_own = jnp.exp(own(log_rates))
    coef = jnp.concatenate(
        [
            own(taps).reshape(3 * TAPS, channels),
            own(skip)[None],
            jnp.zeros((RES_ROW - SKIP_ROW - 1, channels), f32),
            residues_own,
            jnp.exp(-rates_own),
        ],
        axis=0,
    )
    coef = chain(coef)
    chain.mark(coef)
    first, got, piece = normed_rows.third(
        ring_in.coming(0), ring_in.coming(1), ring_out.coming()
    )
    ring_in.came(first, 0)
    ring_in.came(got, 1)
    ring_out.came(piece)
    ring_in.send(1)
    ring_out.send()
    ring_gu.trade(*chain.held)
    normed_rows.trade()
    normed_all = normed_rows.whole(position)
    got, piece, traded = chain.wait(ring_in.coming(1), ring_out.coming(), ring_gu.got)
    ring_in.came(got, 1)
    ring_out.came(piece)
    ring_out.send()
    ring_gu.traded(True, traded)
    gate_blocks = ring_gu.gather(0, hidden)
    up_blocks = ring_gu.gather(hidden, 2 * hidden)
    cotangent = chain(cotangent)
    back_rows = GatherRows(net, chain, cotangent)
    (w_in,) = ring_in.whole(position, [(0, 3 * channels)])

    proj = rows_product(chain(normed_all), w_in)
    chain.mark(proj)
    back_rows.second()
    branch, conv = mixer_forward(position, chain(proj), coef)
    chain.mark(branch)
    (piece,) = back_rows.third(ring_out.coming())
    ring_out.came(piece)
    (w_out,) = ring_out.whole(position, [(0, channels)])
    product = ScatterProduct(net, chain, [branch], [w_out])
    product.trade()
    product.near()
    product.send()
    back_rows.trade()
    product.hold()
    back_all = back_rows.whole(position)
    (gate_blocks,) = product.second(gate_blocks)
    ring_down.trade(*chain.held)
    w_gate = assemble_blocks(chain(gate_blocks), position)
    chain.mark(w_gate)
    (more,) = product.last()
    middle = resid + more
    scale_two = lax.rsqrt(jnp.mean(middle * middle, axis=1, keepdims=True) + EPSILON)
    normed_two = low(middle * scale_two * gains[1])
    chain.mark(normed_two)
    normed_two_rows = GatherRows(net, chain, normed_two)
    normed_two_rows.second()
    got, up_blocks = chain.wait(ring_down.got, up_blocks)
    ring_down.traded(True, got)
    down_blocks = ring_down.gather(0, hidden)
    w_up = assemble_blocks(chain(up_blocks), position)
    chain.mark(w_up)
    scales = chain(jnp.concatenate([sequence_scale.reshape(1), other_scale.reshape(1)]))
    chain.mark(scales)
    normed_two_rows.third()
    normed_two_rows.trade()
    normed_two_all = normed_two_rows.whole(position)
    inner_low, inner_scaled, by_gate, by_up = ffn_up(
        scales, chain(normed_two_all), w_gate, w_up
    )
    chain.mark(inner_scaled, inner_low)

    def weight_grad(left, right):
        grad = weight_product(chain(left), right)
        chain.mark(grad)
        return grad

    def blocks_of(left, right):
        grad = weight_product(chain(left), right, net.groups)
        chain.mark(grad)
        return grad

    def reduced(grad):
        return ReducedUnits(net, chain, chain(grad), x, z, depth)

    def scattered(*grads):
        return ScatterUnits(net, chain, grads, x, z, depth)

    sum_down = reduced(blocks_of(inner_scaled, back_all))
    w_down = assemble_blocks(chain.wait(down_blocks), position)
    chain.mark(w_down)
    grad_gate, grad_up = ffn_grad(chain(back_all), w_down, by_gate, by_up)
    chain.mark(grad_gate, grad_up)
    product = ScatterProduct(net, chain, [grad_gate, grad_up], [w_gate, w_up])
    product.trade()
    product.near()
    product.send()
    product.hold()
    grad_gate = blocks_of(grad_gate, normed_two_all)
    grad_up = blocks_of(grad_up, normed_two_all)
    product.second()
    sum_gate, sum_up = reduced(grad_gate), reduced(grad_up)
    output_product = ScatterProduct(net, chain, [inner_low], [w_down])
    output_product.trade()
    (grad_normed_two,) = product.last()
    grad_from_norm, gain_two = norm_back(middle, scale_two, gains[1], grad_normed_two)
    grad_middle = cotangent.astype(f32) * sequence_scale + grad_from_norm
    grad_middle_low = low(grad_middle)
    chain.mark(grad_middle_low)
    grad_middle_rows = GatherRows(net, chain, grad_middle_low)
    output_product.near()
    output_product.hold()
    (got,) = grad_middle_rows.second(sum_down.total)
    sum_down.came(got)
    sum_down.finish()
    sum_gate.came(chain.wait(sum_gate.total))
    sum_gate.finish()
    grad_middle_rows.third()
    grad_middle_rows.trade()
    sum_down.trade()
    sum_gate.trade()
    output_product.send()
    grad_middle_all = grad_middle_rows.whole(position)
    grad_branch = rows_by_rows(chain(grad_middle_all), w_out)
    chain.mark(grad_branch)
    proj_grads, small_sums, sums_in = [], [], []
    for tile in range(tiles):
        part, sums = mixer_backward(position, proj, conv, chain(grad_branch), coef, tile)
        chain.mark(part)
        proj_grads.append(part)
        small_sums.append(sums)
        if tile == 0:
            sums_in.append(reduced(blocks_of(part, normed_all)))
    span_in = 3 * LANES
    w_in_parts = [w_in[tile * span_in : (tile + 1) * span_in] for tile in range(tiles)]
    product = ScatterProduct(net, chain, proj_grads, w_in_parts)
    product.trade()
    grads_in = [blocks_of(part, normed_all) for part in proj_grads[1:]]
    product.near()
    product.send()
    sums_in += [reduced(grad) for grad in grads_in]
    product.hold()
    output_product.second()
    grad_out = blocks_of(branch, grad_middle_all)

    sums = chain(jnp.concatenate(small_sums, axis=1))
    sums = jnp.concatenate(
        [sums[:RATE_ROW], -rates_own * residues_own * sums[RATE_ROW:]], axis=0
    )
    chain.mark(sums)
    sums_across = net.z_across(sums, net.bits[0])
    sum_up.came(chain.wait(sum_up.total))
    sum_up.finish()
    (across,) = product.second(sums_across)
    sum_out = reduced(grad_out)
    sum_up.trade()
    sums = chain(sums) + across
    chain.mark(sums)
    sums_across = net.z_across(sums, net.bits[1])
    (more,) = output_product.last()
    output = low(middle + more)
    chain.mark(output)

    def pair_of(total):
        pair = chain(total.pair())
        chain.mark(pair)
        return pair

    shard_down = pair_of(sum_down).reshape(2 * hidden, depth)
    shard_gate = chain(pair_of(sum_gate).reshape(2 * hidden, depth).T)
    chain.mark(shard_gate)
    grad_normed, first, across = product.last(sums_in[0].total, sums_across)
    sums = sums + across
    for bit in net.bits[2:]:
        sums = sums + net.z_across(sums, bit)
    sums_near = net.x(sums)
    grad_from_first, gain_one = norm_back(resid, scale_one, gains[0], grad_normed)
    grad_input = grad_middle + grad_from_first
    chain.mark(gain_one)
    sums_in[0].came(first)
    sums_in[0].finish()
    sums_in[0].trade()
    sums_in[1].came(chain.wait(sums_in[1].total))
    sums_in[1].finish()
    sums_in[1].trade()
    shard_up = chain(pair_of(sum_up).reshape(2 * hidden, depth).T)
    chain.mark(shard_up)
    sum_out.came(chain.wait(sum_out.total))
    sum_out.finish()
    sum_out.trade()

    totals = (sum_down, sum_gate, sum_up, sum_out, *sums_in)
    square = sum((total.square for total in totals)) + jnp.sum(sums * sums) / net.groups
    last = jnp.concatenate(
        [gain_one.reshape(-1, LANES), gain_two.reshape(-1, LANES), jnp.full((8, LANES), square)]
    )
    last = chain(last)
    chain.mark(last)
    sums = in_order(sums[None], chain.wait(sums_near)[None], x, 0)[None]
    across, more = chain.wait(net.c(last), net.c(sums))
    last = last + across
    sums = in_order(sums, more, c, 0)[None]
    for hop in (net.x, net.y):
        last = last + chain.wait(hop(last))
        chain.mark(last)
    for bit in net.bits:
        across = net.z_across(last, bit)
        if bit == net.bits[0]:
            more = net.y(tie(sums, last))
        if bit == net.bits[1]:
            shard_out = pair_of(sum_out).reshape(2 * channels, depth)
            shard_in = chain(
                jnp.stack([total.pair().reshape(2, 3, LANES, depth) for total in sums_in])
                .transpose(4, 2, 1, 0, 3)
                .reshape(depth, 3, 2 * channels)
            )
            chain.mark(shard_in)
        last = last + chain.wait(across)
        chain.mark(last)
    sums = in_order(sums, chain.wait(more), y, 0)
    input_grad = low(grad_input)
    radial_grad = scale_one[:, 0] * jnp.sum(resid * grad_input, axis=1) / model**0.5
    sums = sums.reshape(8, COEF_ROWS, channels).transpose(1, 0, 2).reshape(COEF_ROWS, model)
    grad_taps = sums[: 3 * TAPS].reshape(taps.shape)
    grad_skip = sums[SKIP_ROW]
    grad_residues = sums[RES_ROW:RATE_ROW]
    grad_log_rates = sums[RATE_ROW:]
    span = model // LANES
    grad_gains = last[: 2 * span].reshape(2, model)
    square_total = last[2 * span, 0] + jnp.sum(grad_gains * grad_gains)
    grad_norm = jnp.sqrt(square_total)
    factor = jnp.minimum(1.0, CLIP / (grad_norm + 1e-06))
    factor = tie(factor, shard_in, shard_out, shard_down, shard_gate, shard_up)

    return (
        output,
        input_grad,
        radial_grad,
        *adam(gains, gains_first, gains_second, grad_gains * factor, RATE_SMALL, 0.0),
        *adam(taps, taps_first, taps_second, grad_taps * factor, RATE_SMALL, 0.0),
        *adam(
            residues, residues_first, residues_second, grad_residues * factor, RATE_SMALL, 0.0
        ),
        *adam(
            log_rates,
            log_rates_first,
            log_rates_second,
            grad_log_rates * factor,
            RATE_RATES,
            0.0,
        ),
        *adam(skip, skip_first, skip_second, grad_skip * factor, RATE_SMALL, 0.0),
        *adam(
            in_weight, in_weight_first, in_weight_second, shard_in * factor, RATE_MATRIX, DECAY
        ),
        *adam(
            out_weight, out_weight_first, out_weight_second, shard_out * factor, RATE_MATRIX, DECAY
        ),
        *adam(
            gate_weight,
            gate_weight_first,
            gate_weight_second,
            shard_gate * factor,
            RATE_MATRIX,
            DECAY,
        ),
        *adam(up_weight, up_weight_first, up_weight_second, shard_up * factor, RATE_MATRIX, DECAY),
        *adam(
            down_weight,
            down_weight_first,
            down_weight_second,
            shard_down * factor,
            RATE_MATRIX,
            DECAY,
        ),
        grad_norm,
    )


def solution(mesh):
    net = Links(mesh.shape["dp"] // 2)
    rows = P(("dp", "mp"), None)
    split_in = P("dp", None, "mp")
    split_out = P("mp", "dp")
    split_up = P("dp", "mp")
    matrices = (split_in,) * 3 + (split_out,) * 3 + (split_up,) * 6 + (split_out,) * 3
    return jax.shard_map(
        functools.partial(on_device, net),
        mesh=mesh,
        in_specs=(rows, rows, P("dp"), P()) + (P(),) * 15 + matrices,
        out_specs=(rows, rows, P(("dp", "mp"))) + (P(),) * 15 + matrices + (P(),),
        check_vma=False,
    )
```

```python
import functools

import jax
import jax.numpy as jnp
from jax import lax
from jax.experimental import pallas as pl
from jax.experimental.pallas import tpu as pltpu
from jax.sharding import PartitionSpec as P

STEP = 10


EPSILON = 1e-05
CLIP = 1.0
BETA_ONE = 0.9
BETA_TWO = 0.95
ADAM_EPSILON = 1e-08
DECAY = 0.1
RATE_MATRIX = 0.05
RATE_SMALL = 0.5
RATE_RATES = 4.0

LANES = 128
CHUNK = 128
CHUNKS = 8
LENGTH = CHUNK * CHUNKS
PAD = 8
TAPS = 3
POLES = 16
SKIP_ROW = TAPS * 3
RES_ROW = 16
RATE_ROW = RES_ROW + POLES
COEF_ROWS = RATE_ROW + POLES
MODE_GROUP = 8

f32 = jnp.float32
bf16 = jnp.bfloat16


def chunk_row(pos_ref, seq, n):
    block, half = n // 2, n % 2
    y, c = pos_ref[0], pos_ref[1]
    dy = y if block // 2 == 0 else 1 - y
    dc = c if block % 2 == 0 else 1 - c
    if half == 0:
        row = dc * LENGTH + seq * (4 * CHUNK) + dy * CHUNK
    else:
        row = dc * LENGTH + dy * (4 * CHUNK) + 2 * CHUNK + seq * CHUNK
    return pl.multiple_of(row, CHUNK)


def mix_chunk(pad_ref, coef, which, n):
    base = PAD + n * CHUNK
    total = coef[which : which + 1, :] * pad_ref[pl.ds(base, CHUNK), :]
    for i in range(1, TAPS):
        row = 3 * i + which
        total = total + coef[row : row + 1, :] * pad_ref[pl.ds(base - i, CHUNK), :]
    return total


def spread(row):
    return jnp.broadcast_to(row, (CHUNKS, LANES))


def power_of_two(value, doublings):
    for _ in range(doublings):
        value = value * value
    return value


def shift_down(value, count):
    rolled = pltpu.roll(value, count, 0)
    place = lax.broadcasted_iota(jnp.int32, (CHUNKS, LANES), 0)
    return jnp.where(place >= count, rolled, 0.0)


def shift_up(value, count):
    rolled = pltpu.roll(value, CHUNKS - count, 0)
    place = lax.broadcasted_iota(jnp.int32, (CHUNKS, LANES), 0)
    return jnp.where(place < CHUNKS - count, rolled, 0.0)


def tile_rows(t):
    return pl.ds(pl.multiple_of(t * CHUNKS, CHUNKS), CHUNKS)


def forward_kernel(pos_ref, proj_ref, coef_ref, branch_ref, conv_ref, pads, u_ref, y_ref):
    coef = coef_ref[...]
    decay = [spread(coef[RATE_ROW + p : RATE_ROW + p + 1, :]) for p in range(POLES)]
    weight = [spread(coef[RES_ROW + p : RES_ROW + p + 1, :]) for p in range(POLES)]
    skip = coef[SKIP_ROW : SKIP_ROW + 1, :]
    y_ref[pl.ds(0, CHUNKS), :] = jnp.zeros((CHUNKS, LANES), f32)
    zero = y_ref[pl.ds(0, CHUNKS), :]
    for seq in range(2):
        for j in range(3):
            pads[j, pl.ds(0, PAD), :] = jnp.zeros((PAD, LANES), f32)
        for n in range(CHUNKS):
            rows = pl.ds(chunk_row(pos_ref, seq, n), CHUNK)
            for j in range(3):
                pads[j, pl.ds(PAD + n * CHUNK, CHUNK), :] = proj_ref[
                    rows, j * LANES : (j + 1) * LANES
                ]
        for n in range(CHUNKS):
            gated = mix_chunk(pads.at[1], coef, 1, n) * mix_chunk(pads.at[2], coef, 2, n)
            u_ref[pl.ds(n, CHUNK, stride=CHUNKS), :] = gated

        def ends(t, state):
            u = u_ref[tile_rows(t), :]
            return [a * h + u for a, h in zip(decay, state)]

        state = lax.fori_loop(0, CHUNK, ends, [zero] * POLES, unroll=2)
        start = []
        for a, h in zip(decay, state):
            jump = power_of_two(a, 7)
            for count in (1, 2, 4):
                h = h + jump * shift_down(h, count)
                jump = jump * jump
            start.append(shift_down(h, 1))

        def outputs(t, state):
            u = u_ref[tile_rows(t), :]
            state = [a * h + u for a, h in zip(decay, state)]
            terms = [w * h for w, h in zip(weight, state)]
            while len(terms) > 1:
                terms = [l + r for l, r in zip(terms[0::2], terms[1::2])]
            y_ref[tile_rows(t), :] = terms[0]
            return state

        lax.fori_loop(0, CHUNK, outputs, start, unroll=2)
        for n in range(CHUNKS):
            rows = pl.ds(chunk_row(pos_ref, seq, n), CHUNK)
            strided = pl.ds(n, CHUNK, stride=CHUNKS)
            conv = y_ref[strided, :] + skip * u_ref[strided, :]
            conv_ref[rows, :] = conv
            branch_ref[rows, :] = (mix_chunk(pads.at[0], coef, 0, n) * conv).astype(bf16)


def backward_kernel(
    pos_ref,
    proj_ref,
    conv_ref,
    grad_ref,
    coef_ref,
    out_ref,
    sums_ref,
    pads,
    mixed,
    grads,
    u_ref,
    g_ref,
    y_ref,
):
    coef = coef_ref[...]
    decay = [spread(coef[RATE_ROW + p : RATE_ROW + p + 1, :]) for p in range(POLES)]
    weight = [spread(coef[RES_ROW + p : RES_ROW + p + 1, :]) for p in range(POLES)]
    skip = coef[SKIP_ROW : SKIP_ROW + 1, :]
    y_ref[pl.ds(0, CHUNKS), :] = jnp.zeros((CHUNKS, LANES), f32)
    zero = y_ref[pl.ds(0, CHUNKS), :]
    row_zero = jnp.zeros((1, LANES), f32)
    tap_sums = [row_zero] * (3 * TAPS)
    skip_sum = row_zero
    res_sums = [zero] * POLES
    rate_sums = [zero] * POLES
    for seq in range(2):
        for j in range(3):
            pads[j, pl.ds(0, PAD), :] = jnp.zeros((PAD, LANES), f32)
            grads[j, pl.ds(LENGTH, PAD), :] = jnp.zeros((PAD, LANES), f32)
        for n in range(CHUNKS):
            rows = pl.ds(chunk_row(pos_ref, seq, n), CHUNK)
            for j in range(3):
                pads[j, pl.ds(PAD + n * CHUNK, CHUNK), :] = proj_ref[
                    rows, j * LANES : (j + 1) * LANES
                ]
        for n in range(CHUNKS):
            rows = pl.ds(chunk_row(pos_ref, seq, n), CHUNK)
            strided = pl.ds(n, CHUNK, stride=CHUNKS)
            plain = pl.ds(n * CHUNK, CHUNK)
            query = mix_chunk(pads.at[0], coef, 0, n)
            key = mix_chunk(pads.at[1], coef, 1, n)
            value = mix_chunk(pads.at[2], coef, 2, n)
            mixed[0, plain, :] = key
            mixed[1, plain, :] = value
            branch_grad = grad_ref[rows, :]
            grads[0, plain, :] = branch_grad * conv_ref[rows, :]
            u_ref[strided, :] = key * value
            g_ref[strided, :] = branch_grad * query

        def ends(step, state):
            g = g_ref[tile_rows(CHUNK - 1 - step), :]
            after = []
            for a, (b, e) in zip(decay, state):
                ab = a * b
                after.append((ab + g, a * e + ab))
            return after

        state = lax.fori_loop(0, CHUNK, ends, [(zero, zero)] * POLES, unroll=2)
        start = []
        for a, (b, e) in zip(decay, state):
            jump = power_of_two(a, 7)
            span = float(CHUNK)
            for count in (1, 2, 4):
                b_next, e_next = shift_up(b, count), shift_up(e, count)
                e = e + jump * (e_next + span * b_next)
                b = b + jump * b_next
                jump = jump * jump
                span = 2.0 * span
            start.append((shift_up(b, 1), shift_up(e, 1)))

        for first in range(0, POLES, MODE_GROUP):
            modes = range(first, first + MODE_GROUP)

            def outputs(step, state, modes=modes, first=first):
                t = CHUNK - 1 - step
                g = g_ref[tile_rows(t), :]
                u = u_ref[tile_rows(t), :]
                after, terms = [], []
                for p, (b, e, res, rate) in zip(modes, state):
                    ab = decay[p] * b
                    e = decay[p] * e + ab
                    b = ab + g
                    terms.append(weight[p] * b)
                    after.append((b, e, res + u * b, rate + u * e))
                while len(terms) > 1:
                    terms = [l + r for l, r in zip(terms[0::2], terms[1::2])]
                total = terms[0]
                if first > 0:
                    total = total + y_ref[tile_rows(t), :]
                y_ref[tile_rows(t), :] = total
                return after

            begin = [(*start[p], res_sums[p], rate_sums[p]) for p in modes]
            after = lax.fori_loop(0, CHUNK, outputs, begin, unroll=2)
            for p, (_, _, res, rate) in zip(modes, after):
                res_sums[p], rate_sums[p] = res, rate

        for n in range(CHUNKS):
            strided = pl.ds(n, CHUNK, stride=CHUNKS)
            plain = pl.ds(n * CHUNK, CHUNK)
            conv_grad = g_ref[strided, :]
            gated_grad = y_ref[strided, :] + skip * conv_grad
            skip_sum = skip_sum + jnp.sum(conv_grad * u_ref[strided, :], axis=0, keepdims=True)
            grads[1, plain, :] = gated_grad * mixed[1, plain, :]
            grads[2, plain, :] = gated_grad * mixed[0, plain, :]
        for n in range(CHUNKS):
            rows = pl.ds(chunk_row(pos_ref, seq, n), CHUNK)
            for j in range(3):
                here = grads[j, pl.ds(n * CHUNK, CHUNK), :]
                total = coef[j : j + 1, :] * here
                for i in range(TAPS):
                    behind = pads[j, pl.ds(PAD + n * CHUNK - i, CHUNK), :]
                    row = 3 * i + j
                    tap_sums[row] = tap_sums[row] + jnp.sum(here * behind, axis=0, keepdims=True)
                    if i > 0:
                        ahead = grads[j, pl.ds(n * CHUNK + i, CHUNK), :]
                        total = total + coef[row : row + 1, :] * ahead
                out_ref[rows, j * LANES : (j + 1) * LANES] = total.astype(bf16)
    for row in range(3 * TAPS):
        sums_ref[row : row + 1, :] = tap_sums[row]
    sums_ref[SKIP_ROW : SKIP_ROW + 1, :] = skip_sum
    for row in range(SKIP_ROW + 1, RES_ROW):
        sums_ref[row : row + 1, :] = row_zero
    for p in range(POLES):
        sums_ref[RES_ROW + p : RES_ROW + p + 1, :] = jnp.sum(res_sums[p], axis=0, keepdims=True)
        sums_ref[RATE_ROW + p : RATE_ROW + p + 1, :] = jnp.sum(
            rate_sums[p], axis=0, keepdims=True
        )


def mixer_forward(position, proj, coef):
    rows, channels = proj.shape[0], coef.shape[1]
    return pl.pallas_call(
        forward_kernel,
        grid=(channels // LANES,),
        in_specs=[
            pl.BlockSpec(memory_space=pltpu.SMEM),
            pl.BlockSpec((rows, 3 * LANES), lambda i: (0, i)),
            pl.BlockSpec((COEF_ROWS, LANES), lambda i: (0, i)),
        ],
        out_specs=[
            pl.BlockSpec((rows, LANES), lambda i: (0, i)),
            pl.BlockSpec((rows, LANES), lambda i: (0, i)),
        ],
        out_shape=[
            jax.ShapeDtypeStruct((rows, channels), bf16),
            jax.ShapeDtypeStruct((rows, channels), f32),
        ],
        scratch_shapes=[
            pltpu.VMEM((3, PAD + LENGTH, LANES), f32),
            pltpu.VMEM((LENGTH, LANES), f32),
            pltpu.VMEM((LENGTH, LANES), f32),
        ],
        compiler_params=pltpu.CompilerParams(vmem_limit_bytes=16 << 20),
        cost_estimate=pl.CostEstimate(
            flops=1 << 20, bytes_accessed=1 << 10, transcendentals=0
        ),
        name="mixer_forward",
    )(position, proj, coef)


def mixer_backward(position, proj, conv, grad, coef):
    rows, channels = proj.shape[0], coef.shape[1]
    return pl.pallas_call(
        backward_kernel,
        grid=(channels // LANES,),
        in_specs=[
            pl.BlockSpec(memory_space=pltpu.SMEM),
            pl.BlockSpec((rows, 3 * LANES), lambda i: (0, i)),
            pl.BlockSpec((rows, LANES), lambda i: (0, i)),
            pl.BlockSpec((rows, LANES), lambda i: (0, i)),
            pl.BlockSpec((COEF_ROWS, LANES), lambda i: (0, i)),
        ],
        out_specs=[
            pl.BlockSpec((rows, 3 * LANES), lambda i: (0, i)),
            pl.BlockSpec((COEF_ROWS, LANES), lambda i: (0, i)),
        ],
        out_shape=[
            jax.ShapeDtypeStruct((rows, 3 * channels), bf16),
            jax.ShapeDtypeStruct((COEF_ROWS, channels), f32),
        ],
        scratch_shapes=[
            pltpu.VMEM((3, PAD + LENGTH, LANES), f32),
            pltpu.VMEM((2, LENGTH, LANES), f32),
            pltpu.VMEM((3, LENGTH + PAD, LANES), f32),
            pltpu.VMEM((LENGTH, LANES), f32),
            pltpu.VMEM((LENGTH, LANES), f32),
            pltpu.VMEM((LENGTH, LANES), f32),
        ],
        compiler_params=pltpu.CompilerParams(vmem_limit_bytes=24 << 20),
        cost_estimate=pl.CostEstimate(
            flops=1 << 20, bytes_accessed=1 << 10, transcendentals=0
        ),
        name="mixer_backward",
    )(position, proj, conv, grad, coef)


TILE = 256
NO_COST = pl.CostEstimate(flops=1 << 10, bytes_accessed=1 << 10, transcendentals=0)
NT = (((1,), (1,)), ((), ()))
NN = (((1,), (0,)), ((), ()))


def whole_spec(array):
    return pl.BlockSpec(array.shape, lambda i: (0,) * array.ndim, pipeline_mode=pl.Buffered(1))


def up_kernel(scales, rows_ref, gate_w, up_w, inner_ref, scaled_ref, by_gate_ref, by_up_ref):
    piece = TILE // 2
    gate_all = lax.dot_general(rows_ref[...], gate_w[...], NT, preferred_element_type=f32)
    up_all = lax.dot_general(rows_ref[...], up_w[...], NT, preferred_element_type=f32)
    for part in range(2):
        at = slice(part * piece, (part + 1) * piece)
        index = lax.rem(2 * pl.program_id(0) + part, 8)
        other = jnp.where(lax.rem(index, 4) < 2, index // 4, lax.rem(index, 2))
        scale = jnp.where(other == 1, scales[1], scales[0])
        gate, up = gate_all[at], up_all[at]
        sigma = jax.nn.sigmoid(gate)
        silu = gate * sigma
        inner = silu * up
        inner_ref[at, :] = inner.astype(bf16)
        scaled_ref[at, :] = (inner * scale).astype(bf16)
        by_gate_ref[at, :] = (scale * up * sigma * (1.0 + gate * (1.0 - sigma))).astype(bf16)
        by_up_ref[at, :] = (scale * silu).astype(bf16)


def ffn_up(scales, rows, gate_w, up_w):
    count, hidden = rows.shape[0], gate_w.shape[0]
    tile = pl.BlockSpec((TILE, hidden), lambda i: (i, 0))
    return pl.pallas_call(
        up_kernel,
        grid=(count // TILE,),
        in_specs=[
            pl.BlockSpec(memory_space=pltpu.SMEM),
            pl.BlockSpec((TILE, rows.shape[1]), lambda i: (i, 0)),
            whole_spec(gate_w),
            whole_spec(up_w),
        ],
        out_specs=[tile] * 4,
        out_shape=[jax.ShapeDtypeStruct((count, hidden), bf16)] * 4,
        compiler_params=pltpu.CompilerParams(vmem_limit_bytes=20 << 20),
        cost_estimate=NO_COST,
        name="ffn_up",
    )(scales, rows, gate_w, up_w)


def rows_kernel(left, right, out):
    out[...] = lax.dot_general(left[...], right[...], NT, preferred_element_type=f32)


def rows_product(left, right):
    count, width = left.shape
    return pl.pallas_call(
        rows_kernel,
        grid=(count // TILE,),
        in_specs=[pl.BlockSpec((TILE, width), lambda i: (i, 0)), whole_spec(right)],
        out_specs=pl.BlockSpec((TILE, right.shape[0]), lambda i: (i, 0)),
        out_shape=jax.ShapeDtypeStruct((count, right.shape[0]), f32),
        compiler_params=pltpu.CompilerParams(vmem_limit_bytes=13 << 20),
        cost_estimate=NO_COST,
        name="rows_product",
    )(left, right)


def grad_kernel(rows_ref, down_w, by_gate_ref, by_up_ref, gate_ref, up_ref):
    grad = lax.dot_general(rows_ref[...], down_w[...], NT, preferred_element_type=f32)
    gate_ref[...] = (grad * by_gate_ref[...].astype(f32)).astype(bf16)
    up_ref[...] = (grad * by_up_ref[...].astype(f32)).astype(bf16)


def ffn_grad(rows, down_w, by_gate, by_up):
    count, hidden = rows.shape[0], down_w.shape[0]
    tile = pl.BlockSpec((TILE, hidden), lambda i: (i, 0))
    return pl.pallas_call(
        grad_kernel,
        grid=(count // TILE,),
        in_specs=[
            pl.BlockSpec((TILE, rows.shape[1]), lambda i: (i, 0)),
            whole_spec(down_w),
            tile,
            tile,
        ],
        out_specs=[tile] * 2,
        out_shape=[jax.ShapeDtypeStruct((count, hidden), bf16)] * 2,
        compiler_params=pltpu.CompilerParams(vmem_limit_bytes=14 << 20),
        cost_estimate=NO_COST,
        name="ffn_grad",
    )(rows, down_w, by_gate, by_up)


def product_kernel(count, adds, tiles, *refs):
    lefts, rights = refs[:count], refs[count : 2 * count]
    outs = refs[-tiles:]
    total = None
    for left, right in zip(lefts, rights):
        term = lax.dot_general(left[...], right[...], NN, preferred_element_type=f32)
        total = term if total is None else total + term
    for tile in range(tiles):

        @pl.when(pl.program_id(0) == tile)
        def _(tile=tile):
            if adds:
                outs[tile][...] = (total + refs[2 * count + tile][...].astype(f32)).astype(bf16)
            else:
                outs[tile][...] = total.astype(bf16)


def product_tiles(lefts, rights, first, tiles, adds=()):
    width = rights[0].shape[1]
    start = first // TILE
    tile_spec = pl.BlockSpec((TILE, width), lambda i: (0, 0))
    return pl.pallas_call(
        functools.partial(product_kernel, len(lefts), len(adds), tiles),
        grid=(tiles,),
        in_specs=[
            pl.BlockSpec((TILE, left.shape[1]), lambda i: (start + i, 0)) for left in lefts
        ]
        + [whole_spec(right) for right in rights]
        + [whole_spec(add) for add in adds],
        out_specs=[tile_spec] * tiles,
        out_shape=[jax.ShapeDtypeStruct((TILE, width), bf16)] * tiles,
        compiler_params=pltpu.CompilerParams(vmem_limit_bytes=22 << 20),
        cost_estimate=NO_COST,
        name="product",
    )(*lefts, *rights, *adds)


def halves_spec(rows, depth):
    return [jax.ShapeDtypeStruct((rows, depth), bf16)] * 2


def mixer_weights_kernel(where_ref, in_ref, out_ref, in_mine, in_other, out_mine, out_other):
    units = in_ref.shape[2] // 2
    tiles = units // LANES
    for side, target in ((where_ref[3], in_mine), (1 - where_ref[3], in_other)):
        for tile in range(tiles):
            start = pl.multiple_of(side * units + tile * LANES, LANES)
            for j in range(3):
                row = (tile * 3 + j) * LANES
                block = in_ref[j, :, pl.ds(start, LANES)]
                target[row : row + LANES, :] = block.T.astype(bf16)
    for side, target in ((where_ref[3], out_mine), (1 - where_ref[3], out_other)):
        rows = pl.ds(pl.multiple_of(side * units, units), units)
        target[...] = out_ref[rows, :].astype(bf16)


def mixer_weights(where, in_weight, out_weight):
    _, depth, channels = in_weight.shape
    units = channels // 2
    return pl.pallas_call(
        mixer_weights_kernel,
        in_specs=[pl.BlockSpec(memory_space=pltpu.SMEM)]
        + [pl.BlockSpec(memory_space=pltpu.VMEM)] * 2,
        out_specs=[pl.BlockSpec(memory_space=pltpu.VMEM)] * 4,
        out_shape=halves_spec(3 * units, depth) + halves_spec(units, depth),
        compiler_params=pltpu.CompilerParams(vmem_limit_bytes=12 << 20),
        cost_estimate=NO_COST,
        name="mixer_weights",
    )(where, in_weight, out_weight)


def ffn_weights_kernel(
    where_ref, gate_ref, up_ref, down_ref, mine, other, down_mine, down_other, turned
):
    units = down_ref.shape[0] // 2
    mine_rows = pl.ds(pl.multiple_of(where_ref[3] * units, units), units)
    other_rows = pl.ds(pl.multiple_of((1 - where_ref[3]) * units, units), units)
    for n, source in enumerate((gate_ref, up_ref)):
        turned[...] = source[...].T
        mine[n * units : (n + 1) * units, :] = turned[mine_rows, :].astype(bf16)
        other[n * units : (n + 1) * units, :] = turned[other_rows, :].astype(bf16)
    down_mine[...] = down_ref[mine_rows, :].astype(bf16)
    down_other[...] = down_ref[other_rows, :].astype(bf16)


def ffn_weights(where, gate_weight, up_weight, down_weight):
    units, depth = down_weight.shape
    return pl.pallas_call(
        ffn_weights_kernel,
        in_specs=[pl.BlockSpec(memory_space=pltpu.SMEM)]
        + [pl.BlockSpec(memory_space=pltpu.VMEM)] * 3,
        out_specs=[pl.BlockSpec(memory_space=pltpu.VMEM)] * 4,
        out_shape=halves_spec(units, depth) + halves_spec(units // 2, depth),
        scratch_shapes=[pltpu.VMEM((units, depth), f32)],
        compiler_params=pltpu.CompilerParams(vmem_limit_bytes=20 << 20),
        cost_estimate=NO_COST,
        name="ffn_weights",
    )(where, gate_weight, up_weight, down_weight)


def branch_grads_kernel(out_w, rows_ref, branch_ref, grad_ref, blocks_ref, total):
    step = pl.program_id(0)
    rows = rows_ref[...]
    grad_ref[...] = lax.dot_general(rows, out_w[...], NT, preferred_element_type=f32)
    term = lax.dot_general(
        branch_ref[...], rows, (((0,), (0,)), ((), ())), preferred_element_type=f32
    )

    @pl.when(step == 0)
    def _():
        total[...] = term

    @pl.when(step > 0)
    def _():
        total[...] += term

    @pl.when(step == pl.num_programs(0) - 1)
    def _():
        groups, _, width = blocks_ref.shape
        for i in range(groups):
            blocks_ref[i] = total[:, i * width : (i + 1) * width].astype(bf16)


def branch_grads(rows, out_w, branch, groups):
    count, model = rows.shape
    channels = out_w.shape[0]
    return pl.pallas_call(
        branch_grads_kernel,
        grid=(count // TILE,),
        in_specs=[
            whole_spec(out_w),
            pl.BlockSpec((TILE, model), lambda i: (i, 0)),
            pl.BlockSpec((TILE, channels), lambda i: (i, 0)),
        ],
        out_specs=[
            pl.BlockSpec((TILE, channels), lambda i: (i, 0)),
            pl.BlockSpec((groups, channels, model // groups), lambda i: (0, 0, 0)),
        ],
        out_shape=[
            jax.ShapeDtypeStruct((count, channels), f32),
            jax.ShapeDtypeStruct((groups, channels, model // groups), bf16),
        ],
        scratch_shapes=[pltpu.VMEM((channels, model), f32)],
        compiler_params=pltpu.CompilerParams(vmem_limit_bytes=12 << 20),
        cost_estimate=NO_COST,
        name="branch_grads",
    )(out_w, rows, branch)


def weight_grad_kernel(left, right, out):
    out[...] = lax.dot_general(
        left[...], right[...], (((0,), (0,)), ((), ())), preferred_element_type=f32
    ).astype(bf16)


def weight_product(left, right, blocks=0):
    depth, units = left.shape
    width = right.shape[1]
    if blocks:
        tile = width // blocks
        out_spec = pl.BlockSpec((None, units, tile), lambda i: (i, 0, 0))
        shape = (blocks, units, tile)
    else:
        tile = min(width, 512)
        out_spec = pl.BlockSpec((units, tile), lambda i: (0, i))
        shape = (units, width)
    return pl.pallas_call(
        weight_grad_kernel,
        grid=(width // tile,),
        in_specs=[whole_spec(left), pl.BlockSpec((depth, tile), lambda i: (0, i))],
        out_specs=out_spec,
        out_shape=jax.ShapeDtypeStruct(shape, bf16),
        compiler_params=pltpu.CompilerParams(vmem_limit_bytes=16 << 20),
        cost_estimate=NO_COST,
        name="weight_product",
    )(left, right)


def finish_kernel(where_ref, total, mine, other, square):
    width = mine.shape[1]
    for side, target in ((where_ref[3], mine), (1 - where_ref[3], other)):
        target[...] = total[:, pl.ds(pl.multiple_of(side * width, LANES), width)]
    values = total[...].astype(f32)
    square[...] = jnp.sum(values * values, axis=0, keepdims=True)


def finish_units(where, total, x):
    units, width = total.shape
    width = width // 2
    if width % LANES != 0:
        mine = lax.dynamic_slice_in_dim(total, x * width, width, 1)
        other = lax.dynamic_slice_in_dim(total, (1 - x) * width, width, 1)
        values = total.astype(f32)
        return mine, other, jnp.sum(values * values, axis=0, keepdims=True)
    return pl.pallas_call(
        finish_kernel,
        in_specs=[
            pl.BlockSpec(memory_space=pltpu.SMEM),
            pl.BlockSpec(memory_space=pltpu.VMEM),
        ],
        out_specs=[pl.BlockSpec(memory_space=pltpu.VMEM)] * 3,
        out_shape=halves_spec(units, width) + [jax.ShapeDtypeStruct((1, 2 * width), f32)],
        compiler_params=pltpu.CompilerParams(vmem_limit_bytes=8 << 20),
        cost_estimate=NO_COST,
        name="finish_units",
    )(where, total)


def rows_shard_kernel(where_ref, mine, other, out):
    units = mine.shape[0]
    for side, source in ((where_ref[3], mine), (1 - where_ref[3], other)):
        rows = pl.ds(pl.multiple_of(side * units, units), units)
        out[rows, :] = source[...].astype(f32)


def turned_shard_kernel(where_ref, mine, other, out, rows):
    rows_shard_kernel(where_ref, mine, other, rows)
    out[...] = rows[...].T


def in_shard_kernel(where_ref, mine, other, out):
    units = mine.shape[0] // 3
    for side, source in ((where_ref[3], mine), (1 - where_ref[3], other)):
        for tile in range(units // LANES):
            start = pl.multiple_of(side * units + tile * LANES, LANES)
            for j in range(3):
                row = (tile * 3 + j) * LANES
                block = source[row : row + LANES, :].astype(f32)
                out[j, :, pl.ds(start, LANES)] = block.T


def shard_of(kernel, where, mine, other, shape, scratch=()):
    return pl.pallas_call(
        kernel,
        in_specs=[pl.BlockSpec(memory_space=pltpu.SMEM)]
        + [pl.BlockSpec(memory_space=pltpu.VMEM)] * 2,
        out_specs=pl.BlockSpec(memory_space=pltpu.VMEM),
        out_shape=jax.ShapeDtypeStruct(shape, f32),
        scratch_shapes=list(scratch),
        compiler_params=pltpu.CompilerParams(vmem_limit_bytes=12 << 20),
        cost_estimate=NO_COST,
        name="shard",
    )(where, mine, other)


def rows_by_rows(left, right):
    return lax.dot_general(left, right, (((1,), (1,)), ((), ())), preferred_element_type=f32)


def columns_by_columns(left, right):
    return lax.dot_general(left, right, (((0,), (0,)), ((), ())), preferred_element_type=f32)


def plain_dot(left, right):
    return jnp.dot(left, right, preferred_element_type=f32)


def low(values):
    return values.astype(bf16)


def add_low(left, right):
    return (left.astype(f32) + right.astype(f32)).astype(bf16)


def norm_back(values, scale, gain, grad):
    weighted = grad * gain
    inner_mean = jnp.mean(values * weighted, axis=1, keepdims=True)
    return (
        scale * weighted - values * (scale * scale * scale) * inner_mean,
        jnp.sum(grad * values * scale, axis=0),
    )


def adam(weight, first, second, grad, rate, decay):
    first_new = BETA_ONE * first + (1.0 - BETA_ONE) * grad
    second_new = BETA_TWO * second + (1.0 - BETA_TWO) * grad * grad
    stride = (
        first_new
        / (1.0 - BETA_ONE**STEP)
        / (jnp.sqrt(second_new / (1.0 - BETA_TWO**STEP)) + ADAM_EPSILON)
    )
    return (weight - rate * (stride + decay * weight), first_new, second_new)


class Links:
    def __init__(self, groups):
        self.groups = groups
        places = [(z, x) for z in range(groups) for x in (0, 1)]
        self.ring = [(2 * z + x, 2 * ((z + 1) % groups) + x) for z, x in places]
        self.lines = [[2 * z + x for z in range(groups)] for x in (0, 1)]
        self.over_x = [(2 * z + x, 2 * z + 1 - x) for z, x in places]
        self.over_y = [(2 * y + c, 2 * (1 - y) + c) for y in (0, 1) for c in (0, 1)]
        self.over_c = [(2 * y + c, 2 * y + 1 - c) for y in (0, 1) for c in (0, 1)]
        self.bits = [1 << n for n in range(groups.bit_length() - 1)]
        self.across = {
            bit: [(2 * z + x, 2 * (z ^ bit) + x) for z, x in places] for bit in self.bits
        }

    def z(self, v):
        return lax.ppermute(v, "dp", self.ring)

    def z_across(self, v, bit):
        return lax.ppermute(v, "dp", self.across[bit])

    def x(self, v):
        return lax.ppermute(v, "dp", self.over_x)

    def y(self, v):
        return lax.ppermute(v, "mp", self.over_y)

    def c(self, v):
        return lax.ppermute(v, "mp", self.over_c)


def tie(value, *before):
    return lax.optimization_barrier((value, *before))[0] if before else value


class Chain:
    def __init__(self):
        self.held = ()

    def __call__(self, value, *before):
        return tie(value, *self.held, *before)

    def mark(self, *done):
        self.held = done

    def wait(self, *arrived):
        together = lax.optimization_barrier((*arrived, *self.held))[: len(arrived)]
        self.held = together[:1]
        return together[0] if len(arrived) == 1 else together


def copy_kernel(count, place, *refs):
    where, pieces, whole, sems = refs[0], refs[1 : count + 1], refs[count + 1], refs[count + 2]
    copies = [
        pltpu.make_async_copy(piece, whole.at[place(where, i)], sems.at[i])
        for i, piece in enumerate(pieces)
    ]
    for copy in copies:
        copy.start()
    for copy in copies:
        copy.wait()


def assemble_columns(first, pieces, place, where, shape):
    arrays, offsets = [first], [pieces[0][1]]
    index = []
    for i, (array, offset) in enumerate(pieces):
        known = [n for n, other in enumerate(arrays) if other is array]
        if i == 0:
            index.append((0, offset))
        elif array is pieces[0][0]:
            index.append((0, offset))
        elif known:
            index.append((known[0], offset))
        else:
            arrays.append(array)
            index.append((len(arrays) - 1, offset))
    count = len(arrays)
    units = shape[0]

    def kernel(*refs):
        where_ref, sources, whole, sems = refs[0], refs[1 : count + 1], refs[count + 1], refs[-1]
        copies = [
            pltpu.make_async_copy(
                sources[n].at[pl.ds(offset, units), :],
                whole.at[place(where_ref, i)],
                sems.at[i],
            )
            for i, (n, offset) in enumerate(index)
        ]
        for copy in copies:
            copy.start()
        for copy in copies:
            copy.wait()

    return pl.pallas_call(
        kernel,
        in_specs=[pl.BlockSpec(memory_space=pltpu.SMEM)]
        + [pl.BlockSpec(memory_space=pl.ANY)] * count,
        out_specs=pl.BlockSpec(memory_space=pltpu.VMEM),
        out_shape=jax.ShapeDtypeStruct(shape, bf16),
        scratch_shapes=[pltpu.SemaphoreType.DMA((len(pieces),))],
        compiler_params=pltpu.CompilerParams(vmem_limit_bytes=8 << 20),
        cost_estimate=pl.CostEstimate(
            flops=0, bytes_accessed=4 * units * shape[1], transcendentals=0
        ),
        name="assemble_columns",
    )(where, *arrays)


def assemble_blocks(blocks, where):
    groups, rows, width = blocks.shape

    def kernel(where_ref, source, whole, sems):
        copies = [
            pltpu.make_async_copy(
                source.at[i], whole.at[:, pl.ds(i * width, width)], sems.at[i]
            )
            for i in range(groups)
        ]
        for copy in copies:
            copy.start()
        for copy in copies:
            copy.wait()

    return pl.pallas_call(
        kernel,
        in_specs=[pl.BlockSpec(memory_space=pltpu.SMEM), pl.BlockSpec(memory_space=pl.ANY)],
        out_specs=pl.BlockSpec(memory_space=pltpu.VMEM),
        out_shape=jax.ShapeDtypeStruct((rows, groups * width), bf16),
        scratch_shapes=[pltpu.SemaphoreType.DMA((groups,))],
        compiler_params=pltpu.CompilerParams(vmem_limit_bytes=10 << 20),
        cost_estimate=NO_COST,
        name="assemble_blocks",
    )(where, blocks)


def assemble_rows(pieces, where, shape):
    arrays = []
    for array, *_ in pieces:
        if not any(array is other for other in arrays):
            arrays.append(array)
    index = [next(n for n, other in enumerate(arrays) if other is p[0]) for p in pieces]
    count = len(arrays)

    def kernel(*refs):
        sources, whole, sems = refs[1 : count + 1], refs[-2], refs[-1]
        copies = []
        for i, (n, (_, start, rows, target)) in enumerate(zip(index, pieces)):
            source = sources[n].at[pl.ds(start, rows), :]
            copies.append(
                pltpu.make_async_copy(source, whole.at[pl.ds(target, rows), :], sems.at[i])
            )
        for copy in copies:
            copy.start()
        for copy in copies:
            copy.wait()

    return pl.pallas_call(
        kernel,
        in_specs=[pl.BlockSpec(memory_space=pltpu.SMEM)]
        + [pl.BlockSpec(memory_space=pl.ANY)] * count,
        out_specs=pl.BlockSpec(memory_space=pltpu.VMEM),
        out_shape=jax.ShapeDtypeStruct(shape, bf16),
        scratch_shapes=[pltpu.SemaphoreType.DMA((len(pieces),))],
        compiler_params=pltpu.CompilerParams(vmem_limit_bytes=10 << 20),
        cost_estimate=NO_COST,
        name="assemble_rows",
    )(where, *arrays)


class GatherRows:
    def __init__(self, net, chain, block):
        self.net, self.chain = net, chain
        half = block.shape[0] // 2
        self.a, self.b = block[:half], block[half:]
        self.a_x, self.b_y = net.x(self.a), net.y(self.b)

    def second(self, *more):
        net, chain = self.net, self.chain
        got = chain.wait(self.a_x, self.b_y, *more)
        a_x, b_y = got[:2]
        self.a = jnp.concatenate([self.a, a_x], axis=0)
        self.b = jnp.concatenate([self.b, b_y], axis=0)
        chain.mark(self.a, self.b)
        self.a_y, self.b_x = net.y(self.a), net.x(self.b)
        self.far_a, self.far_b = net.c(self.a), net.c(self.b)
        return got[2:]

    def third(self, *more):
        got = self.chain.wait(self.a_y, self.b_x, *more)
        self.a_y, self.b_x = got[:2]
        return got[2:]

    def trade(self):
        a_y, b_x = (tie(piece, *self.chain.held) for piece in (self.a_y, self.b_x))
        self.far_a_y, self.far_b_x = self.net.c(a_y), self.net.c(b_x)

    def whole(self, where):
        chain = self.chain
        far_a, far_b, far_a_y, far_b_x = chain.wait(
            self.far_a, self.far_b, self.far_a_y, self.far_b_x
        )
        rows = self.a.shape[0] // 2
        near = (self.a, self.a_y, self.b, self.b_x)
        far = (far_a, far_a_y, far_b, far_b_x)
        pieces = []
        for core, arrays in enumerate((near, far)):
            for place, array in enumerate(arrays):
                first = (8 * core + place) * rows
                pieces += [(array, 0, rows, first), (array, rows, rows, first + 4 * rows)]
        whole = assemble_rows(pieces, where, (16 * rows, self.a.shape[1]))
        chain.mark(whole)
        return whole


class ScatterProduct:
    def __init__(self, net, chain, lefts, rights):
        self.net, self.chain = net, chain
        self.lefts, self.rights = lefts, rights
        self.far = self.tiles(4, 4)

    def tiles(self, first, count, adds=()):
        lefts = [self.chain(self.lefts[0]), *self.lefts[1:]]
        tiles = product_tiles(lefts, self.rights, first * TILE, count, adds)
        self.chain.mark(tiles[0])
        return tiles

    def trade(self):
        held = [tie(tile, *self.chain.held) for tile in self.far]
        self.far = [self.net.c(tile) for tile in held]

    def arrived(self):
        self.far = self.chain.wait(*self.far)

    def near(self):
        self.a, self.b, self.for_x, self.for_y = self.tiles(0, 4, self.far)

    def send(self):
        net = self.net
        for_x, for_y = (tie(tile, *self.chain.held) for tile in (self.for_x, self.for_y))
        self.from_x, self.from_y = net.x(for_x), net.y(for_y)

    def second(self, *more):
        net, chain, piece = self.net, self.chain, TILE // 2
        got = chain.wait(self.from_x, self.from_y, *more)
        self.from_x, self.from_y = got[:2]
        a_y = add_low(self.a[piece:], self.from_x[piece:])
        b_x = add_low(self.b[piece:], self.from_y[piece:])
        self.a_y, self.b_x = net.y(a_y), net.x(b_x)
        chain.mark(a_y, b_x)
        return got[2:]

    def last(self, *more):
        got = self.chain.wait(self.a_y, self.b_x, *more)
        self.a_y, self.b_x = got[:2]
        return (self.sum(), *got[2:])

    def sum(self):
        piece = TILE // 2
        a_y, b_x = self.a_y, self.b_x
        a = self.a[:piece].astype(f32) + self.from_x[:piece].astype(f32) + a_y.astype(f32)
        b = self.b[:piece].astype(f32) + self.from_y[:piece].astype(f32) + b_x.astype(f32)
        return jnp.concatenate([a, b], axis=0)


def pick(pair, index):
    return lax.dynamic_index_in_dim(pair, index, 0, keepdims=False)


def in_order(mine, other, x, axis):
    return jnp.where(
        x == 0,
        jnp.concatenate([mine, other], axis=axis),
        jnp.concatenate([other, mine], axis=axis),
    )


class GatherUnits:
    def __init__(self, net, chain, mine, other, x, z):
        self.net, self.chain, self.x, self.z = net, chain, x, z
        self.first, self.out = mine, other

    def trade(self, *after):
        self.got = self.net.x(tie(self.out, *after))

    def traded(self, merge, got=None):
        got = self.chain.wait(self.got) if got is None else got
        if merge:
            pair = self.chain(jnp.concatenate([self.first, got], axis=0))
            self.chain.mark(pair)
            self.rings = [[pair]]
        else:
            self.rings = [[self.first], [got]]

    def send(self, ring=0, *after):
        hops = self.rings[ring]
        hops.append(self.net.z(tie(hops[-1], *after)))

    def gather(self, first, last):
        pair = self.rings[0][0]
        units = pair.shape[0] // 2
        mine, other = pair[first:last], pair[units + first : units + last]
        piece = self.chain(in_order(mine, other, self.x, 1))
        self.chain.mark(piece)
        return lax.all_gather(piece, "dp", axis_index_groups=self.net.lines)

    def coming(self, ring=0):
        return self.rings[ring][-1]

    def came(self, piece, ring=0):
        self.rings[ring][-1] = piece

    def arrived(self, ring=0):
        self.came(self.chain.wait(self.coming(ring)), ring)

    def whole(self, where, ranges):
        groups, chain = self.net.groups, self.chain
        for ring in range(len(self.rings)):
            while len(self.rings[ring]) < groups:
                self.send(ring)
                self.arrived(ring)
        units, width = self.first.shape
        merged = len(self.rings) == 1
        wholes = []
        for first, last in ranges:
            pieces = []
            for step in range(groups):
                for side in range(2):
                    piece = self.rings[0 if merged else side][step]
                    offset = side * units if merged else 0
                    pieces.append((piece, offset + first))
            if width % LANES == 0:

                def place(where_ref, i):
                    block = lax.rem(where_ref[2] + (groups - i // 2), groups) * 2
                    side = where_ref[3] if i % 2 == 0 else 1 - where_ref[3]
                    start = pl.multiple_of((block + side) * width, LANES)
                    return (slice(None), pl.ds(start, width))

                shape = (last - first, 2 * width * groups)
                whole = assemble_columns(
                    chain(pieces[0][0]), pieces, place, where, shape
                )
            else:
                whole = jnp.zeros((last - first, 2 * width * groups), bf16)
                for i, (piece, offset) in enumerate(pieces):
                    block = 2 * lax.rem(self.z + groups - i // 2, groups)
                    side = self.x if i % 2 == 0 else 1 - self.x
                    part = piece[offset : offset + last - first]
                    whole = lax.dynamic_update_slice(whole, part, (0, (block + side) * width))
            chain.mark(whole)
            wholes.append(whole)
        return wholes


class ReducedUnits:
    def __init__(self, net, chain, blocks, x):
        self.net, self.chain, self.x = net, chain, x
        self.total = lax.psum_scatter(blocks, "dp", axis_index_groups=net.lines)

    def finish(self, where, total=None):
        total = self.chain.wait(self.total) if total is None else total
        self.mine, self.other, self.square = finish_units(where, total, self.x)
        self.chain.mark(self.mine, self.other, self.square)

    def trade(self):
        self.traded = self.net.x(tie(self.other, *self.chain.held))

    def shard(self, kernel, where, shape, scratch=()):
        got = self.chain(self.traded)
        shard = shard_of(kernel, where, self.mine, got, shape, scratch)
        self.chain.mark(shard)
        return shard


def on_device(
    net,
    tokens,
    cotangent,
    group_ids,
    group_scales,
    gains,
    gains_first,
    gains_second,
    taps,
    taps_first,
    taps_second,
    residues,
    residues_first,
    residues_second,
    log_rates,
    log_rates_first,
    log_rates_second,
    skip,
    skip_first,
    skip_second,
    in_weight,
    in_weight_first,
    in_weight_second,
    out_weight,
    out_weight_first,
    out_weight_second,
    gate_weight,
    gate_weight_first,
    gate_weight_second,
    up_weight,
    up_weight_first,
    up_weight_second,
    down_weight,
    down_weight_first,
    down_weight_second,
):
    model = tokens.shape[1]
    depth = in_weight.shape[0]
    channels = in_weight.shape[2] // 2
    hidden = gate_weight.shape[1] // 2
    tiles = channels // LANES
    dp, mp = lax.axis_index("dp"), lax.axis_index("mp")
    z, x, y, c = dp // 2, dp % 2, mp // 2, mp % 2
    begin = (mp * 2 + x) * channels
    position = jnp.stack([y, c, z, x]).astype(jnp.int32)

    def own(array):
        return lax.dynamic_slice_in_dim(array, begin, channels, array.ndim - 1)

    chain = Chain()
    resid = tokens.astype(f32)
    scale_one = lax.rsqrt(jnp.mean(resid * resid, axis=1, keepdims=True) + EPSILON)
    normed = low(resid * scale_one * gains[0])
    chain.mark(normed)
    in_mine, in_other, out_mine, out_other = mixer_weights(
        position, chain(in_weight.transpose(1, 0, 2)), out_weight
    )
    chain.mark(in_mine)
    ring_in = GatherUnits(net, chain, in_mine, in_other, x, z)
    ring_in.trade()
    ring_in.rings = [[ring_in.first]]
    ring_in.send()
    ring_out = GatherUnits(net, chain, out_mine, out_other, x, z)
    sequence_scale = jnp.sum(
        jnp.where(
            group_ids[:, None] == jnp.arange(group_scales.shape[0], dtype=jnp.int32)[None, :],
            group_scales[None, :],
            0.0,
        )
    )

    first, got = chain.wait(ring_in.coming(0), ring_in.got)
    ring_in.came(first, 0)
    ring_in.rings.append([got])
    ring_in.send(0)
    ring_in.send(1)
    normed_rows = GatherRows(net, chain, chain(normed))
    gate_mine, gate_other, down_mine, down_other = ffn_weights(
        position, chain(gate_weight), up_weight, down_weight
    )
    chain.mark(gate_mine)
    ring_gu = GatherUnits(net, chain, gate_mine, gate_other, x, z)
    ring_down = GatherUnits(net, chain, down_mine, down_other, x, z)
    ring_out.trade()
    other_scale = net.x(chain(sequence_scale).reshape(1, 1))
    got, other_scale, first, second = normed_rows.second(
        ring_out.got, other_scale, ring_in.coming(0), ring_in.coming(1)
    )
    ring_in.came(first, 0)
    ring_in.came(second, 1)
    ring_in.send(0)
    ring_in.send(1)
    ring_out.traded(True, got)
    ring_out.send()
    residues_own = own(residues)
    rates_own = jnp.exp(own(log_rates))
    coef = jnp.concatenate(
        [
            own(taps).reshape(3 * TAPS, channels),
            own(skip)[None],
            jnp.zeros((RES_ROW - SKIP_ROW - 1, channels), f32),
            residues_own,
            jnp.exp(-rates_own),
        ],
        axis=0,
    )
    coef = chain(coef)
    chain.mark(coef)
    first, got, piece = normed_rows.third(
        ring_in.coming(0), ring_in.coming(1), ring_out.coming()
    )
    ring_in.came(first, 0)
    ring_in.came(got, 1)
    ring_out.came(piece)
    ring_in.send(1)
    ring_out.send()
    ring_gu.trade(*chain.held)
    normed_rows.trade()
    normed_all = normed_rows.whole(position)
    got, piece, traded = chain.wait(ring_in.coming(1), ring_out.coming(), ring_gu.got)
    ring_in.came(got, 1)
    ring_out.came(piece)
    ring_out.send()
    ring_gu.traded(True, traded)
    gate_blocks = ring_gu.gather(0, hidden)
    up_blocks = ring_gu.gather(hidden, 2 * hidden)
    cotangent = chain(cotangent)
    back_rows = GatherRows(net, chain, cotangent)
    (w_in,) = ring_in.whole(position, [(0, 3 * channels)])

    proj = rows_product(chain(normed_all), w_in)
    chain.mark(proj)
    back_rows.second()
    branch, conv = mixer_forward(position, chain(proj), coef)
    chain.mark(branch)
    (piece,) = back_rows.third(ring_out.coming())
    ring_out.came(piece)
    (w_out,) = ring_out.whole(position, [(0, channels)])
    product = ScatterProduct(net, chain, [branch], [w_out])
    product.trade()
    product.arrived()
    product.near()
    product.send()
    back_rows.trade()
    back_all = back_rows.whole(position)
    (gate_blocks,) = product.second(gate_blocks)
    ring_down.trade(*chain.held)
    w_gate = assemble_blocks(chain(gate_blocks), position)
    chain.mark(w_gate)
    (more,) = product.last()
    middle = resid + more
    scale_two = lax.rsqrt(jnp.mean(middle * middle, axis=1, keepdims=True) + EPSILON)
    normed_two = low(middle * scale_two * gains[1])
    chain.mark(normed_two)
    normed_two_rows = GatherRows(net, chain, normed_two)
    normed_two_rows.second()
    got, up_blocks = chain.wait(ring_down.got, up_blocks)
    ring_down.traded(True, got)
    down_blocks = ring_down.gather(0, hidden)
    w_up = assemble_blocks(chain(up_blocks), position)
    chain.mark(w_up)
    scales = chain(jnp.concatenate([sequence_scale.reshape(1), other_scale.reshape(1)]))
    chain.mark(scales)
    normed_two_rows.third()
    normed_two_rows.trade()
    normed_two_all = normed_two_rows.whole(position)
    inner_low, inner_scaled, by_gate, by_up = ffn_up(
        scales, chain(normed_two_all), w_gate, w_up
    )
    chain.mark(inner_scaled, inner_low)

    def blocks_of(left, right):
        grad = weight_product(chain(left), right, net.groups)
        chain.mark(grad)
        return grad

    def reduced(grad):
        return ReducedUnits(net, chain, chain(grad), x)

    sum_down = reduced(blocks_of(inner_scaled, back_all))
    w_down = assemble_blocks(chain.wait(down_blocks), position)
    chain.mark(w_down)
    grad_gate, grad_up = ffn_grad(chain(back_all), w_down, by_gate, by_up)
    chain.mark(grad_gate, grad_up)
    product = ScatterProduct(net, chain, [grad_gate, grad_up], [w_gate, w_up])
    product.trade()
    product.arrived()
    product.near()
    product.send()
    grad_gate = blocks_of(grad_gate, normed_two_all)
    grad_up = blocks_of(grad_up, normed_two_all)
    product.second()
    sum_gate, sum_up = reduced(grad_gate), reduced(grad_up)
    output_product = ScatterProduct(net, chain, [inner_low], [w_down])
    output_product.trade()
    (grad_normed_two,) = product.last()
    grad_from_norm, gain_two = norm_back(middle, scale_two, gains[1], grad_normed_two)
    grad_middle = cotangent.astype(f32) * sequence_scale + grad_from_norm
    grad_middle_low = low(grad_middle)
    chain.mark(grad_middle_low)
    grad_middle_rows = GatherRows(net, chain, grad_middle_low)
    output_product.arrived()
    output_product.near()
    (got,) = grad_middle_rows.second(sum_down.total)
    sum_down.finish(position, got)
    (got,) = grad_middle_rows.third(sum_gate.total)
    grad_middle_rows.trade()
    output_product.send()
    sum_gate.finish(position, got)
    sum_down.trade()
    sum_gate.trade()
    grad_middle_all = grad_middle_rows.whole(position)
    grad_branch, grad_out = branch_grads(chain(grad_middle_all), w_out, branch, net.groups)
    chain.mark(grad_branch)
    sum_out = reduced(grad_out)
    grad_proj, sums = mixer_backward(position, proj, conv, chain(grad_branch), coef)
    chain.mark(grad_proj)
    product = ScatterProduct(net, chain, [grad_proj], [w_in])
    output_product.from_x, output_product.from_y, sum_down.traded, sum_gate.traded = chain.wait(
        output_product.from_x, output_product.from_y, sum_down.traded, sum_gate.traded
    )
    product.trade()
    grad_in = blocks_of(grad_proj, normed_all)
    product.arrived()
    sum_in = reduced(grad_in)
    product.near()
    product.send()
    sum_up.finish(position)
    turned = [pltpu.VMEM((2 * hidden, depth), f32)]
    shard_down = sum_down.shard(rows_shard_kernel, position, (2 * hidden, depth))
    shard_gate = sum_gate.shard(turned_shard_kernel, position, (depth, 2 * hidden), turned)

    sums = chain(sums)
    sums = jnp.concatenate(
        [sums[:RATE_ROW], -rates_own * residues_own * sums[RATE_ROW:]], axis=0
    )
    chain.mark(sums)
    sums_across = net.z_across(sums, net.bits[0])
    (across,) = product.second(sums_across)
    output_product.second()
    sum_up.trade()
    sums = chain(sums) + across
    chain.mark(sums)
    sums_across = net.z_across(sums, net.bits[1])
    grad_normed, across = product.last(sums_across)
    sums = sums + across
    for bit in net.bits[2:]:
        sums = sums + net.z_across(sums, bit)
    grad_from_first, gain_one = norm_back(resid, scale_one, gains[0], grad_normed)
    grad_input = grad_middle + grad_from_first
    chain.mark(gain_one)
    sum_out.finish(position)
    sum_out.trade()
    sum_in.finish(position)
    sum_in.trade()

    totals = (sum_down, sum_gate, sum_up, sum_out, sum_in)
    square = sum((jnp.sum(total.square) for total in totals))
    square = square + jnp.sum(sums * sums) / net.groups
    last = jnp.concatenate(
        [gain_one.reshape(-1, LANES), gain_two.reshape(-1, LANES), jnp.full((8, LANES), square)]
    )
    last = chain(last)
    chain.mark(last)
    last = last + chain.wait(net.c(last))
    chain.mark(last)
    across, more = chain.wait(net.x(last), net.x(tie(sums, last)))
    last = last + across
    sums = in_order(sums[None], more[None], x, 0)[None]
    across, more = chain.wait(net.y(last), net.c(tie(sums, last)))
    last = last + across
    sums = in_order(sums, more, c, 0)[None]
    chain.mark(last)
    for bit in net.bits:
        across = net.z_across(last, bit)
        if bit == net.bits[0]:
            more = net.y(tie(sums, last))
            shard_out = sum_out.shard(rows_shard_kernel, position, (2 * channels, depth))
            shard_up = sum_up.shard(
                turned_shard_kernel, position, (depth, 2 * hidden), turned
            )
            across, more = chain.wait(across, more)
            sums = in_order(sums, more, y, 0)
            sums = sums.reshape(8, COEF_ROWS, channels).transpose(1, 0, 2)
            sums = chain(sums.reshape(COEF_ROWS, model))
            chain.mark(sums)
        else:
            if bit == net.bits[1]:
                shard_in = sum_in.shard(in_shard_kernel, position, (3, depth, 2 * channels))
                (rest,) = output_product.last()
                output = low(middle + rest)
                chain.mark(output)
            across = chain.wait(across)
        last = last + across
        chain.mark(last)
    shard_in = shard_in.transpose(1, 0, 2)
    input_grad = low(grad_input)
    radial_grad = scale_one[:, 0] * jnp.sum(resid * grad_input, axis=1) / model**0.5
    grad_taps = sums[: 3 * TAPS].reshape(taps.shape)
    grad_skip = sums[SKIP_ROW]
    grad_residues = sums[RES_ROW:RATE_ROW]
    grad_log_rates = sums[RATE_ROW:]
    span = model // LANES
    grad_gains = last[: 2 * span].reshape(2, model)
    square_total = last[2 * span, 0] + jnp.sum(grad_gains * grad_gains)
    grad_norm = jnp.sqrt(square_total)
    factor = jnp.minimum(1.0, CLIP / (grad_norm + 1e-06))
    factor = tie(factor, shard_in, shard_out, shard_down, shard_gate, shard_up, sums)

    return (
        output,
        input_grad,
        radial_grad,
        *adam(gains, gains_first, gains_second, grad_gains * factor, RATE_SMALL, 0.0),
        *adam(taps, taps_first, taps_second, grad_taps * factor, RATE_SMALL, 0.0),
        *adam(
            residues, residues_first, residues_second, grad_residues * factor, RATE_SMALL, 0.0
        ),
        *adam(
            log_rates,
            log_rates_first,
            log_rates_second,
            grad_log_rates * factor,
            RATE_RATES,
            0.0,
        ),
        *adam(skip, skip_first, skip_second, grad_skip * factor, RATE_SMALL, 0.0),
        *adam(
            in_weight, in_weight_first, in_weight_second, shard_in * factor, RATE_MATRIX, DECAY
        ),
        *adam(
            out_weight, out_weight_first, out_weight_second, shard_out * factor, RATE_MATRIX, DECAY
        ),
        *adam(
            gate_weight,
            gate_weight_first,
            gate_weight_second,
            shard_gate * factor,
            RATE_MATRIX,
            DECAY,
        ),
        *adam(up_weight, up_weight_first, up_weight_second, shard_up * factor, RATE_MATRIX, DECAY),
        *adam(
            down_weight,
            down_weight_first,
            down_weight_second,
            shard_down * factor,
            RATE_MATRIX,
            DECAY,
        ),
        grad_norm,
    )


def solution(mesh):
    net = Links(mesh.shape["dp"] // 2)
    rows = P(("dp", "mp"), None)
    split_in = P("dp", None, "mp")
    split_out = P("mp", "dp")
    split_up = P("dp", "mp")
    matrices = (split_in,) * 3 + (split_out,) * 3 + (split_up,) * 6 + (split_out,) * 3
    return jax.shard_map(
        functools.partial(on_device, net),
        mesh=mesh,
        in_specs=(rows, rows, P("dp"), P()) + (P(),) * 15 + matrices,
        out_specs=(rows, rows, P(("dp", "mp"))) + (P(),) * 15 + matrices + (P(),),
        check_vma=False,
    )
```

```python
import functools

import jax
import jax.numpy as jnp
from jax import lax
from jax.experimental import pallas as pl
from jax.experimental.pallas import tpu as pltpu
from jax.sharding import PartitionSpec as P

STEP = 10


EPSILON = 1e-05
CLIP = 1.0
BETA_ONE = 0.9
BETA_TWO = 0.95
ADAM_EPSILON = 1e-08
DECAY = 0.1
RATE_MATRIX = 0.05
RATE_SMALL = 0.5
RATE_RATES = 4.0

LANES = 128
CHUNK = 128
CHUNKS = 8
LENGTH = CHUNK * CHUNKS
PAD = 8
TAPS = 3
POLES = 16
SKIP_ROW = TAPS * 3
RES_ROW = 16
RATE_ROW = RES_ROW + POLES
COEF_ROWS = RATE_ROW + POLES
MODE_GROUP = 8

f32 = jnp.float32
bf16 = jnp.bfloat16


def chunk_row(pos_ref, seq, n):
    block, half = n // 2, n % 2
    y, c = pos_ref[0], pos_ref[1]
    dy = y if block // 2 == 0 else 1 - y
    dc = c if block % 2 == 0 else 1 - c
    if half == 0:
        row = dc * LENGTH + seq * (4 * CHUNK) + dy * CHUNK
    else:
        row = dc * LENGTH + dy * (4 * CHUNK) + 2 * CHUNK + seq * CHUNK
    return pl.multiple_of(row, CHUNK)


def mix_chunk(pad_ref, coef, which, n):
    base = PAD + n * CHUNK
    total = coef[which : which + 1, :] * pad_ref[pl.ds(base, CHUNK), :]
    for i in range(1, TAPS):
        row = 3 * i + which
        total = total + coef[row : row + 1, :] * pad_ref[pl.ds(base - i, CHUNK), :]
    return total


def spread(row):
    return jnp.broadcast_to(row, (CHUNKS, LANES))


def power_of_two(value, doublings):
    for _ in range(doublings):
        value = value * value
    return value


def shift_down(value, count):
    rolled = pltpu.roll(value, count, 0)
    place = lax.broadcasted_iota(jnp.int32, (CHUNKS, LANES), 0)
    return jnp.where(place >= count, rolled, 0.0)


def shift_up(value, count):
    rolled = pltpu.roll(value, CHUNKS - count, 0)
    place = lax.broadcasted_iota(jnp.int32, (CHUNKS, LANES), 0)
    return jnp.where(place < CHUNKS - count, rolled, 0.0)


def tile_rows(t):
    return pl.ds(pl.multiple_of(t * CHUNKS, CHUNKS), CHUNKS)


def forward_kernel(pos_ref, proj_ref, coef_ref, branch_ref, conv_ref, pads, u_ref, y_ref):
    coef = coef_ref[...]
    decay = [spread(coef[RATE_ROW + p : RATE_ROW + p + 1, :]) for p in range(POLES)]
    weight = [spread(coef[RES_ROW + p : RES_ROW + p + 1, :]) for p in range(POLES)]
    skip = coef[SKIP_ROW : SKIP_ROW + 1, :]
    y_ref[pl.ds(0, CHUNKS), :] = jnp.zeros((CHUNKS, LANES), f32)
    zero = y_ref[pl.ds(0, CHUNKS), :]
    for seq in range(2):
        for j in range(3):
            pads[j, pl.ds(0, PAD), :] = jnp.zeros((PAD, LANES), f32)
        for n in range(CHUNKS):
            rows = pl.ds(chunk_row(pos_ref, seq, n), CHUNK)
            for j in range(3):
                pads[j, pl.ds(PAD + n * CHUNK, CHUNK), :] = proj_ref[
                    rows, j * LANES : (j + 1) * LANES
                ]
        for n in range(CHUNKS):
            gated = mix_chunk(pads.at[1], coef, 1, n) * mix_chunk(pads.at[2], coef, 2, n)
            u_ref[pl.ds(n, CHUNK, stride=CHUNKS), :] = gated

        def ends(t, state):
            u = u_ref[tile_rows(t), :]
            return [a * h + u for a, h in zip(decay, state)]

        state = lax.fori_loop(0, CHUNK, ends, [zero] * POLES, unroll=8)
        start = []
        for a, h in zip(decay, state):
            jump = power_of_two(a, 7)
            for count in (1, 2, 4):
                h = h + jump * shift_down(h, count)
                jump = jump * jump
            start.append(shift_down(h, 1))

        def outputs(t, state):
            u = u_ref[tile_rows(t), :]
            state = [a * h + u for a, h in zip(decay, state)]
            terms = [w * h for w, h in zip(weight, state)]
            while len(terms) > 1:
                terms = [l + r for l, r in zip(terms[0::2], terms[1::2])]
            y_ref[tile_rows(t), :] = terms[0]
            return state

        lax.fori_loop(0, CHUNK, outputs, start, unroll=8)
        for n in range(CHUNKS):
            rows = pl.ds(chunk_row(pos_ref, seq, n), CHUNK)
            strided = pl.ds(n, CHUNK, stride=CHUNKS)
            conv = y_ref[strided, :] + skip * u_ref[strided, :]
            conv_ref[rows, :] = conv
            branch_ref[rows, :] = (mix_chunk(pads.at[0], coef, 0, n) * conv).astype(bf16)


def backward_kernel(
    pos_ref,
    proj_ref,
    conv_ref,
    grad_ref,
    coef_ref,
    out_ref,
    sums_ref,
    pads,
    mixed,
    grads,
    u_ref,
    g_ref,
    y_ref,
):
    coef = coef_ref[...]
    decay = [spread(coef[RATE_ROW + p : RATE_ROW + p + 1, :]) for p in range(POLES)]
    weight = [spread(coef[RES_ROW + p : RES_ROW + p + 1, :]) for p in range(POLES)]
    skip = coef[SKIP_ROW : SKIP_ROW + 1, :]
    y_ref[pl.ds(0, CHUNKS), :] = jnp.zeros((CHUNKS, LANES), f32)
    zero = y_ref[pl.ds(0, CHUNKS), :]
    row_zero = jnp.zeros((1, LANES), f32)
    tap_sums = [row_zero] * (3 * TAPS)
    skip_sum = row_zero
    res_sums = [zero] * POLES
    rate_sums = [zero] * POLES
    for seq in range(2):
        for j in range(3):
            pads[j, pl.ds(0, PAD), :] = jnp.zeros((PAD, LANES), f32)
            grads[j, pl.ds(LENGTH, PAD), :] = jnp.zeros((PAD, LANES), f32)
        for n in range(CHUNKS):
            rows = pl.ds(chunk_row(pos_ref, seq, n), CHUNK)
            for j in range(3):
                pads[j, pl.ds(PAD + n * CHUNK, CHUNK), :] = proj_ref[
                    rows, j * LANES : (j + 1) * LANES
                ]
        for n in range(CHUNKS):
            rows = pl.ds(chunk_row(pos_ref, seq, n), CHUNK)
            strided = pl.ds(n, CHUNK, stride=CHUNKS)
            plain = pl.ds(n * CHUNK, CHUNK)
            query = mix_chunk(pads.at[0], coef, 0, n)
            key = mix_chunk(pads.at[1], coef, 1, n)
            value = mix_chunk(pads.at[2], coef, 2, n)
            mixed[0, plain, :] = key
            mixed[1, plain, :] = value
            branch_grad = grad_ref[rows, :]
            grads[0, plain, :] = branch_grad * conv_ref[rows, :]
            u_ref[strided, :] = key * value
            g_ref[strided, :] = branch_grad * query

        def ends(step, state):
            g = g_ref[tile_rows(CHUNK - 1 - step), :]
            after = []
            for a, (b, e) in zip(decay, state):
                ab = a * b
                after.append((ab + g, a * e + ab))
            return after

        state = lax.fori_loop(0, CHUNK, ends, [(zero, zero)] * POLES, unroll=8)
        start = []
        for a, (b, e) in zip(decay, state):
            jump = power_of_two(a, 7)
            span = float(CHUNK)
            for count in (1, 2, 4):
                b_next, e_next = shift_up(b, count), shift_up(e, count)
                e = e + jump * (e_next + span * b_next)
                b = b + jump * b_next
                jump = jump * jump
                span = 2.0 * span
            start.append((shift_up(b, 1), shift_up(e, 1)))

        for first in range(0, POLES, MODE_GROUP):
            modes = range(first, first + MODE_GROUP)

            def outputs(step, state, modes=modes, first=first):
                t = CHUNK - 1 - step
                g = g_ref[tile_rows(t), :]
                u = u_ref[tile_rows(t), :]
                after, terms = [], []
                for p, (b, e, res, rate) in zip(modes, state):
                    ab = decay[p] * b
                    e = decay[p] * e + ab
                    b = ab + g
                    terms.append(weight[p] * b)
                    after.append((b, e, res + u * b, rate + u * e))
                while len(terms) > 1:
                    terms = [l + r for l, r in zip(terms[0::2], terms[1::2])]
                total = terms[0]
                if first > 0:
                    total = total + y_ref[tile_rows(t), :]
                y_ref[tile_rows(t), :] = total
                return after

            begin = [(*start[p], res_sums[p], rate_sums[p]) for p in modes]
            after = lax.fori_loop(0, CHUNK, outputs, begin, unroll=8)
            for p, (_, _, res, rate) in zip(modes, after):
                res_sums[p], rate_sums[p] = res, rate

        for n in range(CHUNKS):
            strided = pl.ds(n, CHUNK, stride=CHUNKS)
            plain = pl.ds(n * CHUNK, CHUNK)
            conv_grad = g_ref[strided, :]
            gated_grad = y_ref[strided, :] + skip * conv_grad
            skip_sum = skip_sum + jnp.sum(conv_grad * u_ref[strided, :], axis=0, keepdims=True)
            grads[1, plain, :] = gated_grad * mixed[1, plain, :]
            grads[2, plain, :] = gated_grad * mixed[0, plain, :]
        for n in range(CHUNKS):
            rows = pl.ds(chunk_row(pos_ref, seq, n), CHUNK)
            for j in range(3):
                here = grads[j, pl.ds(n * CHUNK, CHUNK), :]
                total = coef[j : j + 1, :] * here
                for i in range(TAPS):
                    behind = pads[j, pl.ds(PAD + n * CHUNK - i, CHUNK), :]
                    row = 3 * i + j
                    tap_sums[row] = tap_sums[row] + jnp.sum(here * behind, axis=0, keepdims=True)
                    if i > 0:
                        ahead = grads[j, pl.ds(n * CHUNK + i, CHUNK), :]
                        total = total + coef[row : row + 1, :] * ahead
                out_ref[rows, j * LANES : (j + 1) * LANES] = total.astype(bf16)
    for row in range(3 * TAPS):
        sums_ref[row : row + 1, :] = tap_sums[row]
    sums_ref[SKIP_ROW : SKIP_ROW + 1, :] = skip_sum
    for row in range(SKIP_ROW + 1, RES_ROW):
        sums_ref[row : row + 1, :] = row_zero
    for p in range(POLES):
        sums_ref[RES_ROW + p : RES_ROW + p + 1, :] = jnp.sum(res_sums[p], axis=0, keepdims=True)
        sums_ref[RATE_ROW + p : RATE_ROW + p + 1, :] = jnp.sum(
            rate_sums[p], axis=0, keepdims=True
        )


def mixer_forward(position, proj, coef):
    rows, channels = proj.shape[0], coef.shape[1]
    return pl.pallas_call(
        forward_kernel,
        grid=(channels // LANES,),
        in_specs=[
            pl.BlockSpec(memory_space=pltpu.SMEM),
            pl.BlockSpec((rows, 3 * LANES), lambda i: (0, i)),
            pl.BlockSpec((COEF_ROWS, LANES), lambda i: (0, i)),
        ],
        out_specs=[
            pl.BlockSpec((rows, LANES), lambda i: (0, i)),
            pl.BlockSpec((rows, LANES), lambda i: (0, i)),
        ],
        out_shape=[
            jax.ShapeDtypeStruct((rows, channels), bf16),
            jax.ShapeDtypeStruct((rows, channels), f32),
        ],
        scratch_shapes=[
            pltpu.VMEM((3, PAD + LENGTH, LANES), f32),
            pltpu.VMEM((LENGTH, LANES), f32),
            pltpu.VMEM((LENGTH, LANES), f32),
        ],
        compiler_params=pltpu.CompilerParams(vmem_limit_bytes=16 << 20),
        cost_estimate=pl.CostEstimate(
            flops=1 << 20, bytes_accessed=1 << 10, transcendentals=0
        ),
        name="mixer_forward",
    )(position, proj, coef)


def mixer_backward(position, proj, conv, grad, coef):
    rows, channels = proj.shape[0], coef.shape[1]
    return pl.pallas_call(
        backward_kernel,
        grid=(channels // LANES,),
        in_specs=[
            pl.BlockSpec(memory_space=pltpu.SMEM),
            pl.BlockSpec((rows, 3 * LANES), lambda i: (0, i)),
            pl.BlockSpec((rows, LANES), lambda i: (0, i)),
            pl.BlockSpec((rows, LANES), lambda i: (0, i)),
            pl.BlockSpec((COEF_ROWS, LANES), lambda i: (0, i)),
        ],
        out_specs=[
            pl.BlockSpec((rows, 3 * LANES), lambda i: (0, i)),
            pl.BlockSpec((COEF_ROWS, LANES), lambda i: (0, i)),
        ],
        out_shape=[
            jax.ShapeDtypeStruct((rows, 3 * channels), bf16),
            jax.ShapeDtypeStruct((COEF_ROWS, channels), f32),
        ],
        scratch_shapes=[
            pltpu.VMEM((3, PAD + LENGTH, LANES), f32),
            pltpu.VMEM((2, LENGTH, LANES), f32),
            pltpu.VMEM((3, LENGTH + PAD, LANES), f32),
            pltpu.VMEM((LENGTH, LANES), f32),
            pltpu.VMEM((LENGTH, LANES), f32),
            pltpu.VMEM((LENGTH, LANES), f32),
        ],
        compiler_params=pltpu.CompilerParams(vmem_limit_bytes=24 << 20),
        cost_estimate=pl.CostEstimate(
            flops=1 << 20, bytes_accessed=1 << 10, transcendentals=0
        ),
        name="mixer_backward",
    )(position, proj, conv, grad, coef)


TILE = 256
NO_COST = pl.CostEstimate(flops=1 << 10, bytes_accessed=1 << 10, transcendentals=0)
NT = (((1,), (1,)), ((), ()))
NN = (((1,), (0,)), ((), ()))


def whole_spec(array):
    return pl.BlockSpec(array.shape, lambda i: (0,) * array.ndim, pipeline_mode=pl.Buffered(1))


def up_kernel(scales, rows_ref, gate_w, up_w, inner_ref, scaled_ref, by_gate_ref, by_up_ref):
    piece = TILE // 2
    gate_all = lax.dot_general(rows_ref[...], gate_w[...], NT, preferred_element_type=f32)
    up_all = lax.dot_general(rows_ref[...], up_w[...], NT, preferred_element_type=f32)
    for part in range(2):
        at = slice(part * piece, (part + 1) * piece)
        index = lax.rem(2 * pl.program_id(0) + part, 8)
        other = jnp.where(lax.rem(index, 4) < 2, index // 4, lax.rem(index, 2))
        scale = jnp.where(other == 1, scales[1], scales[0])
        gate, up = gate_all[at], up_all[at]
        sigma = jax.nn.sigmoid(gate)
        silu = gate * sigma
        inner = silu * up
        inner_ref[at, :] = inner.astype(bf16)
        scaled_ref[at, :] = (inner * scale).astype(bf16)
        by_gate_ref[at, :] = (scale * up * sigma * (1.0 + gate * (1.0 - sigma))).astype(bf16)
        by_up_ref[at, :] = (scale * silu).astype(bf16)


def ffn_up(scales, rows, gate_w, up_w):
    count, hidden = rows.shape[0], gate_w.shape[0]
    tile = pl.BlockSpec((TILE, hidden), lambda i: (i, 0))
    return pl.pallas_call(
        up_kernel,
        grid=(count // TILE,),
        in_specs=[
            pl.BlockSpec(memory_space=pltpu.SMEM),
            pl.BlockSpec((TILE, rows.shape[1]), lambda i: (i, 0)),
            whole_spec(gate_w),
            whole_spec(up_w),
        ],
        out_specs=[tile] * 4,
        out_shape=[jax.ShapeDtypeStruct((count, hidden), bf16)] * 4,
        compiler_params=pltpu.CompilerParams(vmem_limit_bytes=20 << 20),
        cost_estimate=NO_COST,
        name="ffn_up",
    )(scales, rows, gate_w, up_w)


def rows_kernel(left, right, out):
    out[...] = lax.dot_general(left[...], right[...], NT, preferred_element_type=f32)


def rows_product(left, right):
    count, width = left.shape
    return pl.pallas_call(
        rows_kernel,
        grid=(count // (2 * TILE),),
        in_specs=[pl.BlockSpec((2 * TILE, width), lambda i: (i, 0)), whole_spec(right)],
        out_specs=pl.BlockSpec((2 * TILE, right.shape[0]), lambda i: (i, 0)),
        out_shape=jax.ShapeDtypeStruct((count, right.shape[0]), f32),
        compiler_params=pltpu.CompilerParams(vmem_limit_bytes=16 << 20),
        cost_estimate=NO_COST,
        name="rows_product",
    )(left, right)


def grad_kernel(rows_ref, down_w, by_gate_ref, by_up_ref, gate_ref, up_ref):
    grad = lax.dot_general(rows_ref[...], down_w[...], NT, preferred_element_type=f32)
    gate_ref[...] = (grad * by_gate_ref[...].astype(f32)).astype(bf16)
    up_ref[...] = (grad * by_up_ref[...].astype(f32)).astype(bf16)


def ffn_grad(rows, down_w, by_gate, by_up):
    count, hidden = rows.shape[0], down_w.shape[0]
    tile = pl.BlockSpec((2 * TILE, hidden), lambda i: (i, 0))
    return pl.pallas_call(
        grad_kernel,
        grid=(count // (2 * TILE),),
        in_specs=[
            pl.BlockSpec((2 * TILE, rows.shape[1]), lambda i: (i, 0)),
            whole_spec(down_w),
            tile,
            tile,
        ],
        out_specs=[tile] * 2,
        out_shape=[jax.ShapeDtypeStruct((count, hidden), bf16)] * 2,
        compiler_params=pltpu.CompilerParams(vmem_limit_bytes=18 << 20),
        cost_estimate=NO_COST,
        name="ffn_grad",
    )(rows, down_w, by_gate, by_up)


def product_kernel(count, adds, tiles, *refs):
    lefts, rights = refs[:count], refs[count : 2 * count]
    outs = refs[-tiles:]
    total = None
    for left, right in zip(lefts, rights):
        term = lax.dot_general(left[...], right[...], NN, preferred_element_type=f32)
        total = term if total is None else total + term
    for tile in range(tiles):

        @pl.when(pl.program_id(0) == tile)
        def _(tile=tile):
            if adds:
                outs[tile][...] = (total + refs[2 * count + tile][...].astype(f32)).astype(bf16)
            else:
                outs[tile][...] = total.astype(bf16)


def product_tiles(lefts, rights, first, tiles, adds=()):
    width = rights[0].shape[1]
    start = first // TILE
    tile_spec = pl.BlockSpec((TILE, width), lambda i: (0, 0))
    return pl.pallas_call(
        functools.partial(product_kernel, len(lefts), len(adds), tiles),
        grid=(tiles,),
        in_specs=[
            pl.BlockSpec((TILE, left.shape[1]), lambda i: (start + i, 0)) for left in lefts
        ]
        + [whole_spec(right) for right in rights]
        + [whole_spec(add) for add in adds],
        out_specs=[tile_spec] * tiles,
        out_shape=[jax.ShapeDtypeStruct((TILE, width), bf16)] * tiles,
        compiler_params=pltpu.CompilerParams(vmem_limit_bytes=22 << 20),
        cost_estimate=NO_COST,
        name="product",
    )(*lefts, *rights, *adds)


def halves_spec(rows, depth):
    return [jax.ShapeDtypeStruct((rows, depth), bf16)] * 2


def mixer_weights_kernel(where_ref, in_ref, out_ref, in_mine, in_other, out_mine, out_other):
    units = in_ref.shape[2] // 2
    tiles = units // LANES
    for side, target in ((where_ref[3], in_mine), (1 - where_ref[3], in_other)):
        for tile in range(tiles):
            start = pl.multiple_of(side * units + tile * LANES, LANES)
            for j in range(3):
                row = (tile * 3 + j) * LANES
                block = in_ref[j, :, pl.ds(start, LANES)]
                target[row : row + LANES, :] = block.T.astype(bf16)
    for side, target in ((where_ref[3], out_mine), (1 - where_ref[3], out_other)):
        rows = pl.ds(pl.multiple_of(side * units, units), units)
        target[...] = out_ref[rows, :].astype(bf16)


def mixer_weights(where, in_weight, out_weight):
    _, depth, channels = in_weight.shape
    units = channels // 2
    return pl.pallas_call(
        mixer_weights_kernel,
        in_specs=[pl.BlockSpec(memory_space=pltpu.SMEM)]
        + [pl.BlockSpec(memory_space=pltpu.VMEM)] * 2,
        out_specs=[pl.BlockSpec(memory_space=pltpu.VMEM)] * 4,
        out_shape=halves_spec(3 * units, depth) + halves_spec(units, depth),
        compiler_params=pltpu.CompilerParams(vmem_limit_bytes=12 << 20),
        cost_estimate=NO_COST,
        name="mixer_weights",
    )(where, in_weight, out_weight)


def ffn_weights_kernel(
    where_ref, gate_ref, up_ref, down_ref, mine, other, down_mine, down_other, turned
):
    units = down_ref.shape[0] // 2
    mine_rows = pl.ds(pl.multiple_of(where_ref[3] * units, units), units)
    other_rows = pl.ds(pl.multiple_of((1 - where_ref[3]) * units, units), units)
    for n, source in enumerate((gate_ref, up_ref)):
        turned[...] = source[...].T
        mine[n * units : (n + 1) * units, :] = turned[mine_rows, :].astype(bf16)
        other[n * units : (n + 1) * units, :] = turned[other_rows, :].astype(bf16)
    down_mine[...] = down_ref[mine_rows, :].astype(bf16)
    down_other[...] = down_ref[other_rows, :].astype(bf16)


def ffn_weights(where, gate_weight, up_weight, down_weight):
    units, depth = down_weight.shape
    return pl.pallas_call(
        ffn_weights_kernel,
        in_specs=[pl.BlockSpec(memory_space=pltpu.SMEM)]
        + [pl.BlockSpec(memory_space=pltpu.VMEM)] * 3,
        out_specs=[pl.BlockSpec(memory_space=pltpu.VMEM)] * 4,
        out_shape=halves_spec(units, depth) + halves_spec(units // 2, depth),
        scratch_shapes=[pltpu.VMEM((units, depth), f32)],
        compiler_params=pltpu.CompilerParams(vmem_limit_bytes=20 << 20),
        cost_estimate=NO_COST,
        name="ffn_weights",
    )(where, gate_weight, up_weight, down_weight)


def branch_grads_kernel(out_w, rows_ref, branch_ref, grad_ref, blocks_ref, total):
    step = pl.program_id(0)
    rows = rows_ref[...]
    grad_ref[...] = lax.dot_general(rows, out_w[...], NT, preferred_element_type=f32)
    term = lax.dot_general(
        branch_ref[...], rows, (((0,), (0,)), ((), ())), preferred_element_type=f32
    )

    @pl.when(step == 0)
    def _():
        total[...] = term

    @pl.when(step > 0)
    def _():
        total[...] += term

    @pl.when(step == pl.num_programs(0) - 1)
    def _():
        groups, _, width = blocks_ref.shape
        for i in range(groups):
            blocks_ref[i] = total[:, i * width : (i + 1) * width].astype(bf16)


def branch_grads(rows, out_w, branch, groups):
    count, model = rows.shape
    channels = out_w.shape[0]
    return pl.pallas_call(
        branch_grads_kernel,
        grid=(count // TILE,),
        in_specs=[
            whole_spec(out_w),
            pl.BlockSpec((TILE, model), lambda i: (i, 0)),
            pl.BlockSpec((TILE, channels), lambda i: (i, 0)),
        ],
        out_specs=[
            pl.BlockSpec((TILE, channels), lambda i: (i, 0)),
            pl.BlockSpec((groups, channels, model // groups), lambda i: (0, 0, 0)),
        ],
        out_shape=[
            jax.ShapeDtypeStruct((count, channels), f32),
            jax.ShapeDtypeStruct((groups, channels, model // groups), bf16),
        ],
        scratch_shapes=[pltpu.VMEM((channels, model), f32)],
        compiler_params=pltpu.CompilerParams(vmem_limit_bytes=12 << 20),
        cost_estimate=NO_COST,
        name="branch_grads",
    )(out_w, rows, branch)


def weight_grad_kernel(left, right, out):
    out[...] = lax.dot_general(
        left[...], right[...], (((0,), (0,)), ((), ())), preferred_element_type=f32
    ).astype(bf16)


def weight_product(left, right, blocks=0):
    depth, units = left.shape
    width = right.shape[1]
    if blocks:
        tile = width // blocks
        out_spec = pl.BlockSpec((None, units, tile), lambda i: (i, 0, 0))
        shape = (blocks, units, tile)
    else:
        tile = min(width, 512)
        out_spec = pl.BlockSpec((units, tile), lambda i: (0, i))
        shape = (units, width)
    return pl.pallas_call(
        weight_grad_kernel,
        grid=(width // tile,),
        in_specs=[whole_spec(left), pl.BlockSpec((depth, tile), lambda i: (0, i))],
        out_specs=out_spec,
        out_shape=jax.ShapeDtypeStruct(shape, bf16),
        compiler_params=pltpu.CompilerParams(vmem_limit_bytes=16 << 20),
        cost_estimate=NO_COST,
        name="weight_product",
    )(left, right)


def finish_kernel(where_ref, total, mine, other, square):
    width = mine.shape[1]
    for side, target in ((where_ref[3], mine), (1 - where_ref[3], other)):
        target[...] = total[:, pl.ds(pl.multiple_of(side * width, LANES), width)]
    values = total[...].astype(f32)
    square[...] = jnp.sum(values * values, axis=0, keepdims=True)


def finish_units(where, total, x):
    units, width = total.shape
    width = width // 2
    if width % LANES != 0:
        mine = lax.dynamic_slice_in_dim(total, x * width, width, 1)
        other = lax.dynamic_slice_in_dim(total, (1 - x) * width, width, 1)
        values = total.astype(f32)
        return mine, other, jnp.sum(values * values, axis=0, keepdims=True)
    return pl.pallas_call(
        finish_kernel,
        in_specs=[
            pl.BlockSpec(memory_space=pltpu.SMEM),
            pl.BlockSpec(memory_space=pltpu.VMEM),
        ],
        out_specs=[pl.BlockSpec(memory_space=pltpu.VMEM)] * 3,
        out_shape=halves_spec(units, width) + [jax.ShapeDtypeStruct((1, 2 * width), f32)],
        compiler_params=pltpu.CompilerParams(vmem_limit_bytes=8 << 20),
        cost_estimate=NO_COST,
        name="finish_units",
    )(where, total)


def rows_shard_kernel(where_ref, mine, other, out):
    units = mine.shape[0]
    for side, source in ((where_ref[3], mine), (1 - where_ref[3], other)):
        rows = pl.ds(pl.multiple_of(side * units, units), units)
        out[rows, :] = source[...].astype(f32)


def turned_shard_kernel(where_ref, mine, other, out, rows):
    rows_shard_kernel(where_ref, mine, other, rows)
    out[...] = rows[...].T


def in_shard_kernel(where_ref, mine, other, out):
    units = mine.shape[0] // 3
    for side, source in ((where_ref[3], mine), (1 - where_ref[3], other)):
        for tile in range(units // LANES):
            start = pl.multiple_of(side * units + tile * LANES, LANES)
            for j in range(3):
                row = (tile * 3 + j) * LANES
                block = source[row : row + LANES, :].astype(f32)
                out[j, :, pl.ds(start, LANES)] = block.T


def shard_of(kernel, where, mine, other, shape, scratch=()):
    return pl.pallas_call(
        kernel,
        in_specs=[pl.BlockSpec(memory_space=pltpu.SMEM)]
        + [pl.BlockSpec(memory_space=pltpu.VMEM)] * 2,
        out_specs=pl.BlockSpec(memory_space=pltpu.VMEM),
        out_shape=jax.ShapeDtypeStruct(shape, f32),
        scratch_shapes=list(scratch),
        compiler_params=pltpu.CompilerParams(vmem_limit_bytes=12 << 20),
        cost_estimate=NO_COST,
        name="shard",
    )(where, mine, other)


def rows_by_rows(left, right):
    return lax.dot_general(left, right, (((1,), (1,)), ((), ())), preferred_element_type=f32)


def columns_by_columns(left, right):
    return lax.dot_general(left, right, (((0,), (0,)), ((), ())), preferred_element_type=f32)


def plain_dot(left, right):
    return jnp.dot(left, right, preferred_element_type=f32)


def low(values):
    return values.astype(bf16)


def add_low(left, right):
    return (left.astype(f32) + right.astype(f32)).astype(bf16)


def norm_back(values, scale, gain, grad):
    weighted = grad * gain
    inner_mean = jnp.mean(values * weighted, axis=1, keepdims=True)
    return (
        scale * weighted - values * (scale * scale * scale) * inner_mean,
        jnp.sum(grad * values * scale, axis=0),
    )


def adam(weight, first, second, grad, rate, decay):
    first_new = BETA_ONE * first + (1.0 - BETA_ONE) * grad
    second_new = BETA_TWO * second + (1.0 - BETA_TWO) * grad * grad
    stride = (
        first_new
        / (1.0 - BETA_ONE**STEP)
        / (jnp.sqrt(second_new / (1.0 - BETA_TWO**STEP)) + ADAM_EPSILON)
    )
    return (weight - rate * (stride + decay * weight), first_new, second_new)


class Links:
    def __init__(self, groups):
        self.groups = groups
        places = [(z, x) for z in range(groups) for x in (0, 1)]
        self.ring = [(2 * z + x, 2 * ((z + 1) % groups) + x) for z, x in places]
        self.lines = [[2 * z + x for z in range(groups)] for x in (0, 1)]
        self.over_x = [(2 * z + x, 2 * z + 1 - x) for z, x in places]
        self.over_y = [(2 * y + c, 2 * (1 - y) + c) for y in (0, 1) for c in (0, 1)]
        self.over_c = [(2 * y + c, 2 * y + 1 - c) for y in (0, 1) for c in (0, 1)]
        self.bits = [1 << n for n in range(groups.bit_length() - 1)]
        self.across = {
            bit: [(2 * z + x, 2 * (z ^ bit) + x) for z, x in places] for bit in self.bits
        }

    def z(self, v):
        return lax.ppermute(v, "dp", self.ring)

    def z_across(self, v, bit):
        return lax.ppermute(v, "dp", self.across[bit])

    def x(self, v):
        return lax.ppermute(v, "dp", self.over_x)

    def y(self, v):
        return lax.ppermute(v, "mp", self.over_y)

    def c(self, v):
        return lax.ppermute(v, "mp", self.over_c)


def tie(value, *before):
    return lax.optimization_barrier((value, *before))[0] if before else value


class Chain:
    def __init__(self):
        self.held = ()

    def __call__(self, value, *before):
        return tie(value, *self.held, *before)

    def mark(self, *done):
        self.held = done

    def wait(self, *arrived):
        together = lax.optimization_barrier((*arrived, *self.held))[: len(arrived)]
        self.held = together[:1]
        return together[0] if len(arrived) == 1 else together


def copy_kernel(count, place, *refs):
    where, pieces, whole, sems = refs[0], refs[1 : count + 1], refs[count + 1], refs[count + 2]
    copies = [
        pltpu.make_async_copy(piece, whole.at[place(where, i)], sems.at[i])
        for i, piece in enumerate(pieces)
    ]
    for copy in copies:
        copy.start()
    for copy in copies:
        copy.wait()


def assemble_columns(first, pieces, place, where, shape):
    arrays, offsets = [first], [pieces[0][1]]
    index = []
    for i, (array, offset) in enumerate(pieces):
        known = [n for n, other in enumerate(arrays) if other is array]
        if i == 0:
            index.append((0, offset))
        elif array is pieces[0][0]:
            index.append((0, offset))
        elif known:
            index.append((known[0], offset))
        else:
            arrays.append(array)
            index.append((len(arrays) - 1, offset))
    count = len(arrays)
    units = shape[0]

    def kernel(*refs):
        where_ref, sources, whole, sems = refs[0], refs[1 : count + 1], refs[count + 1], refs[-1]
        copies = [
            pltpu.make_async_copy(
                sources[n].at[pl.ds(offset, units), :],
                whole.at[place(where_ref, i)],
                sems.at[i],
            )
            for i, (n, offset) in enumerate(index)
        ]
        for copy in copies:
            copy.start()
        for copy in copies:
            copy.wait()

    return pl.pallas_call(
        kernel,
        in_specs=[pl.BlockSpec(memory_space=pltpu.SMEM)]
        + [pl.BlockSpec(memory_space=pl.ANY)] * count,
        out_specs=pl.BlockSpec(memory_space=pltpu.VMEM),
        out_shape=jax.ShapeDtypeStruct(shape, bf16),
        scratch_shapes=[pltpu.SemaphoreType.DMA((len(pieces),))],
        compiler_params=pltpu.CompilerParams(vmem_limit_bytes=8 << 20),
        cost_estimate=pl.CostEstimate(
            flops=0, bytes_accessed=4 * units * shape[1], transcendentals=0
        ),
        name="assemble_columns",
    )(where, *arrays)


def assemble_blocks(blocks, where):
    groups, rows, width = blocks.shape

    def kernel(where_ref, source, whole, sems):
        copies = [
            pltpu.make_async_copy(
                source.at[i], whole.at[:, pl.ds(i * width, width)], sems.at[i]
            )
            for i in range(groups)
        ]
        for copy in copies:
            copy.start()
        for copy in copies:
            copy.wait()

    return pl.pallas_call(
        kernel,
        in_specs=[pl.BlockSpec(memory_space=pltpu.SMEM), pl.BlockSpec(memory_space=pl.ANY)],
        out_specs=pl.BlockSpec(memory_space=pltpu.VMEM),
        out_shape=jax.ShapeDtypeStruct((rows, groups * width), bf16),
        scratch_shapes=[pltpu.SemaphoreType.DMA((groups,))],
        compiler_params=pltpu.CompilerParams(vmem_limit_bytes=10 << 20),
        cost_estimate=NO_COST,
        name="assemble_blocks",
    )(where, blocks)


def assemble_rows(pieces, where, shape):
    arrays = []
    for array, *_ in pieces:
        if not any(array is other for other in arrays):
            arrays.append(array)
    index = [next(n for n, other in enumerate(arrays) if other is p[0]) for p in pieces]
    count = len(arrays)

    def kernel(*refs):
        sources, whole, sems = refs[1 : count + 1], refs[-2], refs[-1]
        copies = []
        for i, (n, (_, start, rows, target)) in enumerate(zip(index, pieces)):
            source = sources[n].at[pl.ds(start, rows), :]
            copies.append(
                pltpu.make_async_copy(source, whole.at[pl.ds(target, rows), :], sems.at[i])
            )
        for copy in copies:
            copy.start()
        for copy in copies:
            copy.wait()

    return pl.pallas_call(
        kernel,
        in_specs=[pl.BlockSpec(memory_space=pltpu.SMEM)]
        + [pl.BlockSpec(memory_space=pl.ANY)] * count,
        out_specs=pl.BlockSpec(memory_space=pltpu.VMEM),
        out_shape=jax.ShapeDtypeStruct(shape, bf16),
        scratch_shapes=[pltpu.SemaphoreType.DMA((len(pieces),))],
        compiler_params=pltpu.CompilerParams(vmem_limit_bytes=10 << 20),
        cost_estimate=NO_COST,
        name="assemble_rows",
    )(where, *arrays)


class GatherRows:
    def __init__(self, net, chain, block):
        self.net, self.chain = net, chain
        half = block.shape[0] // 2
        self.a, self.b = block[:half], block[half:]
        self.a_x, self.b_y = net.x(self.a), net.y(self.b)

    def second(self, *more):
        net, chain = self.net, self.chain
        got = chain.wait(self.a_x, self.b_y, *more)
        a_x, b_y = got[:2]
        self.a = jnp.concatenate([self.a, a_x], axis=0)
        self.b = jnp.concatenate([self.b, b_y], axis=0)
        chain.mark(self.a, self.b)
        self.a_y, self.b_x = net.y(self.a), net.x(self.b)
        self.far_a, self.far_b = net.c(self.a), net.c(self.b)
        return got[2:]

    def third(self, *more):
        got = self.chain.wait(self.a_y, self.b_x, *more)
        self.a_y, self.b_x = got[:2]
        return got[2:]

    def trade(self):
        a_y, b_x = (tie(piece, *self.chain.held) for piece in (self.a_y, self.b_x))
        self.far_a_y, self.far_b_x = self.net.c(a_y), self.net.c(b_x)

    def whole(self, where):
        chain = self.chain
        far_a, far_b, far_a_y, far_b_x = chain.wait(
            self.far_a, self.far_b, self.far_a_y, self.far_b_x
        )
        rows = self.a.shape[0] // 2
        near = (self.a, self.a_y, self.b, self.b_x)
        far = (far_a, far_a_y, far_b, far_b_x)
        pieces = []
        for core, arrays in enumerate((near, far)):
            for place, array in enumerate(arrays):
                first = (8 * core + place) * rows
                pieces += [(array, 0, rows, first), (array, rows, rows, first + 4 * rows)]
        whole = assemble_rows(pieces, where, (16 * rows, self.a.shape[1]))
        chain.mark(whole)
        return whole


class ScatterProduct:
    def __init__(self, net, chain, lefts, rights):
        self.net, self.chain = net, chain
        self.lefts, self.rights = lefts, rights
        self.far = self.tiles(4, 4)

    def tiles(self, first, count, adds=()):
        lefts = [self.chain(self.lefts[0]), *self.lefts[1:]]
        tiles = product_tiles(lefts, self.rights, first * TILE, count, adds)
        self.chain.mark(tiles[0])
        return tiles

    def trade(self):
        held = [tie(tile, *self.chain.held) for tile in self.far]
        self.far = [self.net.c(tile) for tile in held]

    def arrived(self):
        self.far = self.chain.wait(*self.far)

    def near(self):
        self.a, self.b, self.for_x, self.for_y = self.tiles(0, 4, self.far)

    def send(self):
        net = self.net
        for_x, for_y = (tie(tile, *self.chain.held) for tile in (self.for_x, self.for_y))
        self.from_x, self.from_y = net.x(for_x), net.y(for_y)

    def second(self, *more):
        net, chain, piece = self.net, self.chain, TILE // 2
        got = chain.wait(self.from_x, self.from_y, *more)
        self.from_x, self.from_y = got[:2]
        a_y = add_low(self.a[piece:], self.from_x[piece:])
        b_x = add_low(self.b[piece:], self.from_y[piece:])
        self.a_y, self.b_x = net.y(a_y), net.x(b_x)
        chain.mark(a_y, b_x)
        return got[2:]

    def last(self, *more):
        got = self.chain.wait(self.a_y, self.b_x, *more)
        self.a_y, self.b_x = got[:2]
        return (self.sum(), *got[2:])

    def sum(self):
        piece = TILE // 2
        a_y, b_x = self.a_y, self.b_x
        a = self.a[:piece].astype(f32) + self.from_x[:piece].astype(f32) + a_y.astype(f32)
        b = self.b[:piece].astype(f32) + self.from_y[:piece].astype(f32) + b_x.astype(f32)
        return jnp.concatenate([a, b], axis=0)


def pick(pair, index):
    return lax.dynamic_index_in_dim(pair, index, 0, keepdims=False)


def in_order(mine, other, x, axis):
    return jnp.where(
        x == 0,
        jnp.concatenate([mine, other], axis=axis),
        jnp.concatenate([other, mine], axis=axis),
    )


class GatherUnits:
    def __init__(self, net, chain, mine, other, x, z):
        self.net, self.chain, self.x, self.z = net, chain, x, z
        self.first, self.out = mine, other

    def trade(self, *after):
        self.got = self.net.x(tie(self.out, *after))

    def traded(self, merge, got=None):
        got = self.chain.wait(self.got) if got is None else got
        if merge:
            pair = self.chain(jnp.concatenate([self.first, got], axis=0))
            self.chain.mark(pair)
            self.rings = [[pair]]
        else:
            self.rings = [[self.first], [got]]

    def send(self, ring=0, *after):
        hops = self.rings[ring]
        hops.append(self.net.z(tie(hops[-1], *after)))

    def gather(self, first, last):
        pair = self.rings[0][0]
        units = pair.shape[0] // 2
        mine, other = pair[first:last], pair[units + first : units + last]
        piece = self.chain(in_order(mine, other, self.x, 1))
        self.chain.mark(piece)
        return lax.all_gather(piece, "dp", axis_index_groups=self.net.lines)

    def coming(self, ring=0):
        return self.rings[ring][-1]

    def came(self, piece, ring=0):
        self.rings[ring][-1] = piece

    def arrived(self, ring=0):
        self.came(self.chain.wait(self.coming(ring)), ring)

    def whole(self, where, ranges):
        groups, chain = self.net.groups, self.chain
        for ring in range(len(self.rings)):
            while len(self.rings[ring]) < groups:
                self.send(ring)
                self.arrived(ring)
        units, width = self.first.shape
        merged = len(self.rings) == 1
        wholes = []
        for first, last in ranges:
            pieces = []
            for step in range(groups):
                for side in range(2):
                    piece = self.rings[0 if merged else side][step]
                    offset = side * units if merged else 0
                    pieces.append((piece, offset + first))
            if width % LANES == 0:

                def place(where_ref, i):
                    block = lax.rem(where_ref[2] + (groups - i // 2), groups) * 2
                    side = where_ref[3] if i % 2 == 0 else 1 - where_ref[3]
                    start = pl.multiple_of((block + side) * width, LANES)
                    return (slice(None), pl.ds(start, width))

                shape = (last - first, 2 * width * groups)
                whole = assemble_columns(
                    chain(pieces[0][0]), pieces, place, where, shape
                )
            else:
                whole = jnp.zeros((last - first, 2 * width * groups), bf16)
                for i, (piece, offset) in enumerate(pieces):
                    block = 2 * lax.rem(self.z + groups - i // 2, groups)
                    side = self.x if i % 2 == 0 else 1 - self.x
                    part = piece[offset : offset + last - first]
                    whole = lax.dynamic_update_slice(whole, part, (0, (block + side) * width))
            chain.mark(whole)
            wholes.append(whole)
        return wholes


class ReducedUnits:
    def __init__(self, net, chain, blocks, x):
        self.net, self.chain, self.x = net, chain, x
        self.total = lax.psum_scatter(blocks, "dp", axis_index_groups=net.lines)

    def finish(self, where, total=None):
        total = self.chain.wait(self.total) if total is None else total
        self.mine, self.other, self.square = finish_units(where, total, self.x)
        self.chain.mark(self.mine, self.other, self.square)

    def trade(self):
        self.traded = self.net.x(tie(self.other, *self.chain.held))

    def shard(self, kernel, where, shape, scratch=()):
        got = self.chain(self.traded)
        shard = shard_of(kernel, where, self.mine, got, shape, scratch)
        self.chain.mark(shard)
        return shard


def on_device(
    net,
    tokens,
    cotangent,
    group_ids,
    group_scales,
    gains,
    gains_first,
    gains_second,
    taps,
    taps_first,
    taps_second,
    residues,
    residues_first,
    residues_second,
    log_rates,
    log_rates_first,
    log_rates_second,
    skip,
    skip_first,
    skip_second,
    in_weight,
    in_weight_first,
    in_weight_second,
    out_weight,
    out_weight_first,
    out_weight_second,
    gate_weight,
    gate_weight_first,
    gate_weight_second,
    up_weight,
    up_weight_first,
    up_weight_second,
    down_weight,
    down_weight_first,
    down_weight_second,
):
    model = tokens.shape[1]
    depth = in_weight.shape[0]
    channels = in_weight.shape[2] // 2
    hidden = gate_weight.shape[1] // 2
    tiles = channels // LANES
    dp, mp = lax.axis_index("dp"), lax.axis_index("mp")
    z, x, y, c = dp // 2, dp % 2, mp // 2, mp % 2
    begin = (mp * 2 + x) * channels
    position = jnp.stack([y, c, z, x]).astype(jnp.int32)

    def own(array):
        return lax.dynamic_slice_in_dim(array, begin, channels, array.ndim - 1)

    chain = Chain()
    resid = tokens.astype(f32)
    scale_one = lax.rsqrt(jnp.mean(resid * resid, axis=1, keepdims=True) + EPSILON)
    normed = low(resid * scale_one * gains[0])
    chain.mark(normed)
    in_mine, in_other, out_mine, out_other = mixer_weights(
        position, chain(in_weight.transpose(1, 0, 2)), out_weight
    )
    chain.mark(in_mine)
    ring_in = GatherUnits(net, chain, in_mine, in_other, x, z)
    ring_in.trade()
    ring_in.rings = [[ring_in.first]]
    ring_in.send()
    ring_out = GatherUnits(net, chain, out_mine, out_other, x, z)
    sequence_scale = jnp.sum(
        jnp.where(
            group_ids[:, None] == jnp.arange(group_scales.shape[0], dtype=jnp.int32)[None, :],
            group_scales[None, :],
            0.0,
        )
    )

    first, got = chain.wait(ring_in.coming(0), ring_in.got)
    ring_in.came(first, 0)
    ring_in.rings.append([got])
    ring_in.send(0)
    ring_in.send(1)
    normed_rows = GatherRows(net, chain, chain(normed))
    gate_mine, gate_other, down_mine, down_other = ffn_weights(
        position, chain(gate_weight), up_weight, down_weight
    )
    chain.mark(gate_mine)
    ring_gu = GatherUnits(net, chain, gate_mine, gate_other, x, z)
    ring_down = GatherUnits(net, chain, down_mine, down_other, x, z)
    ring_out.trade()
    other_scale = net.x(chain(sequence_scale).reshape(1, 1))
    got, other_scale, first, second = normed_rows.second(
        ring_out.got, other_scale, ring_in.coming(0), ring_in.coming(1)
    )
    ring_in.came(first, 0)
    ring_in.came(second, 1)
    ring_in.send(0)
    ring_in.send(1)
    ring_out.traded(True, got)
    ring_out.send()
    residues_own = own(residues)
    rates_own = jnp.exp(own(log_rates))
    coef = jnp.concatenate(
        [
            own(taps).reshape(3 * TAPS, channels),
            own(skip)[None],
            jnp.zeros((RES_ROW - SKIP_ROW - 1, channels), f32),
            residues_own,
            jnp.exp(-rates_own),
        ],
        axis=0,
    )
    coef = chain(coef)
    chain.mark(coef)
    first, got, piece = normed_rows.third(
        ring_in.coming(0), ring_in.coming(1), ring_out.coming()
    )
    ring_in.came(first, 0)
    ring_in.came(got, 1)
    ring_out.came(piece)
    ring_in.send(1)
    ring_out.send()
    ring_gu.trade(*chain.held)
    normed_rows.trade()
    normed_all = normed_rows.whole(position)
    got, piece, traded = chain.wait(ring_in.coming(1), ring_out.coming(), ring_gu.got)
    ring_in.came(got, 1)
    ring_out.came(piece)
    ring_out.send()
    ring_gu.traded(True, traded)
    gate_blocks = ring_gu.gather(0, hidden)
    up_blocks = ring_gu.gather(hidden, 2 * hidden)
    cotangent = chain(cotangent)
    back_rows = GatherRows(net, chain, cotangent)
    (w_in,) = ring_in.whole(position, [(0, 3 * channels)])

    proj = rows_product(chain(normed_all), w_in)
    chain.mark(proj)
    back_rows.second()
    branch, conv = mixer_forward(position, chain(proj), coef)
    chain.mark(branch)
    (piece,) = back_rows.third(ring_out.coming())
    ring_out.came(piece)
    (w_out,) = ring_out.whole(position, [(0, channels)])
    product = ScatterProduct(net, chain, [branch], [w_out])
    product.trade()
    product.arrived()
    product.near()
    product.send()
    back_rows.trade()
    back_all = back_rows.whole(position)
    (gate_blocks,) = product.second(gate_blocks)
    ring_down.trade(*chain.held)
    w_gate = assemble_blocks(chain(gate_blocks), position)
    chain.mark(w_gate)
    (more,) = product.last()
    middle = resid + more
    scale_two = lax.rsqrt(jnp.mean(middle * middle, axis=1, keepdims=True) + EPSILON)
    normed_two = low(middle * scale_two * gains[1])
    chain.mark(normed_two)
    normed_two_rows = GatherRows(net, chain, normed_two)
    normed_two_rows.second()
    got, up_blocks = chain.wait(ring_down.got, up_blocks)
    ring_down.traded(True, got)
    down_blocks = ring_down.gather(0, hidden)
    w_up = assemble_blocks(chain(up_blocks), position)
    chain.mark(w_up)
    scales = chain(jnp.concatenate([sequence_scale.reshape(1), other_scale.reshape(1)]))
    chain.mark(scales)
    normed_two_rows.third()
    normed_two_rows.trade()
    normed_two_all = normed_two_rows.whole(position)
    inner_low, inner_scaled, by_gate, by_up = ffn_up(
        scales, chain(normed_two_all), w_gate, w_up
    )
    chain.mark(inner_scaled, inner_low)

    def blocks_of(left, right):
        grad = weight_product(chain(left), right, net.groups)
        chain.mark(grad)
        return grad

    def reduced(grad):
        return ReducedUnits(net, chain, chain(grad), x)

    sum_down = reduced(blocks_of(inner_scaled, back_all))
    w_down = assemble_blocks(chain.wait(down_blocks), position)
    chain.mark(w_down)
    grad_gate, grad_up = ffn_grad(chain(back_all), w_down, by_gate, by_up)
    chain.mark(grad_gate, grad_up)
    product = ScatterProduct(net, chain, [grad_gate, grad_up], [w_gate, w_up])
    product.trade()
    product.arrived()
    product.near()
    product.send()
    grad_gate = blocks_of(grad_gate, normed_two_all)
    grad_up = blocks_of(grad_up, normed_two_all)
    product.second()
    sum_gate, sum_up = reduced(grad_gate), reduced(grad_up)
    output_product = ScatterProduct(net, chain, [inner_low], [w_down])
    output_product.trade()
    (grad_normed_two,) = product.last()
    grad_from_norm, gain_two = norm_back(middle, scale_two, gains[1], grad_normed_two)
    grad_middle = cotangent.astype(f32) * sequence_scale + grad_from_norm
    grad_middle_low = low(grad_middle)
    chain.mark(grad_middle_low)
    grad_middle_rows = GatherRows(net, chain, grad_middle_low)
    output_product.arrived()
    output_product.near()
    (got,) = grad_middle_rows.second(sum_down.total)
    sum_down.finish(position, got)
    (got,) = grad_middle_rows.third(sum_gate.total)
    grad_middle_rows.trade()
    output_product.send()
    sum_gate.finish(position, got)
    sum_down.trade()
    sum_gate.trade()
    grad_middle_all = grad_middle_rows.whole(position)
    grad_branch, grad_out = branch_grads(chain(grad_middle_all), w_out, branch, net.groups)
    chain.mark(grad_branch)
    sum_out = reduced(grad_out)
    grad_proj, sums = mixer_backward(position, proj, conv, chain(grad_branch), coef)
    chain.mark(grad_proj)
    product = ScatterProduct(net, chain, [grad_proj], [w_in])
    output_product.from_x, output_product.from_y, sum_down.traded, sum_gate.traded = chain.wait(
        output_product.from_x, output_product.from_y, sum_down.traded, sum_gate.traded
    )
    product.trade()
    grad_in = blocks_of(grad_proj, normed_all)
    product.arrived()
    sum_in = reduced(grad_in)
    product.near()
    product.send()
    sum_up.finish(position)
    turned = [pltpu.VMEM((2 * hidden, depth), f32)]
    shard_down = sum_down.shard(rows_shard_kernel, position, (2 * hidden, depth))
    shard_gate = sum_gate.shard(turned_shard_kernel, position, (depth, 2 * hidden), turned)

    sums = chain(sums)
    sums = jnp.concatenate(
        [sums[:RATE_ROW], -rates_own * residues_own * sums[RATE_ROW:]], axis=0
    )
    chain.mark(sums)
    sums_across = net.z_across(sums, net.bits[0])
    (across,) = product.second(sums_across)
    output_product.second()
    sum_up.trade()
    sums = chain(sums) + across
    chain.mark(sums)
    sums_across = net.z_across(sums, net.bits[1])
    grad_normed, across = product.last(sums_across)
    sums = sums + across
    for bit in net.bits[2:]:
        sums = sums + net.z_across(sums, bit)
    grad_from_first, gain_one = norm_back(resid, scale_one, gains[0], grad_normed)
    grad_input = grad_middle + grad_from_first
    chain.mark(gain_one)
    sum_out.finish(position)
    sum_out.trade()
    sum_in.finish(position)
    sum_in.trade()

    totals = (sum_down, sum_gate, sum_up, sum_out, sum_in)
    square = sum((jnp.sum(total.square) for total in totals))
    square = square + jnp.sum(sums * sums) / net.groups
    last = jnp.concatenate(
        [gain_one.reshape(-1, LANES), gain_two.reshape(-1, LANES), jnp.full((8, LANES), square)]
    )
    last = chain(last)
    chain.mark(last)
    last = last + chain.wait(net.c(last))
    chain.mark(last)
    across, more = chain.wait(net.x(last), net.x(tie(sums, last)))
    last = last + across
    sums = in_order(sums[None], more[None], x, 0)[None]
    across, more = chain.wait(net.y(last), net.c(tie(sums, last)))
    last = last + across
    sums = in_order(sums, more, c, 0)[None]
    chain.mark(last)
    for bit in net.bits:
        across = net.z_across(last, bit)
        if bit == net.bits[0]:
            more = net.y(tie(sums, last))
            shard_out = sum_out.shard(rows_shard_kernel, position, (2 * channels, depth))
            shard_up = sum_up.shard(
                turned_shard_kernel, position, (depth, 2 * hidden), turned
            )
            across, more = chain.wait(across, more)
            sums = in_order(sums, more, y, 0)
            sums = sums.reshape(8, COEF_ROWS, channels).transpose(1, 0, 2)
            sums = chain(sums.reshape(COEF_ROWS, model))
            chain.mark(sums)
        else:
            if bit == net.bits[1]:
                shard_in = sum_in.shard(in_shard_kernel, position, (3, depth, 2 * channels))
                (rest,) = output_product.last()
                output = low(middle + rest)
                chain.mark(output)
            across = chain.wait(across)
        last = last + across
        chain.mark(last)
    shard_in = shard_in.transpose(1, 0, 2)
    input_grad = low(grad_input)
    radial_grad = scale_one[:, 0] * jnp.sum(resid * grad_input, axis=1) / model**0.5
    grad_taps = sums[: 3 * TAPS].reshape(taps.shape)
    grad_skip = sums[SKIP_ROW]
    grad_residues = sums[RES_ROW:RATE_ROW]
    grad_log_rates = sums[RATE_ROW:]
    span = model // LANES
    grad_gains = last[: 2 * span].reshape(2, model)
    square_total = last[2 * span, 0] + jnp.sum(grad_gains * grad_gains)
    grad_norm = jnp.sqrt(square_total)
    factor = jnp.minimum(1.0, CLIP / (grad_norm + 1e-06))
    factor = tie(factor, shard_in, shard_out, shard_down, shard_gate, shard_up, sums)

    return (
        output,
        input_grad,
        radial_grad,
        *adam(gains, gains_first, gains_second, grad_gains * factor, RATE_SMALL, 0.0),
        *adam(taps, taps_first, taps_second, grad_taps * factor, RATE_SMALL, 0.0),
        *adam(
            residues, residues_first, residues_second, grad_residues * factor, RATE_SMALL, 0.0
        ),
        *adam(
            log_rates,
            log_rates_first,
            log_rates_second,
            grad_log_rates * factor,
            RATE_RATES,
            0.0,
        ),
        *adam(skip, skip_first, skip_second, grad_skip * factor, RATE_SMALL, 0.0),
        *adam(
            in_weight, in_weight_first, in_weight_second, shard_in * factor, RATE_MATRIX, DECAY
        ),
        *adam(
            out_weight, out_weight_first, out_weight_second, shard_out * factor, RATE_MATRIX, DECAY
        ),
        *adam(
            gate_weight,
            gate_weight_first,
            gate_weight_second,
            shard_gate * factor,
            RATE_MATRIX,
            DECAY,
        ),
        *adam(up_weight, up_weight_first, up_weight_second, shard_up * factor, RATE_MATRIX, DECAY),
        *adam(
            down_weight,
            down_weight_first,
            down_weight_second,
            shard_down * factor,
            RATE_MATRIX,
            DECAY,
        ),
        grad_norm,
    )


def solution(mesh):
    net = Links(mesh.shape["dp"] // 2)
    rows = P(("dp", "mp"), None)
    split_in = P("dp", None, "mp")
    split_out = P("mp", "dp")
    split_up = P("dp", "mp")
    matrices = (split_in,) * 3 + (split_out,) * 3 + (split_up,) * 6 + (split_out,) * 3
    return jax.shard_map(
        functools.partial(on_device, net),
        mesh=mesh,
        in_specs=(rows, rows, P("dp"), P()) + (P(),) * 15 + matrices,
        out_specs=(rows, rows, P(("dp", "mp"))) + (P(),) * 15 + matrices + (P(),),
        check_vma=False,
    )
```
